32 devices in a mesh: dp: 4 (over y, x), gx: 2 (over core), gy: 4 (over z).
Axes of the slice: x: 2, y: 2, z: 4, core: 2. Of those that a mesh axis runs over, the one named last changes fastest.
Arguments:
- magnetic: bfloat16 [4, 3, 8, 64, 512], P('dp', None, None, 'gx', 'gy'), may hold values from -6 to 6
- kernel_one: bfloat16 [3, 3, 3, 3, 32], replicated, may hold values from -0.625 to 0.625
- kernel_two: bfloat16 [3, 3, 3, 32, 64], replicated, may hold values from -0.21875 to 0.21875
- cotangent: bfloat16 [4, 2, 16, 8192], P('dp', None, 'gx', 'gy'), may hold values from -6 to 6
Outputs:
- features: bfloat16 [4, 2, 16, 8192], P('dp', None, 'gx', 'gy')
- level_grad: bfloat16 [4, 4, 32, 8192], P('dp', None, 'gx', 'gy')
- grad_one: float32 [3, 3, 3, 3, 32], P(None, None, None, None, 'dp')
- grad_two: float32 [3, 3, 3, 32, 64], P(None, None, None, None, 'dp')
The draws below stay inside these ranges and needn't reach their ends.
All inputs are finite; a program needn't handle non-finite values.
Results may differ from the reference program's by a relative error of at most 0.012.
Values may be sent and summed in bfloat16 or wider, within the bound.
No kernel may reach another device: no remote copies, remote signals or barrier semaphores. Data moves between devices by JAX's collectives and lax.ppermute only.
A program may use at most 64 MiB of HBM per device.

```python
import math
import jax
import jax.numpy as jnp
from jax import lax

C0 = 3
C1 = 32
C2 = 64
SLAB = 8
SAMPLES = 4
X = 64
Y = 512


def level_of(key, shape, pieces, low, top_value):
    gain, own = 1.0, jax.random.fold_in(key, 6)
    for position, shards_of in pieces:
        draws = jnp.exp(jax.random.uniform(jax.random.fold_in(own, position), (shards_of,), jnp.float32, low / len(pieces), top_value / len(pieces)))
        gain = gain * jnp.repeat(draws, shape[position] // shards_of).reshape([-1 if axis == position else 1 for axis in range(len(shape))])
    return gain


def noise(stream_key, dims, spread, limit, split=(), dtype=jnp.bfloat16):
    result = jax.random.normal(stream_key, dims, jnp.float32) * spread
    if len(split) > 0:
        result = level_of(stream_key, dims, split, -0.22, 0.18) * result
    return jnp.clip(result, min=-limit, max=limit).astype(dtype)


def setup_inputs(seed: int = 0) -> dict:
    key_of = jax.random.split(jax.random.key(seed), 5)
    magnetic = noise(key_of[0], (SAMPLES, C0, SLAB, X, Y), 1.0, 6.0, ((0, 4), (3, 2), (4, 4)))
    kernel_one = noise(key_of[1], (3, 3, 3, C0, C1), (27 * C0) ** -0.5, 0.625)
    kernel_two = noise(key_of[2], (3, 3, 3, C1, C2), (27 * C1) ** -0.5, 0.21875)
    cotangent = noise(key_of[3], (SAMPLES, SLAB // 4, X // 4, (Y // 4) * C2), 1.0, 6.0, ((0, 4), (2, 2), (3, 4)))
    return {"magnetic": magnetic, "kernel_one": kernel_one, "kernel_two": kernel_two, "cotangent": cotangent}


def conv_down(inputs, kernel):
    return lax.conv_general_dilated(inputs.astype(jnp.float32), kernel.astype(jnp.float32), (2, 2, 2), ((1, 0), (1, 0), (1, 0)), dimension_numbers=('NCDHW', 'DHWIO', 'NCDHW'), precision=lax.Precision.HIGHEST)

def silu_slope(pre):
    sig = jax.nn.sigmoid(pre)
    return sig * (1.0 + pre * (1.0 - sig))

def reference(magnetic, kernel_one, kernel_two, cotangent):
    kone = kernel_one.astype(jnp.float32)
    ktwo = kernel_two.astype(jnp.float32)
    upstream_all = jnp.transpose(cotangent.reshape(SAMPLES, SLAB // 4, X // 4, Y // 4, C2), (0, 4, 1, 2, 3))

    def one_sample(totals, inputs_now):
        source, upstream = inputs_now
        source = source[None]
        upstream = upstream[None]
        pre_one = conv_down(source, kone)
        hidden = jax.nn.silu(pre_one).astype(jnp.bfloat16)
        pre_two = conv_down(hidden, ktwo)
        features = jax.nn.silu(pre_two).astype(jnp.bfloat16)
        delta_two = (upstream.astype(jnp.float32) * silu_slope(pre_two)).astype(jnp.bfloat16)
        _, pull_two = jax.vjp(lambda act_in, kern: conv_down(act_in, kern), hidden.astype(jnp.float32), ktwo)
        back_hidden, back_two = pull_two(delta_two.astype(jnp.float32))
        level_grad = back_hidden.astype(jnp.bfloat16)
        delta_one = (level_grad.astype(jnp.float32) * silu_slope(pre_one)).astype(jnp.bfloat16)
        _, pull_one = jax.vjp(lambda kern: conv_down(source, kern), kone)
        back_one, = pull_one(delta_one.astype(jnp.float32))
        return ((totals[0] + back_one, totals[1] + back_two), (features[0], level_grad[0]))
    start = (jnp.zeros(kone.shape, jnp.float32), jnp.zeros(ktwo.shape, jnp.float32))
    (sum_one, sum_two), (features, level_grad) = lax.scan(one_sample, start, (magnetic, upstream_all))
    features = jnp.transpose(features, (0, 2, 3, 4, 1)).reshape(SAMPLES, SLAB // 4, X // 4, Y // 4 * C2)
    level_grad = jnp.transpose(level_grad, (0, 2, 3, 4, 1)).reshape(SAMPLES, SLAB // 2, X // 2, Y // 2 * C1)
    scale_one = 1.0 / math.sqrt(SAMPLES * (SLAB // 2) * (X // 2) * (Y // 2))
    scale_two = 1.0 / math.sqrt(SAMPLES * (SLAB // 4) * (X // 4) * (Y // 4))
    return (features, level_grad, sum_one * scale_one, sum_two * scale_two)
```

```python
import math

import jax
import jax.numpy as jnp
from jax import lax
from jax.experimental import pallas as pl
from jax.experimental.pallas import tpu as pltpu
from jax.sharding import PartitionSpec as P

BF = jnp.bfloat16
F32 = jnp.float32
VMEM_LIMIT = 32 * 1024 * 1024


def iota(shape, dim):
    return lax.broadcasted_iota(jnp.int32, shape, dim)


def dot(lhs, rhs, contract=((1,), (0,))):
    return lax.dot_general(lhs, rhs, (contract, ((), ())), preferred_element_type=F32)


def swaps(axis):
    count, ranks = lax.axis_size(axis), lax.axis_size("dp")
    found = []
    for first in range(min(2, count - 1)):
        pairs = []
        for d in range(ranks):
            for i in range(count):
                other = i + 1 if i % 2 == first else i - 1
                if 0 <= other < count:
                    pairs.append((d * count + i, d * count + other))
                else:
                    pairs.append((d * count + i, (d ^ 1) % ranks * count + i))
        found.append(pairs)
    return found


def position(axis):
    index = lax.axis_index(axis)
    return lax.rem(index, 2) == 1, index == 0, index == lax.axis_size(axis) - 1


def from_low(place, got):
    odd, first, _ = place
    second = got[1] if len(got) > 1 else got[0]
    return jnp.where(first, 0.0, jnp.where(odd, got[0], second))


def from_high(place, got):
    odd, _, last = place
    second = got[1] if len(got) > 1 else got[0]
    return jnp.where(last, 0.0, jnp.where(odd, second, got[0]))


def edge_x_kernel(count, *refs):
    hbm, refs = refs[:4], refs[4:]
    held, outs, (stage, sems) = refs[:4], refs[4 : 4 + count], refs[4 + count :]
    fetches = [pltpu.make_async_copy(hbm[i], held[i], sems.at[i]) for i in range(4)]
    for fetch in fetches:
        fetch.start()
    mag_ref, cot_ref = held[:2]
    odd = position("gx")[0]
    planes = mag_ref.shape[0]
    blocks = cot_ref.shape[2] // 128
    for fetch in fetches:
        fetch.wait()
    field = mag_ref[...].astype(F32)
    low = field[:, 0:4, :]
    high = field[:, field.shape[1] - 4 :, :]
    cot = [cot_ref[k].astype(F32)[0:1, :] for k in range(2)]
    for turn in range(count):
        toward_high = odd if turn == 1 else jnp.logical_not(odd)
        picked = jnp.where(toward_high, high, low)
        for g in range(planes):
            stage[4 * g : 4 * g + 4, :] = picked[g]
        for k in range(2):
            for m in range(blocks):
                row = 4 * planes + 16 * k + m
                stage[row : row + 1, :] = cot[k][:, 128 * m : 128 * m + 128]
        outs[turn][...] = stage[...].astype(BF)


def edge_y_kernel(count_x, count_y, mag_ref, cot_ref, *refs):
    got_refs, refs = refs[:count_x], refs[count_x:]
    split_ref, outs = refs[0], refs[1 : 1 + count_y]
    tall, = refs[1 + count_y :]
    place_x, place_y = position("gx"), position("gy")
    planes = mag_ref.shape[0]
    got = [ref[...].astype(F32) for ref in got_refs]
    low = from_low(place_x, got)
    high = from_high(place_x, got)
    zeros = jnp.zeros((24, 128), F32)
    for g in range(planes):
        edge = low[4 * g : 4 * g + 4, :]
        tall[g, 0:8, :] = jnp.broadcast_to(edge[3:4, :], (8, 128))
        tall[g, 8:40, :] = mag_ref[g].astype(F32)
        tall[g, 40:44, :] = high[4 * g : 4 * g + 4, :]
        tall[g, 44:68, :] = zeros
        tall[g, 68:72, :] = edge
    starts = (8, 9, 10, 11, 7)
    split = []
    for slot in range(5):
        parts = [tall[g, pl.ds(starts[slot], 16, stride=4), :].astype(BF) for g in range(planes)]
        whole = jnp.concatenate(parts, axis=0)
        split_ref[slot] = whole
        split.append(whole)
    rows = planes // 3 * 16
    lhs = jnp.concatenate(
        [split[s][rows * c : rows * c + rows] for s in range(4) for c in range(3)], axis=1
    )
    lane = iota((128, 128), 1)
    cell = iota((128, 128), 0)
    slot = lane & 3
    wanted = jnp.where(lane < 64, 124 + slot, slot)
    group = (lane & 63) >> 2
    picks = []
    for s in range(4):
        for c in range(3):
            hit = (group == 4 * s + c) & (cell == wanted)
            picks.append(jnp.where(hit, 1.0, 0.0).astype(BF))
    both = dot(lhs, jnp.concatenate(picks, axis=0)).reshape(4, 2, 16, 128)
    lower, upper = both[:, 0].reshape(64, 128), both[:, 1].reshape(64, 128)
    left = iota((64, 128), 1) < 64
    toward = [
        jnp.where(left, lower, pltpu.roll(upper, 64, 1)),
        jnp.where(left, pltpu.roll(lower, 64, 1), upper),
    ]
    cot_rows = []
    for k in range(2):
        own = cot_ref[k].astype(F32)[:, 0:128]
        row = 4 * planes + 16 * k
        cot_rows.append(jnp.concatenate([own, high[row : row + 1, :], jnp.zeros((7, 128), F32)], axis=0))
    cot_rows = jnp.where(iota((16, 128), 1) < 64, cot_rows[0], pltpu.roll(cot_rows[1], 64, 1))
    odd = place_y[0]
    for turn in range(count_y):
        toward_high = odd if turn == 1 else jnp.logical_not(odd)
        outs[turn][0:64, :] = jnp.where(toward_high, toward[0], toward[1]).astype(BF)
        outs[turn][64:80, :] = cot_rows.astype(BF)


def weights_kernel(one_ref, two_ref, w_one, w_two, halo_ref, rows_one):
    lane = iota((32, 256), 1)
    spread = jnp.where(iota((32, 256), 0) == (lane & 31), 1.0, 0.0).astype(BF)
    rows_one[80:88, :] = jnp.zeros((8, 32), F32)
    for i in range(27):
        rows_one[3 * i : 3 * i + 3, :] = one_ref[i].astype(F32)
    wide = dot(rows_one[...].astype(BF), spread)
    window = iota((32, 256), 0) - 2 * (lane >> 5)
    for tap in range(9):
        for c in range(3):
            block = jnp.zeros((32, 256), F32)
            for e in range(3):
                row = (3 * tap + e) * 3 + c
                block = jnp.where(window == e, wide[row : row + 1, :], block)
            w_one[128 * tap + 32 * c : 128 * tap + 32 * c + 32, :] = block.astype(BF)
        w_one[128 * tap + 96 : 128 * tap + 128, :] = jnp.zeros((32, 256), BF)

    lane = iota((64, 128), 1)
    spread = jnp.where(iota((64, 128), 0) == (lane & 63), 1.0, 0.0).astype(BF)
    twice = dot(two_ref[...], spread)
    left = iota((32, 128), 1) < 64
    for tap in range(9):
        k0, k1, k2 = (twice[32 * (3 * tap + e) : 32 * (3 * tap + e) + 32] for e in range(3))
        base = 128 * tap
        w_two[base : base + 32, 0:128] = jnp.where(left, k1, 0.0).astype(BF)
        w_two[base + 32 : base + 64, 0:128] = jnp.where(left, k2, k0).astype(BF)
        w_two[base + 64 : base + 96, 0:128] = jnp.where(left, 0.0, k1).astype(BF)
        w_two[base + 96 : base + 128, 0:128] = jnp.where(left, 0.0, k2).astype(BF)
        w_two[base : base + 96, 128:256] = jnp.zeros((96, 128), BF)
        w_two[base + 96 : base + 128, 128:256] = jnp.where(left, k0, 0.0).astype(BF)

    lane = iota((256, 256), 1)
    code = iota((256, 256), 0)
    offset = lane & 31
    part = (lane & 127) >> 5
    wanted = jnp.where(
        lane < 128,
        jnp.where(offset == 0, 3, -999),
        jnp.where(
            (offset >= 1) & (offset <= 4), 127 + offset, jnp.where((offset >= 14) & (offset <= 16), offset - 13, -999)
        ),
    )
    wanted = jnp.where(part < 3, wanted + 4 * part, -999)
    for s in range(4):
        for parity in range(2):
            hit = code - (64 * parity + 16 * s) == wanted
            base = 256 * (2 * s + parity)
            halo_ref[:, base : base + 256] = jnp.where(hit, 1.0, 0.0).astype(BF)


SLOTS = ((4, 0, 1), (1, 2, 3))


def first_level(pre, t):
    sig = jax.nn.sigmoid(pre)
    hidden = pre * sig
    slope = sig * (1.0 + pre * (1.0 - sig))
    if t == 0:
        return [(1, hidden)], slope
    rows, width = hidden.shape
    later = hidden.reshape(rows // 16, 16, width)
    later = jnp.concatenate([later[:, 15:16], later[:, 0:15]], axis=1).reshape(rows, width)
    return [(2, hidden), (0, later)], slope


def second_level(pre, cot):
    sig = jax.nn.sigmoid(pre)
    return pre * sig, cot * (sig * (1.0 + pre * (1.0 - sig)))


def short_pair(value, row):
    return jnp.concatenate([value[row : row + 8, 0:128], value[row : row + 8, 128:256]], axis=0)


def windows_kernel(count_x, split_ref, w_one, w_two, cot_ref, *refs):
    gx_refs, refs = refs[:count_x], refs[count_x:]
    short_ref, outer_ref, short_act, slope_ref, cot_all = refs[:5]
    ends_ref, feat_ref, here_ref, after_ref, grad_ref, inner_ref, act_ref = refs[5:]
    high_x = from_high(position("gx"), [ref[96:128, :].astype(F32) for ref in gx_refs])
    for k in range(2):
        cot = cot_ref[k].astype(F32)
        for m in range(16):
            row = 16 * k + m
            cot_all[k, 16 * m : 16 * m + 8, :] = cot[:, 128 * m : 128 * m + 128]
            cot_all[k, 16 * m + 8 : 16 * m + 16, :] = jnp.where(
                iota((8, 128), 0) == 0, high_x[row : row + 1, :], 0.0
            )

    lane = iota((128, 1152), 1)
    cell = iota((128, 1152), 0)
    block = lane >> 7
    offset = lane & 31
    part = (lane & 127) >> 5
    wanted = jnp.where(offset <= 16, 16 * block - 1 + offset, -9)
    wanted = jnp.where(block == 8, jnp.where(offset == 0, 127, -9), wanted)
    hit = cell == wanted
    picks = jnp.concatenate(
        [jnp.where(hit & (part == c), 1.0, 0.0).astype(BF) for c in range(3)], axis=0
    )
    for s in range(5):
        lhs = jnp.concatenate([split_ref[s, 128 * c : 128 * c + 128, :] for c in range(3)], axis=1)
        exact = dot(lhs, picks)
        found = exact.astype(BF)
        for z in range(8):
            for q in range(4):
                first = exact[16 * z : 16 * z + 8, 256 * q + 128 : 256 * q + 256]
                if q < 3:
                    second = exact[16 * z : 16 * z + 8, 256 * q + 256 : 256 * q + 384]
                else:
                    second = jnp.zeros((8, 128), F32)
                short_ref[s, z, 16 * q : 16 * q + 16, :] = jnp.concatenate([first, second], axis=0).astype(BF)
        for n in range(1, 8):
            for z in range(8):
                inner_ref[s, z, 16 * n - 16 : 16 * n, :] = found[16 * z : 16 * z + 16, 128 * n : 128 * n + 128]
        outer_ref[s, :, 0:128] = found[:, 0:128]
        outer_ref[s, :, 128:256] = found[:, 1024:1152]
    weights = w_one[...]
    for p in range(4):
        for t in range(2):
            pieces = []
            for a in range(3):
                for b in range(3):
                    z = 2 * p + a - 1
                    pieces.append(inner_ref[SLOTS[t][b], z] if z >= 0 else jnp.zeros((112, 128), BF))
            versions, slope = first_level(dot(jnp.concatenate(pieces, axis=1), weights), t)
            for b, value in versions:
                for n in range(7):
                    short_act[b, p, 16 * n : 16 * n + 16, :] = short_pair(value, 16 * n).astype(BF)
                value = value.astype(BF)
                for n in range(7):
                    act_ref[b, p, 32 * n : 32 * n + 16, :] = value[16 * n : 16 * n + 16, 0:128]
                    act_ref[b, p, 32 * n + 16 : 32 * n + 32, :] = value[16 * n : 16 * n + 16, 128:256]
            for n in range(7):
                slope_ref[p, t, 16 * n : 16 * n + 16, :] = short_pair(slope, 16 * n)
    weights = w_two[...]
    delta, patches = [], []
    for k in range(2):
        planes = [(b, 2 * k + a - 1) for a in range(3) for b in range(3)]
        lhs = [act_ref[b, p] if p >= 0 else jnp.zeros((224, 128), BF) for b, p in planes]
        out = dot(jnp.concatenate(lhs, axis=1), weights)
        ends_ref[k, 0] = out[0:16, 0:128]
        ends_ref[k, 1] = out[208:224, 128:256]
        feat, value = second_level(out[16:224, 0:128] + out[0:208, 128:256], cot_all[k, 48:256, :])
        feat_ref[k] = jnp.concatenate([feat[16 * m : 16 * m + 8] for m in range(13)], axis=1).astype(BF)
        value = value.reshape(13, 16, 128)
        here = value[:, 0:8].reshape(104, 128)
        here_ref[k] = here
        after_ref[k] = value[:, 1:9].reshape(104, 128)
        zero = jnp.zeros((8, 128), F32)
        both = [jnp.concatenate([zero, here], axis=0), jnp.concatenate([here, zero], axis=0)]
        delta.append(jnp.concatenate(both, axis=1).astype(BF))
        short = [short_act[b, p] if p >= 0 else jnp.zeros((112, 128), BF) for b, p in planes]
        patches.append(jnp.concatenate(short, axis=1))
    grad_ref[...] = dot(jnp.concatenate(delta, axis=0), jnp.concatenate(patches, axis=0), ((0,), (0,)))[0:192]


def main_kernel(
    count_y,
    ranks,
    short_ref,
    outer_ref,
    short_act,
    slope_ref,
    cot_ref,
    ends_ref,
    feat_in,
    here_in,
    after_in,
    grad_in,
    halo_ref,
    w_one,
    w_two,
    *refs,
):
    gy_refs, refs = refs[:count_y], refs[count_y:]
    feat_hbm, level_hbm, refs = refs[0], refs[1], refs[2:]
    dealt, refs = refs[:ranks], refs[ranks:]
    edges, short_edges, outer_act, outer_short, outer_slope, rows_out, total, feat_ref, level_ref, sems = refs
    place_y = position("gy")
    copies = []

    got_y = [ref[...].astype(F32) for ref in gy_refs]
    low_y = from_low(place_y, got_y)
    high_y = from_high(place_y, got_y)
    halo = jnp.concatenate([low_y[0:64], high_y[0:64]], axis=1).astype(BF)
    first_half = iota((16, 128), 1) < 64
    cot_y = [jnp.where(first_half, value, 0.0) for value in (high_y[64:80], pltpu.roll(high_y[64:80], 64, 1))]
    brought = dot(halo, halo_ref[...])
    for s in range(5):
        base = 512 * min(s, 3)
        found = [brought[:, base + 256 * parity : base + 256 * parity + 256].reshape(4, 16, 256) for parity in range(2)]
        edge = jnp.stack(found, axis=1).reshape(8, 16, 256)
        if s == 4:
            edge = jnp.concatenate([edge[:, 15:16], edge[:, 0:15]], axis=1)
        exact = outer_ref[s].astype(F32) + edge.reshape(128, 256)
        value = exact.astype(BF)
        for z in range(8):
            edges[s, z, 0:16, :] = value[16 * z : 16 * z + 16, 0:128]
            edges[s, z, 16:32, :] = value[16 * z : 16 * z + 16, 128:256]
            other = short_ref[s, z, 48:64, :].astype(F32)
            short_edges[s, z] = jnp.concatenate([other[0:8], exact[16 * z : 16 * z + 8, 0:128]], axis=0).astype(BF)

    def window(s, z):
        if z < 0:
            return jnp.zeros((64, 128), BF)
        return jnp.concatenate([short_ref[s, z, 0:48, :], short_edges[s, z]], axis=0)

    weights = w_one[...]
    for t in range(2):
        rows = []
        for p in range(4):
            pieces = []
            for a in range(3):
                for b in range(3):
                    z = 2 * p + a - 1
                    pieces.append(edges[SLOTS[t][b], z] if z >= 0 else jnp.zeros((32, 128), BF))
            rows.append(jnp.concatenate(pieces, axis=1))
        versions, slope = first_level(dot(jnp.concatenate(rows, axis=0), weights), t)
        for p in range(4):
            first, second = 32 * p, 32 * p + 16
            for b, value in versions:
                before = jnp.concatenate([value[second : second + 8, 128:256], jnp.zeros((8, 128), F32)], axis=0)
                outer_short[b, p, 0:16, :] = before.astype(BF)
                outer_short[b, p, 16:32, :] = short_pair(value, first).astype(BF)
                outer_act[b, p, 0:16, :] = value[second : second + 16, 128:256].astype(BF)
                outer_act[b, p, 16:32, :] = value[first : first + 16, 0:128].astype(BF)
                outer_act[b, p, 32:48, :] = value[first : first + 16, 128:256].astype(BF)
                outer_act[b, p, 48:64, :] = value[second : second + 16, 0:128].astype(BF)
            outer_slope[p, t] = short_pair(slope, first)

    lhs = []
    for k in range(2):
        planes = [(b, 2 * k + a - 1) for a in range(3) for b in range(3)]
        lhs.append(
            jnp.concatenate([outer_act[b, p] if p >= 0 else jnp.zeros((64, 128), BF) for b, p in planes], axis=1)
        )
    out = dot(jnp.concatenate(lhs, axis=0), w_two[...])
    pairs, pairs_next, delta, patches = [], [], [], []
    for k in range(2):
        own = out[64 * k : 64 * k + 64]
        pre = jnp.concatenate(
            [own[16:48, 0:128], ends_ref[k, 0], own[48:64, 0:128]], axis=0
        ) + jnp.concatenate([own[0:48, 128:256], ends_ref[k, 1]], axis=0)
        feat, value = second_level(pre, jnp.concatenate([cot_ref[k, 0:48, :], cot_y[k]], axis=0))
        feat_ref[k, :, 0:384] = jnp.concatenate([feat[16 * m : 16 * m + 8] for m in range(3)], axis=1).astype(BF)
        feat_ref[k, :, 384:2048] = feat_in[k]
        copies.append(pltpu.make_async_copy(feat_ref.at[k], feat_hbm.at[k], sems.at[k]))
        copies[-1].start()
        value = value.reshape(4, 16, 128)
        outer = value[:, 0:8].reshape(32, 128)
        here = jnp.concatenate([outer[0:24], here_in[k], outer[24:32]], axis=0)
        outer_after = value[:, 1:9].reshape(32, 128)
        after = jnp.concatenate([outer_after[0:24], after_in[k], outer_after[24:32]], axis=0)
        pairs.append(jnp.concatenate([here[0:128], here[8:136]], axis=1).astype(BF))
        pairs_next.append(jnp.concatenate([after[0:128], after[8:136]], axis=1).astype(BF))
        zero = jnp.zeros((8, 128), F32)
        both = [
            jnp.concatenate([zero, zero, outer[0:24], zero], axis=0),
            jnp.concatenate([outer[0:8], zero, outer[8:24], zero, zero], axis=0),
        ]
        delta.append(jnp.concatenate(both, axis=1).astype(BF))
        short = []
        for a in range(3):
            for b in range(3):
                p = 2 * k + a - 1
                if p < 0:
                    short.append(jnp.zeros((48, 128), BF))
                else:
                    short.append(jnp.concatenate([outer_short[b, p], short_act[b, p, 0:16, :]], axis=0))
        patches.append(jnp.concatenate(short, axis=1))
    grad = dot(jnp.concatenate(delta, axis=0), jnp.concatenate(patches, axis=0), ((0,), (0,)))
    grad = grad_in[...] + grad[0:192]

    place = iota((64, 128), 1) >> 5
    turned = []
    for ab in range(9):
        a0, a1, a2 = (grad[64 * j : 64 * j + 64, 128 * ab : 128 * ab + 128] for j in range(3))
        across = pltpu.roll(jnp.where(place == 2, a1, jnp.where(place == 3, a2, a0)), 64, 1)
        joined = jnp.where(place == 0, a0, a1) + across
        shift = (3 * ab - 1) % 4
        other = (shift + 2) % 4
        outer = pltpu.roll(joined, 32 * shift, 1) if shift else joined
        inner = pltpu.roll(joined, 32 * other, 1) if other else joined
        turned += [outer, inner, outer]
    turned.append(jnp.zeros((64, 128), F32))
    for v in range(7):
        t0, t1, t2, t3 = turned[4 * v : 4 * v + 4]
        total[:, 128 * v : 128 * v + 128] = jnp.where(
            place < 2, jnp.where(place == 0, t0, t1), jnp.where(place == 2, t2, t3)
        )

    lhs_rows, rhs_rows = [], []
    for p in range(4):
        depth = [(1, p // 2)] if p % 2 == 0 else [(2, (p - 1) // 2), (0, (p + 1) // 2)]
        for t in range(2):
            width = [(1, pairs)] if t == 0 else [(2, pairs), (0, pairs_next)]
            taps = [(3 * a + b, source[k]) for a, k in depth if k < 2 for b, source in width]
            level = dot(
                jnp.concatenate([source for _, source in taps], axis=1),
                jnp.concatenate([w_two[128 * tap : 128 * tap + 128, :] for tap, _ in taps], axis=1),
                ((1,), (1,)),
            )
            level = level.astype(BF).astype(F32)
            for m in range(16):
                rows_out[m, pl.ds(t, 8, stride=2), :] = level[8 * m : 8 * m + 8]
            slope = jnp.concatenate([outer_slope[p, t], slope_ref[p, t]], axis=0)
            value = level * slope
            blocks = [
                jnp.concatenate([value[16 * n : 16 * n + 8], value[16 * n + 8 : 16 * n + 16]], axis=1)
                for n in (1, 2, 3, 4, 5, 6, 7, 0)
            ]
            lhs_rows.append(jnp.concatenate(blocks, axis=0).astype(BF))
            rhs_rows.append(
                jnp.concatenate([window(SLOTS[t][b], 2 * p + a - 1) for a in range(3) for b in range(3)], axis=1)
            )
        level_ref[p] = jnp.concatenate([rows_out[m] for m in range(16)], axis=1).astype(BF)
        copies.append(pltpu.make_async_copy(level_ref.at[p], level_hbm.at[p], sems.at[2 + p]))
        copies[-1].start()
    grad = dot(jnp.concatenate(lhs_rows, axis=0), jnp.concatenate(rhs_rows, axis=0), ((0,), (0,)))

    place = iota((32, 128), 1)
    found = jnp.zeros((32, 128), F32)
    for tap in range(9):
        some = jnp.zeros((32, 128), F32)
        for t in range(8):
            piece = grad[32 * t : 32 * t + 32, 128 * tap : 128 * tap + 128]
            shift = (3 * tap - 2 * t) % 128
            some = some + (pltpu.roll(piece, shift, 1) if shift else piece)
        local = place & 31
        found = jnp.where((local >= 3 * tap) & (local < 3 * tap + 3), some, found)
    total[:, 896:1024] = jnp.zeros((64, 128), F32)
    tall, short = 64 // ranks, 32 // ranks
    for d in range(ranks):
        total[tall * d : tall * d + short, 896:1024] = found[short * d : short * d + short]
    rank = lax.axis_index("dp")
    for step, out in enumerate(dealt):
        if tall % 8 == 0:
            start = pl.multiple_of((rank ^ step) * tall, tall)
            picked = total[pl.ds(start, tall), :]
        else:
            picked = total[0:tall, :]
            for d in range(1, ranks):
                picked = jnp.where((rank ^ step) == d, total[d * tall : d * tall + tall, :], picked)
        out[...] = picked.astype(BF)
    for copy in copies:
        copy.wait()


def sum_kernel(*refs):
    parts, out_ref = refs[:-1], refs[-1]
    values = [ref[...].astype(F32) for ref in parts]
    while len(values) > 1:
        values = [values[i] + values[i + 1] for i in range(0, len(values), 2)]
    out_ref[...] = values[0].astype(out_ref.dtype)


def share_kernel(mine_ref, first_ref, second_ref, out_ref):
    first = first_ref[...].astype(F32)
    odd = position("gx")[0]
    out_ref[...] = first + jnp.where(odd, second_ref[...], mine_ref[...]).astype(F32)


def last_kernel(scale_one, scale_two, *refs):
    parts, (two_hbm, one_ref, two_ref, sems) = refs[:-4], refs[-4:]
    values = [ref[...].astype(F32) for ref in parts]
    while len(values) > 1:
        values = [values[i] + values[i + 1] for i in range(0, len(values), 2)]
    value = values[0]
    tall = value.shape[0]
    short = tall // 2
    scaled = value[:, 0:896] * scale_two
    copies = []
    for tap in range(27):
        two_ref[tap] = scaled[:, 32 * tap : 32 * tap + 32]
        if tap % 9 == 8:
            part = pl.ds(tap - 8, 9)
            copies.append(pltpu.make_async_copy(two_ref.at[part], two_hbm.at[part], sems.at[tap // 9]))
            copies[-1].start()
    rows = value[0:short, 896:1024] * scale_one
    if short < 8:
        rows = jnp.concatenate([rows, jnp.zeros((8 - short, 128), F32)], axis=0)
    turned = rows.T
    for c in range(3):
        one_ref[:, c, :] = turned[32 * c : 32 * c + 27, 0:short]
    for copy in copies:
        copy.wait()


def call(kernel, outs, args, scratch=(), space=pltpu.VMEM, in_hbm=0, flops=0):
    spaces = [pltpu.HBM] * in_hbm + [pltpu.VMEM] * (len(outs) - in_hbm)
    return pl.pallas_call(
        kernel,
        out_shape=outs,
        in_specs=[pl.BlockSpec(memory_space=space)] * len(args),
        out_specs=[pl.BlockSpec(memory_space=kind) for kind in spaces],
        scratch_shapes=list(scratch),
        compiler_params=pltpu.CompilerParams(vmem_limit_bytes=VMEM_LIMIT),
        cost_estimate=pl.CostEstimate(flops=flops, bytes_accessed=1 << 20, transcendentals=0),
    )(*args)


def shape(dims, dtype):
    return jax.ShapeDtypeStruct(dims, dtype)


def exchange(value, axis, step):
    return lax.ppermute(value, axis, [(i, i ^ step) for i in range(lax.axis_size(axis))])


def trade_shared(value, steps):
    count, columns = lax.axis_size("gy"), lax.axis_size("gx")
    pairs = [(g * count + i, g * count + (i ^ steps[g % 2])) for g in range(columns) for i in range(count)]
    return lax.ppermute(value, ("gx", "gy"), pairs)


def body(magnetic, kernel_one, kernel_two, cotangent):
    ranks, count_gx, count_gy = (lax.axis_size(axis) for axis in ("dp", "gx", "gy"))
    depth = magnetic.shape[2]
    samples_all = magnetic.shape[0] * ranks
    cells_x = magnetic.shape[3] * count_gx
    cells_y = magnetic.shape[4] * count_gy
    scale_one = 1.0 / math.sqrt(samples_all * (depth // 2) * (cells_x // 2) * (cells_y // 2))
    scale_two = 1.0 / math.sqrt(samples_all * (depth // 4) * (cells_x // 4) * (cells_y // 4))
    field = magnetic.reshape(24, 32, 128)
    cot = cotangent.reshape(2, 8, 2048)
    one = kernel_one.reshape(27, 3, 32)
    two = kernel_two.reshape(864, 64)

    swaps_x, swaps_y = swaps("gx"), swaps("gy")
    nx, ny = len(swaps_x), len(swaps_y)
    operands = [pltpu.with_memory_space_constraint(array, pltpu.HBM) for array in (field, cot, one, two)]
    field, cot, one, two, *edges = call(
        lambda *refs: edge_x_kernel(nx, *refs),
        [shape(array.shape, BF) for array in operands] + [shape((128, 128), BF)] * nx,
        operands,
        [pltpu.VMEM((128, 128), F32), pltpu.SemaphoreType.DMA((4,))],
        space=pltpu.HBM,
    )
    got_x = [lax.ppermute(edge, ("dp", "gx"), pairs) for edge, pairs in zip(edges, swaps_x)]
    w_one, w_two, picks = call(
        weights_kernel,
        [shape((1152, 256), BF), shape((1152, 256), BF), shape((256, 2048), BF)],
        (one, two),
        [pltpu.VMEM((88, 32), F32)],
        flops=1 << 30,
    )
    split, *edges = call(
        lambda *refs: edge_y_kernel(nx, ny, *refs),
        [shape((5, 384, 128), BF)] + [shape((80, 128), BF)] * ny,
        (field, cot, *got_x),
        [pltpu.VMEM((24, 72, 128), F32)],
    )
    got_y = [lax.ppermute(edge, ("dp", "gy"), pairs) for edge, pairs in zip(edges, swaps_y)]
    first = call(
        lambda *refs: windows_kernel(nx, *refs),
        [
            shape((5, 8, 64, 128), BF),
            shape((5, 128, 256), BF),
            shape((3, 4, 112, 128), BF),
            shape((4, 2, 112, 128), F32),
            shape((2, 256, 128), F32),
            shape((2, 2, 16, 128), F32),
            shape((2, 8, 1664), BF),
            shape((2, 104, 128), F32),
            shape((2, 104, 128), F32),
            shape((192, 1152), F32),
        ],
        (split, w_one, w_two, cot, *got_x),
        [pltpu.VMEM((5, 8, 112, 128), BF), pltpu.VMEM((3, 4, 224, 128), BF)],
        flops=1 << 31,
    )
    tall = 64 // ranks
    features, level, *dealt = call(
        lambda *refs: main_kernel(ny, ranks, *refs),
        [shape((2, 8, 2048), BF), shape((4, 16, 2048), BF)] + [shape((tall, 1024), BF)] * ranks,
        (*first, picks, w_one, w_two, *got_y),
        [
            pltpu.VMEM((5, 8, 32, 128), BF),
            pltpu.VMEM((5, 8, 16, 128), BF),
            pltpu.VMEM((3, 4, 64, 128), BF),
            pltpu.VMEM((3, 4, 32, 128), BF),
            pltpu.VMEM((4, 2, 16, 128), F32),
            pltpu.VMEM((16, 16, 128), F32),
            pltpu.VMEM((64, 1024), F32),
            pltpu.VMEM((2, 8, 2048), BF),
            pltpu.VMEM((4, 16, 2048), BF),
            pltpu.SemaphoreType.DMA((6,)),
        ],
        in_hbm=2,
    )
    terms = dealt[:1] + [exchange(dealt[step], "dp", step) for step in range(1, ranks)]
    mine, = call(sum_kernel, [shape((tall, 1024), BF)], terms)
    step = 1
    while step < count_gx:
        mine, = call(sum_kernel, [shape((tall, 1024), BF)], (mine, exchange(mine, "gx", step)))
        step *= 2
    if count_gy == 4:
        terms = [mine, trade_shared(mine, (1, 2)), trade_shared(mine, (1, 3))]
        mine, = call(share_kernel, [shape((tall, 1024), F32)], terms)
        terms = [mine, exchange(mine, "gx", 1)]
    else:
        terms = [mine] + [exchange(mine, "gy", step) for step in range(1, count_gy)]
    grad_two, grad_one = call(
        lambda *refs: last_kernel(scale_one, scale_two, *refs),
        [shape((27, tall, 32), F32), shape((27, 3, tall // 2), F32)],
        terms,
        [pltpu.VMEM((27, tall, 32), F32), pltpu.SemaphoreType.DMA((3,))],
        in_hbm=1,
    )
    grad_one = grad_one.reshape(3, 3, 3, 3, tall // 2)
    grad_two = jnp.transpose(grad_two.reshape(3, 3, 3, tall, 32), (0, 1, 2, 4, 3))
    return (
        features.reshape(1, 2, 8, 2048),
        level.reshape(1, 4, 16, 2048),
        grad_one,
        grad_two,
    )


def solution(mesh):
    in_specs = (P("dp", None, None, "gx", "gy"), P(), P(), P("dp", None, "gx", "gy"))
    out_specs = (
        P("dp", None, "gx", "gy"),
        P("dp", None, "gx", "gy"),
        P(None, None, None, None, "dp"),
        P(None, None, None, None, "dp"),
    )
    return jax.shard_map(body, mesh=mesh, in_specs=in_specs, out_specs=out_specs, check_vma=False)
```

```python
import math

import jax
import jax.numpy as jnp
from jax import lax
from jax.experimental import pallas as pl
from jax.experimental.pallas import tpu as pltpu
from jax.sharding import PartitionSpec as P

BF = jnp.bfloat16
F32 = jnp.float32
VMEM_LIMIT = 32 * 1024 * 1024


def iota(shape, dim):
    return lax.broadcasted_iota(jnp.int32, shape, dim)


def dot(lhs, rhs, contract=((1,), (0,))):
    return lax.dot_general(lhs, rhs, (contract, ((), ())), preferred_element_type=F32)


def swaps(axis):
    count, ranks = lax.axis_size(axis), lax.axis_size("dp")
    found = []
    for first in range(min(2, count - 1)):
        pairs = []
        for d in range(ranks):
            for i in range(count):
                other = i + 1 if i % 2 == first else i - 1
                if 0 <= other < count:
                    pairs.append((d * count + i, d * count + other))
                else:
                    pairs.append((d * count + i, (d ^ 1) % ranks * count + i))
        found.append(pairs)
    return found


def position(axis):
    index = lax.axis_index(axis)
    return lax.rem(index, 2) == 1, index == 0, index == lax.axis_size(axis) - 1


def from_low(place, got):
    odd, first, _ = place
    second = got[1] if len(got) > 1 else got[0]
    return jnp.where(first, 0.0, jnp.where(odd, got[0], second))


def from_high(place, got):
    odd, _, last = place
    second = got[1] if len(got) > 1 else got[0]
    return jnp.where(last, 0.0, jnp.where(odd, second, got[0]))


def edge_x_kernel(count, *refs):
    hbm, refs = refs[:4], refs[4:]
    held, outs, (stage, sems) = refs[:4], refs[4 : 4 + count], refs[4 + count :]
    fetches = [pltpu.make_async_copy(hbm[i], held[i], sems.at[i]) for i in range(4)]
    for fetch in fetches:
        fetch.start()
    mag_ref, cot_ref = held[:2]
    odd = position("gx")[0]
    planes = mag_ref.shape[0]
    blocks = cot_ref.shape[2] // 128
    for fetch in fetches:
        fetch.wait()
    field = mag_ref[...].astype(F32)
    low = field[:, 0:4, :]
    high = field[:, field.shape[1] - 4 :, :]
    cot = [cot_ref[k].astype(F32)[0:1, :] for k in range(2)]
    for turn in range(count):
        toward_high = odd if turn == 1 else jnp.logical_not(odd)
        picked = jnp.where(toward_high, high, low)
        for g in range(planes):
            stage[4 * g : 4 * g + 4, :] = picked[g]
        for k in range(2):
            for m in range(blocks):
                row = 4 * planes + 16 * k + m
                stage[row : row + 1, :] = cot[k][:, 128 * m : 128 * m + 128]
        outs[turn][...] = stage[...].astype(BF)


def edge_y_kernel(count_x, count_y, mag_ref, cot_ref, *refs):
    got_refs, refs = refs[:count_x], refs[count_x:]
    split_ref, outs = refs[0], refs[1 : 1 + count_y]
    tall, = refs[1 + count_y :]
    place_x, place_y = position("gx"), position("gy")
    planes = mag_ref.shape[0]
    got = [ref[...].astype(F32) for ref in got_refs]
    low = from_low(place_x, got)
    high = from_high(place_x, got)
    zeros = jnp.zeros((24, 128), F32)
    for g in range(planes):
        edge = low[4 * g : 4 * g + 4, :]
        tall[g, 0:8, :] = jnp.broadcast_to(edge[3:4, :], (8, 128))
        tall[g, 8:40, :] = mag_ref[g].astype(F32)
        tall[g, 40:44, :] = high[4 * g : 4 * g + 4, :]
        tall[g, 44:68, :] = zeros
        tall[g, 68:72, :] = edge
    starts = (8, 9, 10, 11, 7)
    split = []
    for slot in range(5):
        parts = [tall[g, pl.ds(starts[slot], 16, stride=4), :].astype(BF) for g in range(planes)]
        whole = jnp.concatenate(parts, axis=0)
        split_ref[slot] = whole
        split.append(whole)
    rows = planes // 3 * 16
    lhs = jnp.concatenate(
        [split[s][rows * c : rows * c + rows] for s in range(4) for c in range(3)], axis=1
    )
    lane = iota((128, 128), 1)
    cell = iota((128, 128), 0)
    slot = lane & 3
    wanted = jnp.where(lane < 64, 124 + slot, slot)
    group = (lane & 63) >> 2
    picks = []
    for s in range(4):
        for c in range(3):
            hit = (group == 4 * s + c) & (cell == wanted)
            picks.append(jnp.where(hit, 1.0, 0.0).astype(BF))
    both = dot(lhs, jnp.concatenate(picks, axis=0)).reshape(4, 2, 16, 128)
    lower, upper = both[:, 0].reshape(64, 128), both[:, 1].reshape(64, 128)
    left = iota((64, 128), 1) < 64
    toward = [
        jnp.where(left, lower, pltpu.roll(upper, 64, 1)),
        jnp.where(left, pltpu.roll(lower, 64, 1), upper),
    ]
    cot_rows = []
    for k in range(2):
        own = cot_ref[k].astype(F32)[:, 0:128]
        row = 4 * planes + 16 * k
        cot_rows.append(jnp.concatenate([own, high[row : row + 1, :], jnp.zeros((7, 128), F32)], axis=0))
    cot_rows = jnp.where(iota((16, 128), 1) < 64, cot_rows[0], pltpu.roll(cot_rows[1], 64, 1))
    odd = place_y[0]
    for turn in range(count_y):
        toward_high = odd if turn == 1 else jnp.logical_not(odd)
        outs[turn][0:64, :] = jnp.where(toward_high, toward[0], toward[1]).astype(BF)
        outs[turn][64:80, :] = cot_rows.astype(BF)


def weights_kernel(one_ref, two_ref, w_one, w_two, halo_ref, rows_one):
    lane = iota((32, 256), 1)
    spread = jnp.where(iota((32, 256), 0) == (lane & 31), 1.0, 0.0).astype(BF)
    rows_one[80:88, :] = jnp.zeros((8, 32), F32)
    for i in range(27):
        rows_one[3 * i : 3 * i + 3, :] = one_ref[i].astype(F32)
    wide = dot(rows_one[...].astype(BF), spread)
    window = iota((32, 256), 0) - 2 * (lane >> 5)
    for tap in range(9):
        for c in range(3):
            block = jnp.zeros((32, 256), F32)
            for e in range(3):
                row = (3 * tap + e) * 3 + c
                block = jnp.where(window == e, wide[row : row + 1, :], block)
            w_one[128 * tap + 32 * c : 128 * tap + 32 * c + 32, :] = block.astype(BF)
        w_one[128 * tap + 96 : 128 * tap + 128, :] = jnp.zeros((32, 256), BF)

    lane = iota((64, 128), 1)
    spread = jnp.where(iota((64, 128), 0) == (lane & 63), 1.0, 0.0).astype(BF)
    twice = dot(two_ref[...], spread)
    left = iota((32, 128), 1) < 64
    for tap in range(9):
        k0, k1, k2 = (twice[32 * (3 * tap + e) : 32 * (3 * tap + e) + 32] for e in range(3))
        base = 128 * tap
        w_two[base : base + 32, 0:128] = jnp.where(left, k1, 0.0).astype(BF)
        w_two[base + 32 : base + 64, 0:128] = jnp.where(left, k2, k0).astype(BF)
        w_two[base + 64 : base + 96, 0:128] = jnp.where(left, 0.0, k1).astype(BF)
        w_two[base + 96 : base + 128, 0:128] = jnp.where(left, 0.0, k2).astype(BF)
        w_two[base : base + 96, 128:256] = jnp.zeros((96, 128), BF)
        w_two[base + 96 : base + 128, 128:256] = jnp.where(left, k0, 0.0).astype(BF)

    lane = iota((256, 256), 1)
    code = iota((256, 256), 0)
    offset = lane & 31
    part = (lane & 127) >> 5
    wanted = jnp.where(
        lane < 128,
        jnp.where(offset == 0, 3, -999),
        jnp.where(
            (offset >= 1) & (offset <= 4), 127 + offset, jnp.where((offset >= 14) & (offset <= 16), offset - 13, -999)
        ),
    )
    wanted = jnp.where(part < 3, wanted + 4 * part, -999)
    for s in range(4):
        for parity in range(2):
            hit = code - (64 * parity + 16 * s) == wanted
            base = 256 * (2 * s + parity)
            halo_ref[:, base : base + 256] = jnp.where(hit, 1.0, 0.0).astype(BF)


SLOTS = ((4, 0, 1), (1, 2, 3))


def first_level(pre, t):
    sig = jax.nn.sigmoid(pre)
    hidden = pre * sig
    slope = sig * (1.0 + pre * (1.0 - sig))
    if t == 0:
        return [(1, hidden)], slope
    rows, width = hidden.shape
    later = hidden.reshape(rows // 16, 16, width)
    later = jnp.concatenate([later[:, 15:16], later[:, 0:15]], axis=1).reshape(rows, width)
    return [(2, hidden), (0, later)], slope


def second_level(pre, cot):
    sig = jax.nn.sigmoid(pre)
    return pre * sig, cot * (sig * (1.0 + pre * (1.0 - sig)))


def short_pair(value, row):
    return jnp.concatenate([value[row : row + 8, 0:128], value[row : row + 8, 128:256]], axis=0)


def windows_kernel(count_x, split_ref, w_one, w_two, cot_ref, *refs):
    gx_refs, refs = refs[:count_x], refs[count_x:]
    short_ref, outer_ref, short_act, slope_ref, cot_all = refs[:5]
    ends_ref, feat_ref, here_ref, after_ref, grad_ref, inner_ref, act_ref = refs[5:]
    high_x = from_high(position("gx"), [ref[96:128, :].astype(F32) for ref in gx_refs])
    for k in range(2):
        cot = cot_ref[k].astype(F32)
        for m in range(16):
            row = 16 * k + m
            cot_all[k, 16 * m : 16 * m + 8, :] = cot[:, 128 * m : 128 * m + 128]
            cot_all[k, 16 * m + 8 : 16 * m + 16, :] = jnp.where(
                iota((8, 128), 0) == 0, high_x[row : row + 1, :], 0.0
            )

    lane = iota((128, 1152), 1)
    cell = iota((128, 1152), 0)
    block = lane >> 7
    offset = lane & 31
    part = (lane & 127) >> 5
    wanted = jnp.where(offset <= 16, 16 * block - 1 + offset, -9)
    wanted = jnp.where(block == 8, jnp.where(offset == 0, 127, -9), wanted)
    hit = cell == wanted
    picks = jnp.concatenate(
        [jnp.where(hit & (part == c), 1.0, 0.0).astype(BF) for c in range(3)], axis=0
    )
    for s in range(5):
        lhs = jnp.concatenate([split_ref[s, 128 * c : 128 * c + 128, :] for c in range(3)], axis=1)
        exact = dot(lhs, picks)
        found = exact.astype(BF)
        for z in range(8):
            for q in range(4):
                first = exact[16 * z : 16 * z + 8, 256 * q + 128 : 256 * q + 256]
                if q < 3:
                    second = exact[16 * z : 16 * z + 8, 256 * q + 256 : 256 * q + 384]
                else:
                    second = jnp.zeros((8, 128), F32)
                short_ref[s, z, 16 * q : 16 * q + 16, :] = jnp.concatenate([first, second], axis=0).astype(BF)
        for n in range(1, 8):
            for z in range(8):
                inner_ref[s, z, 16 * n - 16 : 16 * n, :] = found[16 * z : 16 * z + 16, 128 * n : 128 * n + 128]
        outer_ref[s, :, 0:128] = found[:, 0:128]
        outer_ref[s, :, 128:256] = found[:, 1024:1152]
    weights = w_one[...]
    for p in range(4):
        for t in range(2):
            pieces = []
            for a in range(3):
                for b in range(3):
                    z = 2 * p + a - 1
                    pieces.append(inner_ref[SLOTS[t][b], z] if z >= 0 else jnp.zeros((112, 128), BF))
            versions, slope = first_level(dot(jnp.concatenate(pieces, axis=1), weights), t)
            for b, value in versions:
                for n in range(7):
                    short_act[b, p, 16 * n : 16 * n + 16, :] = short_pair(value, 16 * n).astype(BF)
                value = value.astype(BF)
                for n in range(7):
                    act_ref[b, p, 32 * n : 32 * n + 16, :] = value[16 * n : 16 * n + 16, 0:128]
                    act_ref[b, p, 32 * n + 16 : 32 * n + 32, :] = value[16 * n : 16 * n + 16, 128:256]
            for n in range(7):
                slope_ref[p, t, 16 * n : 16 * n + 16, :] = short_pair(slope, 16 * n)
    weights = w_two[...]
    delta, patches = [], []
    for k in range(2):
        planes = [(b, 2 * k + a - 1) for a in range(3) for b in range(3)]
        lhs = [act_ref[b, p] if p >= 0 else jnp.zeros((224, 128), BF) for b, p in planes]
        out = dot(jnp.concatenate(lhs, axis=1), weights)
        ends_ref[k, 0] = out[0:16, 0:128]
        ends_ref[k, 1] = out[208:224, 128:256]
        feat, value = second_level(out[16:224, 0:128] + out[0:208, 128:256], cot_all[k, 48:256, :])
        feat_ref[k] = jnp.concatenate([feat[16 * m : 16 * m + 8] for m in range(13)], axis=1).astype(BF)
        value = value.reshape(13, 16, 128)
        here = value[:, 0:8].reshape(104, 128)
        here_ref[k] = here
        after_ref[k] = value[:, 1:9].reshape(104, 128)
        zero = jnp.zeros((8, 128), F32)
        both = [jnp.concatenate([zero, here], axis=0), jnp.concatenate([here, zero], axis=0)]
        delta.append(jnp.concatenate(both, axis=1).astype(BF))
        short = [short_act[b, p] if p >= 0 else jnp.zeros((112, 128), BF) for b, p in planes]
        patches.append(jnp.concatenate(short, axis=1))
    grad_ref[...] = dot(jnp.concatenate(delta, axis=0), jnp.concatenate(patches, axis=0), ((0,), (0,)))


def main_kernel(
    count_y,
    ranks,
    short_ref,
    outer_ref,
    short_act,
    slope_ref,
    cot_ref,
    ends_ref,
    feat_in,
    here_in,
    after_in,
    grad_in,
    halo_ref,
    w_one,
    w_two,
    *refs,
):
    gy_refs, refs = refs[:count_y], refs[count_y:]
    feat_hbm, level_hbm, refs = refs[0], refs[1], refs[2:]
    dealt, refs = refs[:ranks], refs[ranks:]
    edges, short_edges, outer_act, outer_short, outer_slope, rows_out, total, feat_ref, level_ref, sems = refs
    place_y = position("gy")
    copies = []

    got_y = [ref[...].astype(F32) for ref in gy_refs]
    low_y = from_low(place_y, got_y)
    high_y = from_high(place_y, got_y)
    halo = jnp.concatenate([low_y[0:64], high_y[0:64]], axis=1).astype(BF)
    first_half = iota((16, 128), 1) < 64
    cot_y = [jnp.where(first_half, value, 0.0) for value in (high_y[64:80], pltpu.roll(high_y[64:80], 64, 1))]
    brought = dot(halo, halo_ref[...])
    for s in range(5):
        base = 512 * min(s, 3)
        found = [brought[:, base + 256 * parity : base + 256 * parity + 256].reshape(4, 16, 256) for parity in range(2)]
        edge = jnp.stack(found, axis=1).reshape(8, 16, 256)
        if s == 4:
            edge = jnp.concatenate([edge[:, 15:16], edge[:, 0:15]], axis=1)
        exact = outer_ref[s].astype(F32) + edge.reshape(128, 256)
        value = exact.astype(BF)
        for z in range(8):
            edges[s, z, 0:16, :] = value[16 * z : 16 * z + 16, 0:128]
            edges[s, z, 16:32, :] = value[16 * z : 16 * z + 16, 128:256]
            other = short_ref[s, z, 48:64, :].astype(F32)
            short_edges[s, z] = jnp.concatenate([other[0:8], exact[16 * z : 16 * z + 8, 0:128]], axis=0).astype(BF)

    def window(s, z):
        if z < 0:
            return jnp.zeros((64, 128), BF)
        return jnp.concatenate([short_ref[s, z, 0:48, :], short_edges[s, z]], axis=0)

    weights = w_one[...]
    for t in range(2):
        rows = []
        for p in range(4):
            pieces = []
            for a in range(3):
                for b in range(3):
                    z = 2 * p + a - 1
                    pieces.append(edges[SLOTS[t][b], z] if z >= 0 else jnp.zeros((32, 128), BF))
            rows.append(jnp.concatenate(pieces, axis=1))
        versions, slope = first_level(dot(jnp.concatenate(rows, axis=0), weights), t)
        for p in range(4):
            first, second = 32 * p, 32 * p + 16
            for b, value in versions:
                before = jnp.concatenate([value[second : second + 8, 128:256], jnp.zeros((8, 128), F32)], axis=0)
                outer_short[b, p, 0:16, :] = before.astype(BF)
                outer_short[b, p, 16:32, :] = short_pair(value, first).astype(BF)
                outer_act[b, p, 0:16, :] = value[second : second + 16, 128:256].astype(BF)
                outer_act[b, p, 16:32, :] = value[first : first + 16, 0:128].astype(BF)
                outer_act[b, p, 32:48, :] = value[first : first + 16, 128:256].astype(BF)
                outer_act[b, p, 48:64, :] = value[second : second + 16, 0:128].astype(BF)
            outer_slope[p, t] = short_pair(slope, first)

    lhs = []
    for k in range(2):
        planes = [(b, 2 * k + a - 1) for a in range(3) for b in range(3)]
        lhs.append(
            jnp.concatenate([outer_act[b, p] if p >= 0 else jnp.zeros((64, 128), BF) for b, p in planes], axis=1)
        )
    out = dot(jnp.concatenate(lhs, axis=0), w_two[...])
    pairs, pairs_next, delta, patches = [], [], [], []
    for k in range(2):
        own = out[64 * k : 64 * k + 64]
        pre = jnp.concatenate(
            [own[16:48, 0:128], ends_ref[k, 0], own[48:64, 0:128]], axis=0
        ) + jnp.concatenate([own[0:48, 128:256], ends_ref[k, 1]], axis=0)
        feat, value = second_level(pre, jnp.concatenate([cot_ref[k, 0:48, :], cot_y[k]], axis=0))
        feat_ref[k, :, 0:384] = jnp.concatenate([feat[16 * m : 16 * m + 8] for m in range(3)], axis=1).astype(BF)
        feat_ref[k, :, 384:2048] = feat_in[k]
        copies.append(pltpu.make_async_copy(feat_ref.at[k], feat_hbm.at[k], sems.at[k]))
        copies[-1].start()
        value = value.reshape(4, 16, 128)
        outer = value[:, 0:8].reshape(32, 128)
        here = jnp.concatenate([outer[0:24], here_in[k], outer[24:32]], axis=0)
        outer_after = value[:, 1:9].reshape(32, 128)
        after = jnp.concatenate([outer_after[0:24], after_in[k], outer_after[24:32]], axis=0)
        pairs.append(jnp.concatenate([here[0:128], here[8:136]], axis=1).astype(BF))
        pairs_next.append(jnp.concatenate([after[0:128], after[8:136]], axis=1).astype(BF))
        zero = jnp.zeros((8, 128), F32)
        both = [
            jnp.concatenate([zero, zero, outer[0:24], zero], axis=0),
            jnp.concatenate([outer[0:8], zero, outer[8:24], zero, zero], axis=0),
        ]
        delta.append(jnp.concatenate(both, axis=1).astype(BF))
        short = []
        for a in range(3):
            for b in range(3):
                p = 2 * k + a - 1
                if p < 0:
                    short.append(jnp.zeros((48, 128), BF))
                else:
                    short.append(jnp.concatenate([outer_short[b, p], short_act[b, p, 0:16, :]], axis=0))
        patches.append(jnp.concatenate(short, axis=1))
    grad = grad_in[...] + dot(jnp.concatenate(delta, axis=0), jnp.concatenate(patches, axis=0), ((0,), (0,)))

    place = iota((64, 128), 1) >> 5
    turned = []
    for ab in range(9):
        a0, a1, a2 = (grad[64 * j : 64 * j + 64, 128 * ab : 128 * ab + 128] for j in range(3))
        r0, r1, r2 = (pltpu.roll(a, 64, 1) for a in (a0, a1, a2))
        joined = jnp.where(place == 0, a0 + r1, jnp.where(place == 1, a1 + r2, a1 + r0))
        shift = (3 * ab - 1) % 4
        other = (shift + 2) % 4
        outer = pltpu.roll(joined, 32 * shift, 1) if shift else joined
        inner = pltpu.roll(joined, 32 * other, 1) if other else joined
        turned += [outer, inner, outer]
    turned.append(jnp.zeros((64, 128), F32))
    for v in range(7):
        t0, t1, t2, t3 = turned[4 * v : 4 * v + 4]
        total[:, 128 * v : 128 * v + 128] = jnp.where(
            place < 2, jnp.where(place == 0, t0, t1), jnp.where(place == 2, t2, t3)
        )

    lhs_rows, rhs_rows = [], []
    for p in range(4):
        depth = [(1, p // 2)] if p % 2 == 0 else [(2, (p - 1) // 2), (0, (p + 1) // 2)]
        for t in range(2):
            width = [(1, pairs)] if t == 0 else [(2, pairs), (0, pairs_next)]
            taps = [(3 * a + b, source[k]) for a, k in depth if k < 2 for b, source in width]
            level = dot(
                jnp.concatenate([source for _, source in taps], axis=1),
                jnp.concatenate([w_two[128 * tap : 128 * tap + 128, :] for tap, _ in taps], axis=1),
                ((1,), (1,)),
            )
            level = level.astype(BF).astype(F32)
            for m in range(16):
                rows_out[m, pl.ds(t, 8, stride=2), :] = level[8 * m : 8 * m + 8]
            slope = jnp.concatenate([outer_slope[p, t], slope_ref[p, t]], axis=0)
            value = level * slope
            blocks = [
                jnp.concatenate([value[16 * n : 16 * n + 8], value[16 * n + 8 : 16 * n + 16]], axis=1)
                for n in (1, 2, 3, 4, 5, 6, 7, 0)
            ]
            lhs_rows.append(jnp.concatenate(blocks, axis=0).astype(BF))
            rhs_rows.append(
                jnp.concatenate([window(SLOTS[t][b], 2 * p + a - 1) for a in range(3) for b in range(3)], axis=1)
            )
        level_ref[p] = jnp.concatenate([rows_out[m] for m in range(16)], axis=1).astype(BF)
        copies.append(pltpu.make_async_copy(level_ref.at[p], level_hbm.at[p], sems.at[2 + p]))
        copies[-1].start()
    grad = dot(jnp.concatenate(lhs_rows, axis=0), jnp.concatenate(rhs_rows, axis=0), ((0,), (0,)))

    place = iota((32, 128), 1)
    found = jnp.zeros((32, 128), F32)
    for tap in range(9):
        some = jnp.zeros((32, 128), F32)
        for t in range(8):
            piece = grad[32 * t : 32 * t + 32, 128 * tap : 128 * tap + 128]
            shift = (3 * tap - 2 * t) % 128
            some = some + (pltpu.roll(piece, shift, 1) if shift else piece)
        local = place & 31
        found = jnp.where((local >= 3 * tap) & (local < 3 * tap + 3), some, found)
    total[:, 896:1024] = jnp.zeros((64, 128), F32)
    tall, short = 64 // ranks, 32 // ranks
    for d in range(ranks):
        total[tall * d : tall * d + short, 896:1024] = found[short * d : short * d + short]
    rank = lax.axis_index("dp")
    for step, out in enumerate(dealt):
        if tall % 8 == 0:
            start = pl.multiple_of((rank ^ step) * tall, tall)
            picked = total[pl.ds(start, tall), :]
        else:
            picked = total[0:tall, :]
            for d in range(1, ranks):
                picked = jnp.where((rank ^ step) == d, total[d * tall : d * tall + tall, :], picked)
        out[...] = picked.astype(BF)
    for copy in copies:
        copy.wait()


def sum_kernel(*refs):
    parts, out_ref = refs[:-1], refs[-1]
    values = [ref[...].astype(F32) for ref in parts]
    while len(values) > 1:
        values = [values[i] + values[i + 1] for i in range(0, len(values), 2)]
    out_ref[...] = values[0].astype(out_ref.dtype)


def share_kernel(mine_ref, first_ref, second_ref, out_ref):
    first = first_ref[...].astype(F32)
    odd = position("gx")[0]
    out_ref[...] = first + jnp.where(odd, second_ref[...], mine_ref[...]).astype(F32)


def last_kernel(scale_one, scale_two, *refs):
    parts, (one_ref, two_ref) = refs[:-2], refs[-2:]
    values = [ref[...].astype(F32) for ref in parts]
    while len(values) > 1:
        values = [values[i] + values[i + 1] for i in range(0, len(values), 2)]
    value = values[0]
    tall = value.shape[0]
    short = tall // 2
    scaled = value[:, 0:896] * scale_two
    for tap in range(27):
        two_ref[tap] = scaled[:, 32 * tap : 32 * tap + 32]
    rows = value[0:short, 896:1024] * scale_one
    if short < 8:
        rows = jnp.concatenate([rows, jnp.zeros((8 - short, 128), F32)], axis=0)
    turned = rows.T
    for c in range(3):
        one_ref[:, c, :] = turned[32 * c : 32 * c + 27, 0:short]


def call(kernel, outs, args, scratch=(), space=pltpu.VMEM, in_hbm=0, flops=0):
    spaces = [pltpu.HBM] * in_hbm + [pltpu.VMEM] * (len(outs) - in_hbm)
    return pl.pallas_call(
        kernel,
        out_shape=outs,
        in_specs=[pl.BlockSpec(memory_space=space)] * len(args),
        out_specs=[pl.BlockSpec(memory_space=kind) for kind in spaces],
        scratch_shapes=list(scratch),
        compiler_params=pltpu.CompilerParams(vmem_limit_bytes=VMEM_LIMIT),
        cost_estimate=pl.CostEstimate(flops=flops, bytes_accessed=1 << 20, transcendentals=0),
    )(*args)


def shape(dims, dtype):
    return jax.ShapeDtypeStruct(dims, dtype)


def exchange(value, axis, step):
    return lax.ppermute(value, axis, [(i, i ^ step) for i in range(lax.axis_size(axis))])


def trade_shared(value, even_step, odd_step):
    count, columns, ranks = lax.axis_size("gy"), lax.axis_size("gx"), lax.axis_size("dp")
    pairs = []
    for d in range(ranks):
        for g in range(columns):
            for i in range(count):
                to_d, to_i = d, i ^ (odd_step if g % 2 else even_step)
                if g % 2 == 0 and even_step == 0:
                    to_d = (d ^ 1) % ranks
                pairs.append(((d * columns + g) * count + i, (to_d * columns + g) * count + to_i))
    return lax.ppermute(value, ("dp", "gx", "gy"), pairs)


def body(magnetic, kernel_one, kernel_two, cotangent):
    ranks, count_gx, count_gy = (lax.axis_size(axis) for axis in ("dp", "gx", "gy"))
    depth = magnetic.shape[2]
    samples_all = magnetic.shape[0] * ranks
    cells_x = magnetic.shape[3] * count_gx
    cells_y = magnetic.shape[4] * count_gy
    scale_one = 1.0 / math.sqrt(samples_all * (depth // 2) * (cells_x // 2) * (cells_y // 2))
    scale_two = 1.0 / math.sqrt(samples_all * (depth // 4) * (cells_x // 4) * (cells_y // 4))
    field = magnetic.reshape(24, 32, 128)
    cot = cotangent.reshape(2, 8, 2048)
    one = kernel_one.reshape(27, 3, 32)
    two = kernel_two.reshape(864, 64)

    swaps_x, swaps_y = swaps("gx"), swaps("gy")
    nx, ny = len(swaps_x), len(swaps_y)
    operands = [pltpu.with_memory_space_constraint(array, pltpu.HBM) for array in (field, cot, one, two)]
    field, cot, one, two, *edges = call(
        lambda *refs: edge_x_kernel(nx, *refs),
        [shape(array.shape, BF) for array in operands] + [shape((128, 128), BF)] * nx,
        operands,
        [pltpu.VMEM((128, 128), F32), pltpu.SemaphoreType.DMA((4,))],
        space=pltpu.HBM,
    )
    got_x = [lax.ppermute(edge, ("dp", "gx"), pairs) for edge, pairs in zip(edges, swaps_x)]
    w_one, w_two, picks = call(
        weights_kernel,
        [shape((1152, 256), BF), shape((1152, 256), BF), shape((256, 2048), BF)],
        (one, two),
        [pltpu.VMEM((88, 32), F32)],
        flops=1 << 30,
    )
    split, *edges = call(
        lambda *refs: edge_y_kernel(nx, ny, *refs),
        [shape((5, 384, 128), BF)] + [shape((80, 128), BF)] * ny,
        (field, cot, *got_x),
        [pltpu.VMEM((24, 72, 128), F32)],
    )
    got_y = [lax.ppermute(edge, ("dp", "gy"), pairs) for edge, pairs in zip(edges, swaps_y)]
    first = call(
        lambda *refs: windows_kernel(nx, *refs),
        [
            shape((5, 8, 64, 128), BF),
            shape((5, 128, 256), BF),
            shape((3, 4, 112, 128), BF),
            shape((4, 2, 112, 128), F32),
            shape((2, 256, 128), F32),
            shape((2, 2, 16, 128), F32),
            shape((2, 8, 1664), BF),
            shape((2, 104, 128), F32),
            shape((2, 104, 128), F32),
            shape((256, 1152), F32),
        ],
        (split, w_one, w_two, cot, *got_x),
        [pltpu.VMEM((5, 8, 112, 128), BF), pltpu.VMEM((3, 4, 224, 128), BF)],
        flops=1 << 31,
    )
    tall = 64 // ranks
    features, level, *dealt = call(
        lambda *refs: main_kernel(ny, ranks, *refs),
        [shape((2, 8, 2048), BF), shape((4, 16, 2048), BF)] + [shape((tall, 1024), BF)] * ranks,
        (*first, picks, w_one, w_two, *got_y),
        [
            pltpu.VMEM((5, 8, 32, 128), BF),
            pltpu.VMEM((5, 8, 16, 128), BF),
            pltpu.VMEM((3, 4, 64, 128), BF),
            pltpu.VMEM((3, 4, 32, 128), BF),
            pltpu.VMEM((4, 2, 16, 128), F32),
            pltpu.VMEM((16, 16, 128), F32),
            pltpu.VMEM((64, 1024), F32),
            pltpu.VMEM((2, 8, 2048), BF),
            pltpu.VMEM((4, 16, 2048), BF),
            pltpu.SemaphoreType.DMA((6,)),
        ],
        in_hbm=2,
    )
    terms = [exchange(dealt[step], "dp", step) for step in (ranks - 1, *range(1, ranks - 1))] + dealt[:1]
    mine, = call(sum_kernel, [shape((tall, 1024), BF)], terms)
    step = 1
    while step < count_gx:
        mine, = call(sum_kernel, [shape((tall, 1024), BF)], (mine, exchange(mine, "gx", step)))
        step *= 2
    if count_gy == 4:
        terms = [mine, trade_shared(mine, 1, 2), trade_shared(mine, 0, 3)]
        mine, = call(share_kernel, [shape((tall, 1024), F32)], terms)
        terms = [mine, exchange(mine, "gx", 1)]
    else:
        terms = [mine] + [exchange(mine, "gy", step) for step in range(1, count_gy)]
    grad_one, grad_two = call(
        lambda *refs: last_kernel(scale_one, scale_two, *refs),
        [shape((27, 3, tall // 2), F32), shape((27, tall, 32), F32)],
        terms,
    )
    grad_one = grad_one.reshape(3, 3, 3, 3, tall // 2)
    grad_two = jnp.transpose(grad_two.reshape(3, 3, 3, tall, 32), (0, 1, 2, 4, 3))
    return (
        features.reshape(1, 2, 8, 2048),
        level.reshape(1, 4, 16, 2048),
        grad_one,
        grad_two,
    )


def solution(mesh):
    in_specs = (P("dp", None, None, "gx", "gy"), P(), P(), P("dp", None, "gx", "gy"))
    out_specs = (
        P("dp", None, "gx", "gy"),
        P("dp", None, "gx", "gy"),
        P(None, None, None, None, "dp"),
        P(None, None, None, None, "dp"),
    )
    return jax.shard_map(body, mesh=mesh, in_specs=in_specs, out_specs=out_specs, check_vma=False)
```

```python
import math

import jax
import jax.numpy as jnp
from jax import lax
from jax.experimental import pallas as pl
from jax.experimental.pallas import tpu as pltpu
from jax.sharding import PartitionSpec as P

BF = jnp.bfloat16
F32 = jnp.float32
VMEM_LIMIT = 32 * 1024 * 1024


def iota(shape, dim):
    return lax.broadcasted_iota(jnp.int32, shape, dim)


def dot(lhs, rhs, contract=((1,), (0,))):
    return lax.dot_general(lhs, rhs, (contract, ((), ())), preferred_element_type=F32)


def swaps(axis):
    count, ranks = lax.axis_size(axis), lax.axis_size("dp")
    found = []
    for first in range(min(2, count - 1)):
        pairs = []
        for d in range(ranks):
            for i in range(count):
                other = i + 1 if i % 2 == first else i - 1
                if 0 <= other < count:
                    pairs.append((d * count + i, d * count + other))
                else:
                    pairs.append((d * count + i, (d ^ 1) % ranks * count + i))
        found.append(pairs)
    return found


def position(axis):
    index = lax.axis_index(axis)
    return lax.rem(index, 2) == 1, index == 0, index == lax.axis_size(axis) - 1


def from_low(place, got):
    odd, first, _ = place
    second = got[1] if len(got) > 1 else got[0]
    return jnp.where(first, 0.0, jnp.where(odd, got[0], second))


def from_high(place, got):
    odd, _, last = place
    second = got[1] if len(got) > 1 else got[0]
    return jnp.where(last, 0.0, jnp.where(odd, second, got[0]))


def edge_x_kernel(count, *refs):
    hbm, refs = refs[:4], refs[4:]
    held, outs, (stage, sems) = refs[:4], refs[4 : 4 + count], refs[4 + count :]
    fetches = [pltpu.make_async_copy(hbm[i], held[i], sems.at[i]) for i in range(4)]
    for fetch in fetches:
        fetch.start()
    mag_ref, cot_ref = held[:2]
    odd = position("gx")[0]
    planes = mag_ref.shape[0]
    blocks = cot_ref.shape[2] // 128
    for fetch in fetches:
        fetch.wait()
    field = mag_ref[...].astype(F32)
    low = field[:, 0:4, :]
    high = field[:, field.shape[1] - 4 :, :]
    cot = [cot_ref[k].astype(F32)[0:1, :] for k in range(2)]
    for turn in range(count):
        toward_high = odd if turn == 1 else jnp.logical_not(odd)
        picked = jnp.where(toward_high, high, low)
        for g in range(planes):
            stage[4 * g : 4 * g + 4, :] = picked[g]
        for k in range(2):
            for m in range(blocks):
                row = 4 * planes + 16 * k + m
                stage[row : row + 1, :] = cot[k][:, 128 * m : 128 * m + 128]
        outs[turn][...] = stage[...].astype(BF)


def edge_y_kernel(count_x, count_y, mag_ref, cot_ref, *refs):
    got_refs, refs = refs[:count_x], refs[count_x:]
    split_ref, outs = refs[0], refs[1 : 1 + count_y]
    tall, = refs[1 + count_y :]
    place_x, place_y = position("gx"), position("gy")
    planes = mag_ref.shape[0]
    got = [ref[...].astype(F32) for ref in got_refs]
    low = from_low(place_x, got)
    high = from_high(place_x, got)
    zeros = jnp.zeros((24, 128), F32)
    for g in range(planes):
        edge = low[4 * g : 4 * g + 4, :]
        tall[g, 0:8, :] = jnp.broadcast_to(edge[3:4, :], (8, 128))
        tall[g, 8:40, :] = mag_ref[g].astype(F32)
        tall[g, 40:44, :] = high[4 * g : 4 * g + 4, :]
        tall[g, 44:68, :] = zeros
        tall[g, 68:72, :] = edge
    starts = (8, 9, 10, 11, 7)
    split = []
    for slot in range(5):
        parts = [tall[g, pl.ds(starts[slot], 16, stride=4), :].astype(BF) for g in range(planes)]
        whole = jnp.concatenate(parts, axis=0)
        split_ref[slot] = whole
        split.append(whole)
    rows = planes // 3 * 16
    lhs = jnp.concatenate(
        [split[s][rows * c : rows * c + rows] for s in range(4) for c in range(3)], axis=1
    )
    lane = iota((128, 128), 1)
    cell = iota((128, 128), 0)
    slot = lane & 3
    wanted = jnp.where(lane < 64, 124 + slot, slot)
    group = (lane & 63) >> 2
    picks = []
    for s in range(4):
        for c in range(3):
            hit = (group == 4 * s + c) & (cell == wanted)
            picks.append(jnp.where(hit, 1.0, 0.0).astype(BF))
    both = dot(lhs, jnp.concatenate(picks, axis=0)).reshape(4, 2, 16, 128)
    lower, upper = both[:, 0].reshape(64, 128), both[:, 1].reshape(64, 128)
    left = iota((64, 128), 1) < 64
    toward = [
        jnp.where(left, lower, pltpu.roll(upper, 64, 1)),
        jnp.where(left, pltpu.roll(lower, 64, 1), upper),
    ]
    cot_rows = []
    for k in range(2):
        own = cot_ref[k].astype(F32)[:, 0:128]
        row = 4 * planes + 16 * k
        cot_rows.append(jnp.concatenate([own, high[row : row + 1, :], jnp.zeros((7, 128), F32)], axis=0))
    cot_rows = jnp.where(iota((16, 128), 1) < 64, cot_rows[0], pltpu.roll(cot_rows[1], 64, 1))
    odd = place_y[0]
    for turn in range(count_y):
        toward_high = odd if turn == 1 else jnp.logical_not(odd)
        outs[turn][0:64, :] = jnp.where(toward_high, toward[0], toward[1]).astype(BF)
        outs[turn][64:80, :] = cot_rows.astype(BF)


def weights_kernel(one_ref, two_ref, w_one, w_two, halo_ref, rows_one):
    lane = iota((32, 256), 1)
    spread = jnp.where(iota((32, 256), 0) == (lane & 31), 1.0, 0.0).astype(BF)
    rows_one[80:88, :] = jnp.zeros((8, 32), F32)
    for i in range(27):
        rows_one[3 * i : 3 * i + 3, :] = one_ref[i].astype(F32)
    wide = dot(rows_one[...].astype(BF), spread)
    window = iota((32, 256), 0) - 2 * (lane >> 5)
    for tap in range(9):
        for c in range(3):
            block = jnp.zeros((32, 256), F32)
            for e in range(3):
                row = (3 * tap + e) * 3 + c
                block = jnp.where(window == e, wide[row : row + 1, :], block)
            w_one[128 * tap + 32 * c : 128 * tap + 32 * c + 32, :] = block.astype(BF)
        w_one[128 * tap + 96 : 128 * tap + 128, :] = jnp.zeros((32, 256), BF)

    lane = iota((64, 128), 1)
    spread = jnp.where(iota((64, 128), 0) == (lane & 63), 1.0, 0.0).astype(BF)
    twice = dot(two_ref[...], spread)
    left = iota((32, 128), 1) < 64
    for tap in range(9):
        k0, k1, k2 = (twice[32 * (3 * tap + e) : 32 * (3 * tap + e) + 32] for e in range(3))
        base = 128 * tap
        w_two[base : base + 32, 0:128] = jnp.where(left, k1, 0.0).astype(BF)
        w_two[base + 32 : base + 64, 0:128] = jnp.where(left, k2, k0).astype(BF)
        w_two[base + 64 : base + 96, 0:128] = jnp.where(left, 0.0, k1).astype(BF)
        w_two[base + 96 : base + 128, 0:128] = jnp.where(left, 0.0, k2).astype(BF)
        w_two[base : base + 96, 128:256] = jnp.zeros((96, 128), BF)
        w_two[base + 96 : base + 128, 128:256] = jnp.where(left, k0, 0.0).astype(BF)

    lane = iota((256, 256), 1)
    code = iota((256, 256), 0)
    offset = lane & 31
    part = (lane & 127) >> 5
    wanted = jnp.where(
        lane < 128,
        jnp.where(offset == 0, 3, -999),
        jnp.where(
            (offset >= 1) & (offset <= 4), 127 + offset, jnp.where((offset >= 14) & (offset <= 16), offset - 13, -999)
        ),
    )
    wanted = jnp.where(part < 3, wanted + 4 * part, -999)
    for s in range(4):
        for parity in range(2):
            hit = code - (64 * parity + 16 * s) == wanted
            base = 256 * (2 * s + parity)
            halo_ref[:, base : base + 256] = jnp.where(hit, 1.0, 0.0).astype(BF)


SLOTS = ((4, 0, 1), (1, 2, 3))


def first_level(pre, t):
    sig = jax.nn.sigmoid(pre)
    hidden = pre * sig
    slope = sig * (1.0 + pre * (1.0 - sig))
    if t == 0:
        return [(1, hidden)], slope
    rows, width = hidden.shape
    later = hidden.reshape(rows // 16, 16, width)
    later = jnp.concatenate([later[:, 15:16], later[:, 0:15]], axis=1).reshape(rows, width)
    return [(2, hidden), (0, later)], slope


def second_level(pre, cot):
    sig = jax.nn.sigmoid(pre)
    return pre * sig, cot * (sig * (1.0 + pre * (1.0 - sig)))


def short_pair(value, row):
    return jnp.concatenate([value[row : row + 8, 0:128], value[row : row + 8, 128:256]], axis=0)


def windows_kernel(count_x, split_ref, w_one, w_two, cot_ref, *refs):
    gx_refs, refs = refs[:count_x], refs[count_x:]
    short_ref, outer_ref, short_act, slope_ref, cot_all = refs[:5]
    ends_ref, feat_ref, here_ref, after_ref, grad_ref, inner_ref, act_ref = refs[5:]
    high_x = from_high(position("gx"), [ref[96:128, :].astype(F32) for ref in gx_refs])
    for k in range(2):
        cot = cot_ref[k].astype(F32)
        for m in range(16):
            row = 16 * k + m
            cot_all[k, 16 * m : 16 * m + 8, :] = cot[:, 128 * m : 128 * m + 128]
            cot_all[k, 16 * m + 8 : 16 * m + 16, :] = jnp.where(
                iota((8, 128), 0) == 0, high_x[row : row + 1, :], 0.0
            )

    lane = iota((128, 1152), 1)
    cell = iota((128, 1152), 0)
    block = lane >> 7
    offset = lane & 31
    part = (lane & 127) >> 5
    wanted = jnp.where(offset <= 16, 16 * block - 1 + offset, -9)
    wanted = jnp.where(block == 8, jnp.where(offset == 0, 127, -9), wanted)
    hit = cell == wanted
    picks = jnp.concatenate(
        [jnp.where(hit & (part == c), 1.0, 0.0).astype(BF) for c in range(3)], axis=0
    )
    for s in range(5):
        lhs = jnp.concatenate([split_ref[s, 128 * c : 128 * c + 128, :] for c in range(3)], axis=1)
        exact = dot(lhs, picks)
        found = exact.astype(BF)
        for z in range(8):
            for q in range(4):
                first = exact[16 * z : 16 * z + 8, 256 * q + 128 : 256 * q + 256]
                if q < 3:
                    second = exact[16 * z : 16 * z + 8, 256 * q + 256 : 256 * q + 384]
                else:
                    second = jnp.zeros((8, 128), F32)
                short_ref[s, z, 16 * q : 16 * q + 16, :] = jnp.concatenate([first, second], axis=0).astype(BF)
        for n in range(1, 8):
            for z in range(8):
                inner_ref[s, z, 16 * n - 16 : 16 * n, :] = found[16 * z : 16 * z + 16, 128 * n : 128 * n + 128]
        outer_ref[s, :, 0:128] = found[:, 0:128]
        outer_ref[s, :, 128:256] = found[:, 1024:1152]
    weights = w_one[...]
    for p in range(4):
        for t in range(2):
            pieces = []
            for a in range(3):
                for b in range(3):
                    z = 2 * p + a - 1
                    pieces.append(inner_ref[SLOTS[t][b], z] if z >= 0 else jnp.zeros((112, 128), BF))
            versions, slope = first_level(dot(jnp.concatenate(pieces, axis=1), weights), t)
            for b, value in versions:
                for n in range(7):
                    short_act[b, p, 16 * n : 16 * n + 16, :] = short_pair(value, 16 * n).astype(BF)
                value = value.astype(BF)
                for n in range(7):
                    act_ref[b, p, 32 * n : 32 * n + 16, :] = value[16 * n : 16 * n + 16, 0:128]
                    act_ref[b, p, 32 * n + 16 : 32 * n + 32, :] = value[16 * n : 16 * n + 16, 128:256]
            for n in range(7):
                slope_ref[p, t, 16 * n : 16 * n + 16, :] = short_pair(slope, 16 * n)
    weights = w_two[...]
    delta, patches = [], []
    for k in range(2):
        planes = [(b, 2 * k + a - 1) for a in range(3) for b in range(3)]
        lhs = [act_ref[b, p] if p >= 0 else jnp.zeros((224, 128), BF) for b, p in planes]
        out = dot(jnp.concatenate(lhs, axis=1), weights)
        ends_ref[k, 0] = out[0:16, 0:128]
        ends_ref[k, 1] = out[208:224, 128:256]
        feat, value = second_level(out[16:224, 0:128] + out[0:208, 128:256], cot_all[k, 48:256, :])
        feat_ref[k] = jnp.concatenate([feat[16 * m : 16 * m + 8] for m in range(13)], axis=1).astype(BF)
        value = value.reshape(13, 16, 128)
        here = value[:, 0:8].reshape(104, 128)
        here_ref[k] = here
        after_ref[k] = value[:, 1:9].reshape(104, 128)
        zero = jnp.zeros((8, 128), F32)
        both = [jnp.concatenate([zero, here], axis=0), jnp.concatenate([here, zero], axis=0)]
        delta.append(jnp.concatenate(both, axis=1).astype(BF))
        short = [short_act[b, p] if p >= 0 else jnp.zeros((112, 128), BF) for b, p in planes]
        patches.append(jnp.concatenate(short, axis=1))
    delta, patches = jnp.concatenate(delta, axis=0), jnp.concatenate(patches, axis=0)
    for first in range(0, 1152, 256):
        last = min(first + 256, 1152)
        grad_ref[:, first:last] = dot(delta, patches[:, first:last], ((0,), (0,)))[0:192]


def main_kernel(
    count_y,
    ranks,
    short_ref,
    outer_ref,
    short_act,
    slope_ref,
    cot_ref,
    ends_ref,
    feat_in,
    here_in,
    after_in,
    grad_in,
    halo_ref,
    w_one,
    w_two,
    *refs,
):
    gy_refs, refs = refs[:count_y], refs[count_y:]
    feat_hbm, level_hbm, refs = refs[0], refs[1], refs[2:]
    dealt, refs = refs[:ranks], refs[ranks:]
    edges, short_edges, outer_act, outer_short, outer_slope, rows_out, total, feat_ref, level_ref, sems = refs
    place_y = position("gy")
    copies = []

    got_y = [ref[...].astype(F32) for ref in gy_refs]
    low_y = from_low(place_y, got_y)
    high_y = from_high(place_y, got_y)
    halo = jnp.concatenate([low_y[0:64], high_y[0:64]], axis=1).astype(BF)
    first_half = iota((16, 128), 1) < 64
    cot_y = [jnp.where(first_half, value, 0.0) for value in (high_y[64:80], pltpu.roll(high_y[64:80], 64, 1))]
    brought = dot(halo, halo_ref[...])
    for s in range(5):
        base = 512 * min(s, 3)
        found = [brought[:, base + 256 * parity : base + 256 * parity + 256].reshape(4, 16, 256) for parity in range(2)]
        edge = jnp.stack(found, axis=1).reshape(8, 16, 256)
        if s == 4:
            edge = jnp.concatenate([edge[:, 15:16], edge[:, 0:15]], axis=1)
        exact = outer_ref[s].astype(F32) + edge.reshape(128, 256)
        value = exact.astype(BF)
        for z in range(8):
            edges[s, z, 0:16, :] = value[16 * z : 16 * z + 16, 0:128]
            edges[s, z, 16:32, :] = value[16 * z : 16 * z + 16, 128:256]
            other = short_ref[s, z, 48:64, :].astype(F32)
            short_edges[s, z] = jnp.concatenate([other[0:8], exact[16 * z : 16 * z + 8, 0:128]], axis=0).astype(BF)

    def window(s, z):
        if z < 0:
            return jnp.zeros((64, 128), BF)
        return jnp.concatenate([short_ref[s, z, 0:48, :], short_edges[s, z]], axis=0)

    weights = w_one[...]
    for t in range(2):
        rows = []
        for p in range(4):
            pieces = []
            for a in range(3):
                for b in range(3):
                    z = 2 * p + a - 1
                    pieces.append(edges[SLOTS[t][b], z] if z >= 0 else jnp.zeros((32, 128), BF))
            rows.append(jnp.concatenate(pieces, axis=1))
        versions, slope = first_level(dot(jnp.concatenate(rows, axis=0), weights), t)
        for p in range(4):
            first, second = 32 * p, 32 * p + 16
            for b, value in versions:
                before = jnp.concatenate([value[second : second + 8, 128:256], jnp.zeros((8, 128), F32)], axis=0)
                outer_short[b, p, 0:16, :] = before.astype(BF)
                outer_short[b, p, 16:32, :] = short_pair(value, first).astype(BF)
                outer_act[b, p, 0:16, :] = value[second : second + 16, 128:256].astype(BF)
                outer_act[b, p, 16:32, :] = value[first : first + 16, 0:128].astype(BF)
                outer_act[b, p, 32:48, :] = value[first : first + 16, 128:256].astype(BF)
                outer_act[b, p, 48:64, :] = value[second : second + 16, 0:128].astype(BF)
            outer_slope[p, t] = short_pair(slope, first)

    lhs = []
    for k in range(2):
        planes = [(b, 2 * k + a - 1) for a in range(3) for b in range(3)]
        lhs.append(
            jnp.concatenate([outer_act[b, p] if p >= 0 else jnp.zeros((64, 128), BF) for b, p in planes], axis=1)
        )
    out = dot(jnp.concatenate(lhs, axis=0), w_two[...])
    pairs, pairs_next, delta, patches = [], [], [], []
    for k in range(2):
        own = out[64 * k : 64 * k + 64]
        pre = jnp.concatenate(
            [own[16:48, 0:128], ends_ref[k, 0], own[48:64, 0:128]], axis=0
        ) + jnp.concatenate([own[0:48, 128:256], ends_ref[k, 1]], axis=0)
        feat, value = second_level(pre, jnp.concatenate([cot_ref[k, 0:48, :], cot_y[k]], axis=0))
        feat_ref[k, :, 0:384] = jnp.concatenate([feat[16 * m : 16 * m + 8] for m in range(3)], axis=1).astype(BF)
        feat_ref[k, :, 384:2048] = feat_in[k]
        copies.append(pltpu.make_async_copy(feat_ref.at[k], feat_hbm.at[k], sems.at[k]))
        copies[-1].start()
        value = value.reshape(4, 16, 128)
        outer = value[:, 0:8].reshape(32, 128)
        here = jnp.concatenate([outer[0:24], here_in[k], outer[24:32]], axis=0)
        outer_after = value[:, 1:9].reshape(32, 128)
        after = jnp.concatenate([outer_after[0:24], after_in[k], outer_after[24:32]], axis=0)
        pairs.append(jnp.concatenate([here[0:128], here[8:136]], axis=1).astype(BF))
        pairs_next.append(jnp.concatenate([after[0:128], after[8:136]], axis=1).astype(BF))
        zero = jnp.zeros((8, 128), F32)
        both = [
            jnp.concatenate([zero, zero, outer[0:24], zero], axis=0),
            jnp.concatenate([outer[0:8], zero, outer[8:24], zero, zero], axis=0),
        ]
        delta.append(jnp.concatenate(both, axis=1).astype(BF))
        short = []
        for a in range(3):
            for b in range(3):
                p = 2 * k + a - 1
                if p < 0:
                    short.append(jnp.zeros((48, 128), BF))
                else:
                    short.append(jnp.concatenate([outer_short[b, p], short_act[b, p, 0:16, :]], axis=0))
        patches.append(jnp.concatenate(short, axis=1))
    delta, patches = jnp.concatenate(delta, axis=0), jnp.concatenate(patches, axis=0)

    place = iota((64, 128), 1) >> 5
    turned = []
    for ab in range(9):
        if ab % 2 == 0:
            first, last = 128 * ab, min(128 * ab + 256, 1152)
            grad = dot(delta, patches[:, first:last], ((0,), (0,)))[0:192] + grad_in[:, first:last]
        column = 128 * (ab % 2)
        a0, a1, a2 = (grad[64 * j : 64 * j + 64, column : column + 128] for j in range(3))
        r0, r1, r2 = (pltpu.roll(a, 64, 1) for a in (a0, a1, a2))
        joined = jnp.where(place == 0, a0 + r1, jnp.where(place == 1, a1 + r2, a1 + r0))
        shift = (3 * ab - 1) % 4
        other = (shift + 2) % 4
        outer = pltpu.roll(joined, 32 * shift, 1) if shift else joined
        inner = pltpu.roll(joined, 32 * other, 1) if other else joined
        turned += [outer, inner, outer]
    turned.append(jnp.zeros((64, 128), F32))
    for v in range(7):
        t0, t1, t2, t3 = turned[4 * v : 4 * v + 4]
        total[:, 128 * v : 128 * v + 128] = jnp.where(
            place < 2, jnp.where(place == 0, t0, t1), jnp.where(place == 2, t2, t3)
        )

    lhs_rows, rhs_rows = [], []
    for p in range(4):
        depth = [(1, p // 2)] if p % 2 == 0 else [(2, (p - 1) // 2), (0, (p + 1) // 2)]
        for t in range(2):
            width = [(1, pairs)] if t == 0 else [(2, pairs), (0, pairs_next)]
            taps = [(3 * a + b, source[k]) for a, k in depth if k < 2 for b, source in width]
            level = dot(
                jnp.concatenate([source for _, source in taps], axis=1),
                jnp.concatenate([w_two[128 * tap : 128 * tap + 128, :] for tap, _ in taps], axis=1),
                ((1,), (1,)),
            )
            level = level.astype(BF).astype(F32)
            for m in range(16):
                rows_out[m, pl.ds(t, 8, stride=2), :] = level[8 * m : 8 * m + 8]
            slope = jnp.concatenate([outer_slope[p, t], slope_ref[p, t]], axis=0)
            value = level * slope
            blocks = [
                jnp.concatenate([value[16 * n : 16 * n + 8], value[16 * n + 8 : 16 * n + 16]], axis=1)
                for n in (1, 2, 3, 4, 5, 6, 7, 0)
            ]
            lhs_rows.append(jnp.concatenate(blocks, axis=0).astype(BF))
            rhs_rows.append(
                jnp.concatenate([window(SLOTS[t][b], 2 * p + a - 1) for a in range(3) for b in range(3)], axis=1)
            )
        level_ref[p] = jnp.concatenate([rows_out[m] for m in range(16)], axis=1).astype(BF)
        copies.append(pltpu.make_async_copy(level_ref.at[p], level_hbm.at[p], sems.at[2 + p]))
        copies[-1].start()
    delta_one = jnp.concatenate(lhs_rows, axis=0).T
    windows = jnp.concatenate(rhs_rows, axis=0)

    place = iota((32, 128), 1)
    found = jnp.zeros((32, 128), F32)
    for tap in range(9):
        if tap % 2 == 0:
            grad = dot(delta_one, windows[:, 128 * tap : min(128 * tap + 256, 1152)])
        column = 128 * (tap % 2)
        some = jnp.zeros((32, 128), F32)
        for t in range(8):
            piece = grad[32 * t : 32 * t + 32, column : column + 128]
            shift = (3 * tap - 2 * t) % 128
            some = some + (pltpu.roll(piece, shift, 1) if shift else piece)
        local = place & 31
        found = jnp.where((local >= 3 * tap) & (local < 3 * tap + 3), some, found)
    total[:, 896:1024] = jnp.zeros((64, 128), F32)
    tall, short = 64 // ranks, 32 // ranks
    for d in range(ranks):
        total[tall * d : tall * d + short, 896:1024] = found[short * d : short * d + short]
    rank = lax.axis_index("dp")
    for step, out in enumerate(dealt):
        if tall % 8 == 0:
            start = pl.multiple_of((rank ^ step) * tall, tall)
            picked = total[pl.ds(start, tall), :]
        else:
            picked = total[0:tall, :]
            for d in range(1, ranks):
                picked = jnp.where((rank ^ step) == d, total[d * tall : d * tall + tall, :], picked)
        out[...] = picked.astype(BF)
    for copy in copies:
        copy.wait()


def sum_kernel(*refs):
    parts, out_ref = refs[:-1], refs[-1]
    values = [ref[...].astype(F32) for ref in parts]
    while len(values) > 1:
        values = [values[i] + values[i + 1] for i in range(0, len(values), 2)]
    out_ref[...] = values[0].astype(out_ref.dtype)


def share_kernel(mine_ref, first_ref, second_ref, out_ref):
    first = first_ref[...].astype(F32)
    odd = position("gx")[0]
    out_ref[...] = first + jnp.where(odd, second_ref[...], mine_ref[...]).astype(F32)


def last_kernel(scale_one, scale_two, *refs):
    parts, (one_ref, two_ref) = refs[:-2], refs[-2:]
    values = [ref[...].astype(F32) for ref in parts]
    while len(values) > 1:
        values = [values[i] + values[i + 1] for i in range(0, len(values), 2)]
    value = values[0]
    tall = value.shape[0]
    short = tall // 2
    scaled = value[:, 0:896] * scale_two
    for tap in range(27):
        two_ref[tap] = scaled[:, 32 * tap : 32 * tap + 32]
    rows = value[0:short, 896:1024] * scale_one
    if short < 8:
        rows = jnp.concatenate([rows, jnp.zeros((8 - short, 128), F32)], axis=0)
    turned = rows.T
    for c in range(3):
        one_ref[:, c, :] = turned[32 * c : 32 * c + 27, 0:short]


def call(kernel, outs, args, scratch=(), space=pltpu.VMEM, in_hbm=0, flops=0):
    spaces = [pltpu.HBM] * in_hbm + [pltpu.VMEM] * (len(outs) - in_hbm)
    return pl.pallas_call(
        kernel,
        out_shape=outs,
        in_specs=[pl.BlockSpec(memory_space=space)] * len(args),
        out_specs=[pl.BlockSpec(memory_space=kind) for kind in spaces],
        scratch_shapes=list(scratch),
        compiler_params=pltpu.CompilerParams(vmem_limit_bytes=VMEM_LIMIT),
        cost_estimate=pl.CostEstimate(flops=flops, bytes_accessed=1 << 20, transcendentals=0),
    )(*args)


def shape(dims, dtype):
    return jax.ShapeDtypeStruct(dims, dtype)


def exchange(value, axis, step):
    return lax.ppermute(value, axis, [(i, i ^ step) for i in range(lax.axis_size(axis))])


def trade_shared(value, even_step, odd_step):
    count, columns, ranks = lax.axis_size("gy"), lax.axis_size("gx"), lax.axis_size("dp")
    pairs = []
    for d in range(ranks):
        for g in range(columns):
            for i in range(count):
                to_d, to_i = d, i ^ (odd_step if g % 2 else even_step)
                if g % 2 == 0 and even_step == 0:
                    to_d = (d ^ 1) % ranks
                pairs.append(((d * columns + g) * count + i, (to_d * columns + g) * count + to_i))
    return lax.ppermute(value, ("dp", "gx", "gy"), pairs)


def body(magnetic, kernel_one, kernel_two, cotangent):
    ranks, count_gx, count_gy = (lax.axis_size(axis) for axis in ("dp", "gx", "gy"))
    depth = magnetic.shape[2]
    samples_all = magnetic.shape[0] * ranks
    cells_x = magnetic.shape[3] * count_gx
    cells_y = magnetic.shape[4] * count_gy
    scale_one = 1.0 / math.sqrt(samples_all * (depth // 2) * (cells_x // 2) * (cells_y // 2))
    scale_two = 1.0 / math.sqrt(samples_all * (depth // 4) * (cells_x // 4) * (cells_y // 4))
    field = magnetic.reshape(24, 32, 128)
    cot = cotangent.reshape(2, 8, 2048)
    one = kernel_one.reshape(27, 3, 32)
    two = kernel_two.reshape(864, 64)

    swaps_x, swaps_y = swaps("gx"), swaps("gy")
    nx, ny = len(swaps_x), len(swaps_y)
    operands = [pltpu.with_memory_space_constraint(array, pltpu.HBM) for array in (field, cot, one, two)]
    field, cot, one, two, *edges = call(
        lambda *refs: edge_x_kernel(nx, *refs),
        [shape(array.shape, BF) for array in operands] + [shape((128, 128), BF)] * nx,
        operands,
        [pltpu.VMEM((128, 128), F32), pltpu.SemaphoreType.DMA((4,))],
        space=pltpu.HBM,
    )
    got_x = [lax.ppermute(edge, ("dp", "gx"), pairs) for edge, pairs in zip(edges, swaps_x)]
    w_one, w_two, picks = call(
        weights_kernel,
        [shape((1152, 256), BF), shape((1152, 256), BF), shape((256, 2048), BF)],
        (one, two),
        [pltpu.VMEM((88, 32), F32)],
        flops=1 << 30,
    )
    split, *edges = call(
        lambda *refs: edge_y_kernel(nx, ny, *refs),
        [shape((5, 384, 128), BF)] + [shape((80, 128), BF)] * ny,
        (field, cot, *got_x),
        [pltpu.VMEM((24, 72, 128), F32)],
    )
    got_y = [lax.ppermute(edge, ("dp", "gy"), pairs) for edge, pairs in zip(edges, swaps_y)]
    first = call(
        lambda *refs: windows_kernel(nx, *refs),
        [
            shape((5, 8, 64, 128), BF),
            shape((5, 128, 256), BF),
            shape((3, 4, 112, 128), BF),
            shape((4, 2, 112, 128), F32),
            shape((2, 256, 128), F32),
            shape((2, 2, 16, 128), F32),
            shape((2, 8, 1664), BF),
            shape((2, 104, 128), F32),
            shape((2, 104, 128), F32),
            shape((192, 1152), F32),
        ],
        (split, w_one, w_two, cot, *got_x),
        [pltpu.VMEM((5, 8, 112, 128), BF), pltpu.VMEM((3, 4, 224, 128), BF)],
        flops=1 << 31,
    )
    tall = 64 // ranks
    features, level, *dealt = call(
        lambda *refs: main_kernel(ny, ranks, *refs),
        [shape((2, 8, 2048), BF), shape((4, 16, 2048), BF)] + [shape((tall, 1024), BF)] * ranks,
        (*first, picks, w_one, w_two, *got_y),
        [
            pltpu.VMEM((5, 8, 32, 128), BF),
            pltpu.VMEM((5, 8, 16, 128), BF),
            pltpu.VMEM((3, 4, 64, 128), BF),
            pltpu.VMEM((3, 4, 32, 128), BF),
            pltpu.VMEM((4, 2, 16, 128), F32),
            pltpu.VMEM((16, 16, 128), F32),
            pltpu.VMEM((64, 1024), F32),
            pltpu.VMEM((2, 8, 2048), BF),
            pltpu.VMEM((4, 16, 2048), BF),
            pltpu.SemaphoreType.DMA((6,)),
        ],
        in_hbm=2,
    )
    terms = [exchange(dealt[step], "dp", step) for step in (ranks - 1, *range(1, ranks - 1))] + dealt[:1]
    mine, = call(sum_kernel, [shape((tall, 1024), BF)], terms)
    step = 1
    while step < count_gx:
        mine, = call(sum_kernel, [shape((tall, 1024), BF)], (mine, exchange(mine, "gx", step)))
        step *= 2
    if count_gy == 4:
        terms = [mine, trade_shared(mine, 1, 2), trade_shared(mine, 0, 3)]
        mine, = call(share_kernel, [shape((tall, 1024), F32)], terms)
        terms = [mine, exchange(mine, "gx", 1)]
    else:
        terms = [mine] + [exchange(mine, "gy", step) for step in range(1, count_gy)]
    grad_one, grad_two = call(
        lambda *refs: last_kernel(scale_one, scale_two, *refs),
        [shape((27, 3, tall // 2), F32), shape((27, tall, 32), F32)],
        terms,
    )
    grad_one = grad_one.reshape(3, 3, 3, 3, tall // 2)
    grad_two = jnp.transpose(grad_two.reshape(3, 3, 3, tall, 32), (0, 1, 2, 4, 3))
    return (
        features.reshape(1, 2, 8, 2048),
        level.reshape(1, 4, 16, 2048),
        grad_one,
        grad_two,
    )


def solution(mesh):
    in_specs = (P("dp", None, None, "gx", "gy"), P(), P(), P("dp", None, "gx", "gy"))
    out_specs = (
        P("dp", None, "gx", "gy"),
        P("dp", None, "gx", "gy"),
        P(None, None, None, None, "dp"),
        P(None, None, None, None, "dp"),
    )
    return jax.shard_map(body, mesh=mesh, in_specs=in_specs, out_specs=out_specs, check_vma=False)
```

```python
import math

import jax
import jax.numpy as jnp
from jax import lax
from jax.experimental import pallas as pl
from jax.experimental.pallas import tpu as pltpu
from jax.sharding import PartitionSpec as P

BF = jnp.bfloat16
F32 = jnp.float32
VMEM_LIMIT = 32 * 1024 * 1024


def iota(shape, dim):
    return lax.broadcasted_iota(jnp.int32, shape, dim)


def dot(lhs, rhs, contract=((1,), (0,))):
    return lax.dot_general(lhs, rhs, (contract, ((), ())), preferred_element_type=F32)


def swaps(axis):
    count, ranks = lax.axis_size(axis), lax.axis_size("dp")
    found = []
    for first in range(min(2, count - 1)):
        pairs = []
        for d in range(ranks):
            for i in range(count):
                other = i + 1 if i % 2 == first else i - 1
                if 0 <= other < count:
                    pairs.append((d * count + i, d * count + other))
                else:
                    pairs.append((d * count + i, (d ^ 1) % ranks * count + i))
        found.append(pairs)
    return found


def position(axis):
    index = lax.axis_index(axis)
    return lax.rem(index, 2) == 1, index == 0, index == lax.axis_size(axis) - 1


def from_low(place, got):
    odd, first, _ = place
    second = got[1] if len(got) > 1 else got[0]
    return jnp.where(first, 0.0, jnp.where(odd, got[0], second))


def from_high(place, got):
    odd, _, last = place
    second = got[1] if len(got) > 1 else got[0]
    return jnp.where(last, 0.0, jnp.where(odd, second, got[0]))


def edge_x_kernel(count, *refs):
    hbm, refs = refs[:4], refs[4:]
    held, outs, (stage, sems) = refs[:4], refs[4 : 4 + count], refs[4 + count :]
    fetches = [pltpu.make_async_copy(hbm[i], held[i], sems.at[i]) for i in range(4)]
    for fetch in fetches:
        fetch.start()
    mag_ref, cot_ref = held[:2]
    odd = position("gx")[0]
    planes = mag_ref.shape[0]
    blocks = cot_ref.shape[2] // 128
    for fetch in fetches:
        fetch.wait()
    field = mag_ref[...].astype(F32)
    low = field[:, 0:4, :]
    high = field[:, field.shape[1] - 4 :, :]
    cot = [cot_ref[k].astype(F32)[0:1, :] for k in range(2)]
    for turn in range(count):
        toward_high = odd if turn == 1 else jnp.logical_not(odd)
        picked = jnp.where(toward_high, high, low)
        for g in range(planes):
            stage[4 * g : 4 * g + 4, :] = picked[g]
        for k in range(2):
            for m in range(blocks):
                row = 4 * planes + 16 * k + m
                stage[row : row + 1, :] = cot[k][:, 128 * m : 128 * m + 128]
        outs[turn][...] = stage[...].astype(BF)


def edge_y_kernel(count_x, count_y, mag_ref, cot_ref, *refs):
    got_refs, refs = refs[:count_x], refs[count_x:]
    split_ref, outs = refs[0], refs[1 : 1 + count_y]
    tall, = refs[1 + count_y :]
    place_x, place_y = position("gx"), position("gy")
    planes = mag_ref.shape[0]
    got = [ref[...].astype(F32) for ref in got_refs]
    low = from_low(place_x, got)
    high = from_high(place_x, got)
    zeros = jnp.zeros((24, 128), F32)
    for g in range(planes):
        edge = low[4 * g : 4 * g + 4, :]
        tall[g, 0:8, :] = jnp.broadcast_to(edge[3:4, :], (8, 128))
        tall[g, 8:40, :] = mag_ref[g].astype(F32)
        tall[g, 40:44, :] = high[4 * g : 4 * g + 4, :]
        tall[g, 44:68, :] = zeros
        tall[g, 68:72, :] = edge
    starts = (8, 9, 10, 11, 7)
    split = []
    for slot in range(5):
        parts = [tall[g, pl.ds(starts[slot], 16, stride=4), :].astype(BF) for g in range(planes)]
        whole = jnp.concatenate(parts, axis=0)
        split_ref[slot] = whole
        split.append(whole)
    rows = planes // 3 * 16
    lhs = jnp.concatenate(
        [split[s][rows * c : rows * c + rows] for s in range(4) for c in range(3)], axis=1
    )
    lane = iota((128, 128), 1)
    cell = iota((128, 128), 0)
    slot = lane & 3
    wanted = jnp.where(lane < 64, 124 + slot, slot)
    group = (lane & 63) >> 2
    picks = []
    for s in range(4):
        for c in range(3):
            hit = (group == 4 * s + c) & (cell == wanted)
            picks.append(jnp.where(hit, 1.0, 0.0).astype(BF))
    both = dot(lhs, jnp.concatenate(picks, axis=0)).reshape(4, 2, 16, 128)
    lower, upper = both[:, 0].reshape(64, 128), both[:, 1].reshape(64, 128)
    left = iota((64, 128), 1) < 64
    toward = [
        jnp.where(left, lower, pltpu.roll(upper, 64, 1)),
        jnp.where(left, pltpu.roll(lower, 64, 1), upper),
    ]
    cot_rows = []
    for k in range(2):
        own = cot_ref[k].astype(F32)[:, 0:128]
        row = 4 * planes + 16 * k
        cot_rows.append(jnp.concatenate([own, high[row : row + 1, :], jnp.zeros((7, 128), F32)], axis=0))
    cot_rows = jnp.where(iota((16, 128), 1) < 64, cot_rows[0], pltpu.roll(cot_rows[1], 64, 1))
    odd = place_y[0]
    for turn in range(count_y):
        toward_high = odd if turn == 1 else jnp.logical_not(odd)
        outs[turn][0:64, :] = jnp.where(toward_high, toward[0], toward[1]).astype(BF)
        outs[turn][64:80, :] = cot_rows.astype(BF)


def weights_kernel(one_ref, two_ref, w_one, w_two, halo_ref, rows_one):
    lane = iota((32, 256), 1)
    spread = jnp.where(iota((32, 256), 0) == (lane & 31), 1.0, 0.0).astype(BF)
    rows_one[80:88, :] = jnp.zeros((8, 32), F32)
    for i in range(27):
        rows_one[3 * i : 3 * i + 3, :] = one_ref[i].astype(F32)
    wide = dot(rows_one[...].astype(BF), spread)
    window = iota((32, 256), 0) - 2 * (lane >> 5)
    for tap in range(9):
        for c in range(3):
            block = jnp.zeros((32, 256), F32)
            for e in range(3):
                row = (3 * tap + e) * 3 + c
                block = jnp.where(window == e, wide[row : row + 1, :], block)
            w_one[128 * tap + 32 * c : 128 * tap + 32 * c + 32, :] = block.astype(BF)
        w_one[128 * tap + 96 : 128 * tap + 128, :] = jnp.zeros((32, 256), BF)

    lane = iota((64, 128), 1)
    spread = jnp.where(iota((64, 128), 0) == (lane & 63), 1.0, 0.0).astype(BF)
    twice = dot(two_ref[...], spread)
    left = iota((32, 128), 1) < 64
    for tap in range(9):
        k0, k1, k2 = (twice[32 * (3 * tap + e) : 32 * (3 * tap + e) + 32] for e in range(3))
        base = 128 * tap
        w_two[base : base + 32, 0:128] = jnp.where(left, k1, 0.0).astype(BF)
        w_two[base + 32 : base + 64, 0:128] = jnp.where(left, k2, k0).astype(BF)
        w_two[base + 64 : base + 96, 0:128] = jnp.where(left, 0.0, k1).astype(BF)
        w_two[base + 96 : base + 128, 0:128] = jnp.where(left, 0.0, k2).astype(BF)
        w_two[base : base + 96, 128:256] = jnp.zeros((96, 128), BF)
        w_two[base + 96 : base + 128, 128:256] = jnp.where(left, k0, 0.0).astype(BF)

    lane = iota((256, 256), 1)
    code = iota((256, 256), 0)
    offset = lane & 31
    part = (lane & 127) >> 5
    wanted = jnp.where(
        lane < 128,
        jnp.where(offset == 0, 3, -999),
        jnp.where(
            (offset >= 1) & (offset <= 4), 127 + offset, jnp.where((offset >= 14) & (offset <= 16), offset - 13, -999)
        ),
    )
    wanted = jnp.where(part < 3, wanted + 4 * part, -999)
    for s in range(4):
        for parity in range(2):
            hit = code - (64 * parity + 16 * s) == wanted
            base = 256 * (2 * s + parity)
            halo_ref[:, base : base + 256] = jnp.where(hit, 1.0, 0.0).astype(BF)


SLOTS = ((4, 0, 1), (1, 2, 3))


def first_level(pre, t):
    sig = jax.nn.sigmoid(pre)
    hidden = pre * sig
    slope = sig * (1.0 + pre * (1.0 - sig))
    if t == 0:
        return [(1, hidden)], slope
    rows, width = hidden.shape
    later = hidden.reshape(rows // 16, 16, width)
    later = jnp.concatenate([later[:, 15:16], later[:, 0:15]], axis=1).reshape(rows, width)
    return [(2, hidden), (0, later)], slope


def second_level(pre, cot):
    sig = jax.nn.sigmoid(pre)
    return pre * sig, cot * (sig * (1.0 + pre * (1.0 - sig)))


def short_pair(value, row):
    return jnp.concatenate([value[row : row + 8, 0:128], value[row : row + 8, 128:256]], axis=0)


def windows_kernel(count_x, split_ref, w_one, w_two, cot_ref, *refs):
    gx_refs, refs = refs[:count_x], refs[count_x:]
    short_ref, outer_ref, short_act, slope_ref, cot_all = refs[:5]
    ends_ref, feat_ref, here_ref, after_ref, grad_ref, inner_ref, act_ref = refs[5:]
    high_x = from_high(position("gx"), [ref[96:128, :].astype(F32) for ref in gx_refs])
    for k in range(2):
        cot = cot_ref[k].astype(F32)
        for m in range(16):
            row = 16 * k + m
            cot_all[k, 16 * m : 16 * m + 8, :] = cot[:, 128 * m : 128 * m + 128]
            cot_all[k, 16 * m + 8 : 16 * m + 16, :] = jnp.where(
                iota((8, 128), 0) == 0, high_x[row : row + 1, :], 0.0
            )

    lane = iota((128, 1152), 1)
    cell = iota((128, 1152), 0)
    block = lane >> 7
    offset = lane & 31
    part = (lane & 127) >> 5
    wanted = jnp.where(offset <= 16, 16 * block - 1 + offset, -9)
    wanted = jnp.where(block == 8, jnp.where(offset == 0, 127, -9), wanted)
    hit = cell == wanted
    picks = jnp.concatenate(
        [jnp.where(hit & (part == c), 1.0, 0.0).astype(BF) for c in range(3)], axis=0
    )
    for s in range(5):
        lhs = jnp.concatenate([split_ref[s, 128 * c : 128 * c + 128, :] for c in range(3)], axis=1)
        exact = dot(lhs, picks)
        found = exact.astype(BF)
        for z in range(8):
            for q in range(4):
                first = exact[16 * z : 16 * z + 8, 256 * q + 128 : 256 * q + 256]
                if q < 3:
                    second = exact[16 * z : 16 * z + 8, 256 * q + 256 : 256 * q + 384]
                else:
                    second = jnp.zeros((8, 128), F32)
                short_ref[s, z, 16 * q : 16 * q + 16, :] = jnp.concatenate([first, second], axis=0).astype(BF)
        for n in range(1, 8):
            for z in range(8):
                inner_ref[s, z, 16 * n - 16 : 16 * n, :] = found[16 * z : 16 * z + 16, 128 * n : 128 * n + 128]
        outer_ref[s, :, 0:128] = found[:, 0:128]
        outer_ref[s, :, 128:256] = found[:, 1024:1152]
    weights = w_one[...]
    for p in range(4):
        for t in range(2):
            pieces = []
            for a in range(3):
                for b in range(3):
                    z = 2 * p + a - 1
                    pieces.append(inner_ref[SLOTS[t][b], z] if z >= 0 else jnp.zeros((112, 128), BF))
            versions, slope = first_level(dot(jnp.concatenate(pieces, axis=1), weights), t)
            for b, value in versions:
                for n in range(7):
                    short_act[b, p, 16 * n : 16 * n + 16, :] = short_pair(value, 16 * n).astype(BF)
                value = value.astype(BF)
                for n in range(7):
                    act_ref[b, p, 32 * n : 32 * n + 16, :] = value[16 * n : 16 * n + 16, 0:128]
                    act_ref[b, p, 32 * n + 16 : 32 * n + 32, :] = value[16 * n : 16 * n + 16, 128:256]
            for n in range(7):
                slope_ref[p, t, 16 * n : 16 * n + 16, :] = short_pair(slope, 16 * n)
    weights = w_two[...]
    delta, patches = [], []
    for k in range(2):
        planes = [(b, 2 * k + a - 1) for a in range(3) for b in range(3)]
        lhs = [act_ref[b, p] if p >= 0 else jnp.zeros((224, 128), BF) for b, p in planes]
        out = dot(jnp.concatenate(lhs, axis=1), weights)
        ends_ref[k, 0] = out[0:16, 0:128]
        ends_ref[k, 1] = out[208:224, 128:256]
        feat, value = second_level(out[16:224, 0:128] + out[0:208, 128:256], cot_all[k, 48:256, :])
        feat_ref[k] = jnp.concatenate([feat[16 * m : 16 * m + 8] for m in range(13)], axis=1).astype(BF)
        value = value.reshape(13, 16, 128)
        here = value[:, 0:8].reshape(104, 128)
        here_ref[k] = here
        after_ref[k] = value[:, 1:9].reshape(104, 128)
        zero = jnp.zeros((8, 128), F32)
        both = [jnp.concatenate([zero, here], axis=0), jnp.concatenate([here, zero], axis=0)]
        delta.append(jnp.concatenate(both, axis=1).astype(BF))
        short = [short_act[b, p] if p >= 0 else jnp.zeros((112, 128), BF) for b, p in planes]
        patches.append(jnp.concatenate(short, axis=1))
    delta, patches = jnp.concatenate(delta, axis=0), jnp.concatenate(patches, axis=0)
    for first in range(0, 1152, 256):
        last = min(first + 256, 1152)
        grad_ref[:, first:last] = dot(delta, patches[:, first:last], ((0,), (0,)))[0:192]


def main_kernel(
    count_y,
    ranks,
    short_ref,
    outer_ref,
    short_act,
    slope_ref,
    cot_ref,
    ends_ref,
    feat_in,
    here_in,
    after_in,
    grad_in,
    halo_ref,
    w_one,
    w_two,
    *refs,
):
    gy_refs, refs = refs[:count_y], refs[count_y:]
    feat_hbm, level_hbm, refs = refs[0], refs[1], refs[2:]
    parts = 2 if ranks == 4 else ranks
    dealt, refs = refs[:parts], refs[parts:]
    edges, short_edges, outer_act, outer_short, outer_slope, rows_out, total, feat_ref, level_ref, sems = refs
    place_y = position("gy")
    copies = []

    got_y = [ref[...].astype(F32) for ref in gy_refs]
    low_y = from_low(place_y, got_y)
    high_y = from_high(place_y, got_y)
    halo = jnp.concatenate([low_y[0:64], high_y[0:64]], axis=1).astype(BF)
    first_half = iota((16, 128), 1) < 64
    cot_y = [jnp.where(first_half, value, 0.0) for value in (high_y[64:80], pltpu.roll(high_y[64:80], 64, 1))]
    brought = dot(halo, halo_ref[...])
    for s in range(5):
        base = 512 * min(s, 3)
        found = [brought[:, base + 256 * parity : base + 256 * parity + 256].reshape(4, 16, 256) for parity in range(2)]
        edge = jnp.stack(found, axis=1).reshape(8, 16, 256)
        if s == 4:
            edge = jnp.concatenate([edge[:, 15:16], edge[:, 0:15]], axis=1)
        exact = outer_ref[s].astype(F32) + edge.reshape(128, 256)
        value = exact.astype(BF)
        for z in range(8):
            edges[s, z, 0:16, :] = value[16 * z : 16 * z + 16, 0:128]
            edges[s, z, 16:32, :] = value[16 * z : 16 * z + 16, 128:256]
            other = short_ref[s, z, 48:64, :].astype(F32)
            short_edges[s, z] = jnp.concatenate([other[0:8], exact[16 * z : 16 * z + 8, 0:128]], axis=0).astype(BF)

    def window(s, z):
        if z < 0:
            return jnp.zeros((64, 128), BF)
        return jnp.concatenate([short_ref[s, z, 0:48, :], short_edges[s, z]], axis=0)

    weights = w_one[...]
    for t in range(2):
        rows = []
        for p in range(4):
            pieces = []
            for a in range(3):
                for b in range(3):
                    z = 2 * p + a - 1
                    pieces.append(edges[SLOTS[t][b], z] if z >= 0 else jnp.zeros((32, 128), BF))
            rows.append(jnp.concatenate(pieces, axis=1))
        versions, slope = first_level(dot(jnp.concatenate(rows, axis=0), weights), t)
        for p in range(4):
            first, second = 32 * p, 32 * p + 16
            for b, value in versions:
                before = jnp.concatenate([value[second : second + 8, 128:256], jnp.zeros((8, 128), F32)], axis=0)
                outer_short[b, p, 0:16, :] = before.astype(BF)
                outer_short[b, p, 16:32, :] = short_pair(value, first).astype(BF)
                outer_act[b, p, 0:16, :] = value[second : second + 16, 128:256].astype(BF)
                outer_act[b, p, 16:32, :] = value[first : first + 16, 0:128].astype(BF)
                outer_act[b, p, 32:48, :] = value[first : first + 16, 128:256].astype(BF)
                outer_act[b, p, 48:64, :] = value[second : second + 16, 0:128].astype(BF)
            outer_slope[p, t] = short_pair(slope, first)

    lhs = []
    for k in range(2):
        planes = [(b, 2 * k + a - 1) for a in range(3) for b in range(3)]
        lhs.append(
            jnp.concatenate([outer_act[b, p] if p >= 0 else jnp.zeros((64, 128), BF) for b, p in planes], axis=1)
        )
    out = dot(jnp.concatenate(lhs, axis=0), w_two[...])
    pairs, pairs_next, delta, patches = [], [], [], []
    for k in range(2):
        own = out[64 * k : 64 * k + 64]
        pre = jnp.concatenate(
            [own[16:48, 0:128], ends_ref[k, 0], own[48:64, 0:128]], axis=0
        ) + jnp.concatenate([own[0:48, 128:256], ends_ref[k, 1]], axis=0)
        feat, value = second_level(pre, jnp.concatenate([cot_ref[k, 0:48, :], cot_y[k]], axis=0))
        feat_ref[k, :, 0:384] = jnp.concatenate([feat[16 * m : 16 * m + 8] for m in range(3)], axis=1).astype(BF)
        feat_ref[k, :, 384:2048] = feat_in[k]
        copies.append(pltpu.make_async_copy(feat_ref.at[k], feat_hbm.at[k], sems.at[k]))
        copies[-1].start()
        value = value.reshape(4, 16, 128)
        outer = value[:, 0:8].reshape(32, 128)
        here = jnp.concatenate([outer[0:24], here_in[k], outer[24:32]], axis=0)
        outer_after = value[:, 1:9].reshape(32, 128)
        after = jnp.concatenate([outer_after[0:24], after_in[k], outer_after[24:32]], axis=0)
        pairs.append(jnp.concatenate([here[0:128], here[8:136]], axis=1).astype(BF))
        pairs_next.append(jnp.concatenate([after[0:128], after[8:136]], axis=1).astype(BF))
        zero = jnp.zeros((8, 128), F32)
        both = [
            jnp.concatenate([zero, zero, outer[0:24], zero], axis=0),
            jnp.concatenate([outer[0:8], zero, outer[8:24], zero, zero], axis=0),
        ]
        delta.append(jnp.concatenate(both, axis=1).astype(BF))
        short = []
        for a in range(3):
            for b in range(3):
                p = 2 * k + a - 1
                if p < 0:
                    short.append(jnp.zeros((48, 128), BF))
                else:
                    short.append(jnp.concatenate([outer_short[b, p], short_act[b, p, 0:16, :]], axis=0))
        patches.append(jnp.concatenate(short, axis=1))
    delta, patches = jnp.concatenate(delta, axis=0), jnp.concatenate(patches, axis=0)

    place = iota((64, 128), 1) >> 5
    turned = []
    for ab in range(9):
        if ab % 2 == 0:
            first, last = 128 * ab, min(128 * ab + 256, 1152)
            grad = dot(delta, patches[:, first:last], ((0,), (0,)))[0:192] + grad_in[:, first:last]
        column = 128 * (ab % 2)
        a0, a1, a2 = (grad[64 * j : 64 * j + 64, column : column + 128] for j in range(3))
        r0, r1, r2 = (pltpu.roll(a, 64, 1) for a in (a0, a1, a2))
        joined = jnp.where(place == 0, a0 + r1, jnp.where(place == 1, a1 + r2, a1 + r0))
        shift = (3 * ab - 1) % 4
        other = (shift + 2) % 4
        outer = pltpu.roll(joined, 32 * shift, 1) if shift else joined
        inner = pltpu.roll(joined, 32 * other, 1) if other else joined
        turned += [outer, inner, outer]
    turned.append(jnp.zeros((64, 128), F32))
    for v in range(7):
        t0, t1, t2, t3 = turned[4 * v : 4 * v + 4]
        total[:, 128 * v : 128 * v + 128] = jnp.where(
            place < 2, jnp.where(place == 0, t0, t1), jnp.where(place == 2, t2, t3)
        )

    lhs_rows, rhs_rows = [], []
    for p in range(4):
        depth = [(1, p // 2)] if p % 2 == 0 else [(2, (p - 1) // 2), (0, (p + 1) // 2)]
        for t in range(2):
            width = [(1, pairs)] if t == 0 else [(2, pairs), (0, pairs_next)]
            taps = [(3 * a + b, source[k]) for a, k in depth if k < 2 for b, source in width]
            level = dot(
                jnp.concatenate([source for _, source in taps], axis=1),
                jnp.concatenate([w_two[128 * tap : 128 * tap + 128, :] for tap, _ in taps], axis=1),
                ((1,), (1,)),
            )
            level = level.astype(BF).astype(F32)
            for m in range(16):
                rows_out[m, pl.ds(t, 8, stride=2), :] = level[8 * m : 8 * m + 8]
            slope = jnp.concatenate([outer_slope[p, t], slope_ref[p, t]], axis=0)
            value = level * slope
            blocks = [
                jnp.concatenate([value[16 * n : 16 * n + 8], value[16 * n + 8 : 16 * n + 16]], axis=1)
                for n in (1, 2, 3, 4, 5, 6, 7, 0)
            ]
            lhs_rows.append(jnp.concatenate(blocks, axis=0).astype(BF))
            rhs_rows.append(
                jnp.concatenate([window(SLOTS[t][b], 2 * p + a - 1) for a in range(3) for b in range(3)], axis=1)
            )
        level_ref[p] = jnp.concatenate([rows_out[m] for m in range(16)], axis=1).astype(BF)
        copies.append(pltpu.make_async_copy(level_ref.at[p], level_hbm.at[p], sems.at[2 + p]))
        copies[-1].start()
    delta_one = jnp.concatenate(lhs_rows, axis=0).T
    windows = jnp.concatenate(rhs_rows, axis=0)

    place = iota((32, 128), 1)
    found = jnp.zeros((32, 128), F32)
    for tap in range(9):
        if tap % 2 == 0:
            grad = dot(delta_one, windows[:, 128 * tap : min(128 * tap + 256, 1152)])
        column = 128 * (tap % 2)
        some = jnp.zeros((32, 128), F32)
        for t in range(8):
            piece = grad[32 * t : 32 * t + 32, column : column + 128]
            shift = (3 * tap - 2 * t) % 128
            some = some + (pltpu.roll(piece, shift, 1) if shift else piece)
        local = place & 31
        found = jnp.where((local >= 3 * tap) & (local < 3 * tap + 3), some, found)
    total[:, 896:1024] = jnp.zeros((64, 128), F32)
    tall, short = 64 // ranks, 32 // ranks
    for d in range(ranks):
        total[tall * d : tall * d + short, 896:1024] = found[short * d : short * d + short]
    rank = lax.axis_index("dp")
    picked = []
    for step in range(ranks):
        if tall % 8 == 0:
            start = pl.multiple_of((rank ^ step) * tall, tall)
            picked.append(total[pl.ds(start, tall), :])
        else:
            value = total[0:tall, :]
            for d in range(1, ranks):
                value = jnp.where((rank ^ step) == d, total[d * tall : d * tall + tall, :], value)
            picked.append(value)
    if ranks == 4:
        odd = position("gx")[0]
        near, far = jnp.concatenate(picked[:2], axis=0), jnp.concatenate(picked[2:], axis=0)
        dealt[0][...] = jnp.where(odd, far, near).astype(BF)
        dealt[1][...] = jnp.where(odd, near, far).astype(BF)
    else:
        for out, value in zip(dealt, picked):
            out[...] = value.astype(BF)
    for copy in copies:
        copy.wait()


def sum_kernel(*refs):
    parts, out_ref = refs[:-1], refs[-1]
    values = [ref[...].astype(F32) for ref in parts]
    while len(values) > 1:
        values = [values[i] + values[i + 1] for i in range(0, len(values), 2)]
    out_ref[...] = values[0].astype(out_ref.dtype)


def part_kernel(mine_ref, got_ref, own_ref, first_ref, second_ref):
    value = mine_ref[...].astype(F32) + got_ref[...].astype(F32)
    tall = value.shape[0] // 2
    upper, lower = value[:tall].astype(BF), value[tall:].astype(BF)
    own_ref[...] = upper
    first_ref[...] = jnp.where(position("gx")[0], upper, lower)
    second_ref[...] = lower


def share_kernel(mine_ref, first_ref, second_ref, out_ref):
    first = first_ref[...].astype(F32)
    odd = position("gx")[0]
    value = first + jnp.where(odd, second_ref[...].astype(F32), mine_ref[...].astype(F32))
    out_ref[...] = value.astype(out_ref.dtype)


def last_kernel(scale_one, scale_two, *refs):
    parts, (one_ref, two_ref) = refs[:-2], refs[-2:]
    values = [ref[...].astype(F32) for ref in parts]
    while len(values) > 1:
        values = [values[i] + values[i + 1] for i in range(0, len(values), 2)]
    value = values[0]
    tall = value.shape[0]
    short = tall // 2
    scaled = value[:, 0:896] * scale_two
    for tap in range(27):
        two_ref[tap] = scaled[:, 32 * tap : 32 * tap + 32]
    rows = value[0:short, 896:1024] * scale_one
    if short < 8:
        rows = jnp.concatenate([rows, jnp.zeros((8 - short, 128), F32)], axis=0)
    turned = rows.T
    for c in range(3):
        one_ref[:, c, :] = turned[32 * c : 32 * c + 27, 0:short]


def call(kernel, outs, args, scratch=(), space=pltpu.VMEM, in_hbm=0, flops=0):
    spaces = [pltpu.HBM] * in_hbm + [pltpu.VMEM] * (len(outs) - in_hbm)
    return pl.pallas_call(
        kernel,
        out_shape=outs,
        in_specs=[pl.BlockSpec(memory_space=space)] * len(args),
        out_specs=[pl.BlockSpec(memory_space=kind) for kind in spaces],
        scratch_shapes=list(scratch),
        compiler_params=pltpu.CompilerParams(vmem_limit_bytes=VMEM_LIMIT),
        cost_estimate=pl.CostEstimate(flops=flops, bytes_accessed=1 << 20, transcendentals=0),
    )(*args)


def shape(dims, dtype):
    return jax.ShapeDtypeStruct(dims, dtype)


def exchange(value, axis, step):
    return lax.ppermute(value, axis, [(i, i ^ step) for i in range(lax.axis_size(axis))])


def trade_shared(value, even_step, odd_step):
    count, columns, ranks = lax.axis_size("gy"), lax.axis_size("gx"), lax.axis_size("dp")
    pairs = []
    for d in range(ranks):
        for g in range(columns):
            for i in range(count):
                to_d, to_i = d, i ^ (odd_step if g % 2 else even_step)
                if g % 2 == 0 and even_step == 0:
                    to_d = (d ^ 1) % ranks
                pairs.append(((d * columns + g) * count + i, (to_d * columns + g) * count + to_i))
    return lax.ppermute(value, ("dp", "gx", "gy"), pairs)


def trade_ranks(value, even_step, odd_step):
    ranks, columns = lax.axis_size("dp"), lax.axis_size("gx")
    pairs = [
        (d * columns + g, (d ^ (odd_step if g % 2 else even_step)) * columns + g)
        for d in range(ranks)
        for g in range(columns)
    ]
    return lax.ppermute(value, ("dp", "gx"), pairs)


def body(magnetic, kernel_one, kernel_two, cotangent):
    ranks, count_gx, count_gy = (lax.axis_size(axis) for axis in ("dp", "gx", "gy"))
    depth = magnetic.shape[2]
    samples_all = magnetic.shape[0] * ranks
    cells_x = magnetic.shape[3] * count_gx
    cells_y = magnetic.shape[4] * count_gy
    scale_one = 1.0 / math.sqrt(samples_all * (depth // 2) * (cells_x // 2) * (cells_y // 2))
    scale_two = 1.0 / math.sqrt(samples_all * (depth // 4) * (cells_x // 4) * (cells_y // 4))
    field = magnetic.reshape(24, 32, 128)
    cot = cotangent.reshape(2, 8, 2048)
    one = kernel_one.reshape(27, 3, 32)
    two = kernel_two.reshape(864, 64)

    swaps_x, swaps_y = swaps("gx"), swaps("gy")
    nx, ny = len(swaps_x), len(swaps_y)
    operands = [pltpu.with_memory_space_constraint(array, pltpu.HBM) for array in (field, cot, one, two)]
    field, cot, one, two, *edges = call(
        lambda *refs: edge_x_kernel(nx, *refs),
        [shape(array.shape, BF) for array in operands] + [shape((128, 128), BF)] * nx,
        operands,
        [pltpu.VMEM((128, 128), F32), pltpu.SemaphoreType.DMA((4,))],
        space=pltpu.HBM,
    )
    got_x = [lax.ppermute(edge, ("dp", "gx"), pairs) for edge, pairs in zip(edges, swaps_x)]
    w_one, w_two, picks = call(
        weights_kernel,
        [shape((1152, 256), BF), shape((1152, 256), BF), shape((256, 2048), BF)],
        (one, two),
        [pltpu.VMEM((88, 32), F32)],
        flops=1 << 30,
    )
    split, *edges = call(
        lambda *refs: edge_y_kernel(nx, ny, *refs),
        [shape((5, 384, 128), BF)] + [shape((80, 128), BF)] * ny,
        (field, cot, *got_x),
        [pltpu.VMEM((24, 72, 128), F32)],
    )
    got_y = [lax.ppermute(edge, ("dp", "gy"), pairs) for edge, pairs in zip(edges, swaps_y)]
    first = call(
        lambda *refs: windows_kernel(nx, *refs),
        [
            shape((5, 8, 64, 128), BF),
            shape((5, 128, 256), BF),
            shape((3, 4, 112, 128), BF),
            shape((4, 2, 112, 128), F32),
            shape((2, 256, 128), F32),
            shape((2, 2, 16, 128), F32),
            shape((2, 8, 1664), BF),
            shape((2, 104, 128), F32),
            shape((2, 104, 128), F32),
            shape((192, 1152), F32),
        ],
        (split, w_one, w_two, cot, *got_x),
        [pltpu.VMEM((5, 8, 112, 128), BF), pltpu.VMEM((3, 4, 224, 128), BF)],
        flops=1 << 31,
    )
    tall = 64 // ranks
    features, level, *dealt = call(
        lambda *refs: main_kernel(ny, ranks, *refs),
        [shape((2, 8, 2048), BF), shape((4, 16, 2048), BF)]
        + ([shape((32, 1024), BF)] * 2 if ranks == 4 else [shape((tall, 1024), BF)] * ranks),
        (*first, picks, w_one, w_two, *got_y),
        [
            pltpu.VMEM((5, 8, 32, 128), BF),
            pltpu.VMEM((5, 8, 16, 128), BF),
            pltpu.VMEM((3, 4, 64, 128), BF),
            pltpu.VMEM((3, 4, 32, 128), BF),
            pltpu.VMEM((4, 2, 16, 128), F32),
            pltpu.VMEM((16, 16, 128), F32),
            pltpu.VMEM((64, 1024), F32),
            pltpu.VMEM((2, 8, 2048), BF),
            pltpu.VMEM((4, 16, 2048), BF),
            pltpu.SemaphoreType.DMA((6,)),
        ],
        in_hbm=2,
    )
    if ranks == 4:
        own, one_more, two_more = call(
            part_kernel, [shape((tall, 1024), BF)] * 3, (dealt[0], exchange(dealt[1], "gx", 1))
        )
        terms = [own, trade_ranks(one_more, 1, 2), trade_ranks(two_more, 2, 3)]
        mine, = call(share_kernel, [shape((tall, 1024), BF)], terms)
    else:
        terms = [exchange(dealt[step], "dp", step) for step in range(1, ranks)] + dealt[:1]
        mine, = call(sum_kernel, [shape((tall, 1024), BF)], terms)
    step = 1
    while step < count_gx:
        mine, = call(sum_kernel, [shape((tall, 1024), BF)], (mine, exchange(mine, "gx", step)))
        step *= 2
    if count_gy == 4:
        terms = [mine, trade_shared(mine, 1, 2), trade_shared(mine, 0, 3)]
        mine, = call(share_kernel, [shape((tall, 1024), F32)], terms)
        terms = [mine, exchange(mine, "gx", 1)]
    else:
        terms = [mine] + [exchange(mine, "gy", step) for step in range(1, count_gy)]
    grad_one, grad_two = call(
        lambda *refs: last_kernel(scale_one, scale_two, *refs),
        [shape((27, 3, tall // 2), F32), shape((27, tall, 32), F32)],
        terms,
    )
    grad_one = grad_one.reshape(3, 3, 3, 3, tall // 2)
    grad_two = jnp.transpose(grad_two.reshape(3, 3, 3, tall, 32), (0, 1, 2, 4, 3))
    return (
        features.reshape(1, 2, 8, 2048),
        level.reshape(1, 4, 16, 2048),
        grad_one,
        grad_two,
    )


def solution(mesh):
    in_specs = (P("dp", None, None, "gx", "gy"), P(), P(), P("dp", None, "gx", "gy"))
    out_specs = (
        P("dp", None, "gx", "gy"),
        P("dp", None, "gx", "gy"),
        P(None, None, None, None, "dp"),
        P(None, None, None, None, "dp"),
    )
    return jax.shard_map(body, mesh=mesh, in_specs=in_specs, out_specs=out_specs, check_vma=False)
```

```python
import math

import jax
import jax.numpy as jnp
from jax import lax
from jax.experimental import pallas as pl
from jax.experimental.pallas import tpu as pltpu
from jax.sharding import PartitionSpec as P

BF = jnp.bfloat16
F32 = jnp.float32
VMEM_LIMIT = 32 * 1024 * 1024


def iota(shape, dim):
    return lax.broadcasted_iota(jnp.int32, shape, dim)


def dot(lhs, rhs, contract=((1,), (0,))):
    return lax.dot_general(lhs, rhs, (contract, ((), ())), preferred_element_type=F32)


def swaps(axis):
    count, ranks = lax.axis_size(axis), lax.axis_size("dp")
    found = []
    for first in range(min(2, count - 1)):
        pairs = []
        for d in range(ranks):
            for i in range(count):
                other = i + 1 if i % 2 == first else i - 1
                if 0 <= other < count:
                    pairs.append((d * count + i, d * count + other))
                else:
                    pairs.append((d * count + i, (d ^ 1) % ranks * count + i))
        found.append(pairs)
    return found


def position(axis):
    index = lax.axis_index(axis)
    return lax.rem(index, 2) == 1, index == 0, index == lax.axis_size(axis) - 1


def from_low(place, got):
    odd, first, _ = place
    second = got[1] if len(got) > 1 else got[0]
    return jnp.where(first, 0.0, jnp.where(odd, got[0], second))


def from_high(place, got):
    odd, _, last = place
    second = got[1] if len(got) > 1 else got[0]
    return jnp.where(last, 0.0, jnp.where(odd, second, got[0]))


def edge_x_kernel(count, *refs):
    hbm, refs = refs[:4], refs[4:]
    held, outs, (stage, sems) = refs[:4], refs[4 : 4 + count], refs[4 + count :]
    fetches = [pltpu.make_async_copy(hbm[i], held[i], sems.at[i]) for i in range(4)]
    for fetch in fetches:
        fetch.start()
    mag_ref, cot_ref = held[:2]
    odd = position("gx")[0]
    planes = mag_ref.shape[0]
    blocks = cot_ref.shape[2] // 128
    for fetch in fetches[:2]:
        fetch.wait()
    field = mag_ref[...].astype(F32)
    low = field[:, 0:4, :]
    high = field[:, field.shape[1] - 4 :, :]
    cot = [cot_ref[k].astype(F32)[0:1, :] for k in range(2)]
    for turn in range(count):
        toward_high = odd if turn == 1 else jnp.logical_not(odd)
        picked = jnp.where(toward_high, high, low)
        for g in range(planes):
            stage[4 * g : 4 * g + 4, :] = picked[g]
        for k in range(2):
            for m in range(blocks):
                row = 4 * planes + 16 * k + m
                stage[row : row + 1, :] = cot[k][:, 128 * m : 128 * m + 128]
        outs[turn][...] = stage[...].astype(BF)
    for fetch in fetches[2:]:
        fetch.wait()


def edge_y_kernel(count_x, count_y, mag_ref, cot_ref, *refs):
    got_refs, refs = refs[:count_x], refs[count_x:]
    split_ref, outs = refs[0], refs[1 : 1 + count_y]
    tall, = refs[1 + count_y :]
    place_x, place_y = position("gx"), position("gy")
    planes = mag_ref.shape[0]
    got = [ref[...].astype(F32) for ref in got_refs]
    low = from_low(place_x, got)
    high = from_high(place_x, got)
    zeros = jnp.zeros((24, 128), F32)
    for g in range(planes):
        edge = low[4 * g : 4 * g + 4, :]
        tall[g, 0:8, :] = jnp.broadcast_to(edge[3:4, :], (8, 128))
        tall[g, 8:40, :] = mag_ref[g].astype(F32)
        tall[g, 40:44, :] = high[4 * g : 4 * g + 4, :]
        tall[g, 44:68, :] = zeros
        tall[g, 68:72, :] = edge
    starts = (8, 9, 10, 11, 7)
    split = []
    for slot in range(5):
        parts = [tall[g, pl.ds(starts[slot], 16, stride=4), :].astype(BF) for g in range(planes)]
        whole = jnp.concatenate(parts, axis=0)
        split_ref[slot] = whole
        split.append(whole)
    rows = planes // 3 * 16
    lhs = jnp.concatenate(
        [split[s][rows * c : rows * c + rows] for s in range(4) for c in range(3)], axis=1
    )
    lane = iota((128, 128), 1)
    cell = iota((128, 128), 0)
    slot = lane & 3
    wanted = jnp.where(lane < 64, 124 + slot, slot)
    group = (lane & 63) >> 2
    picks = []
    for s in range(4):
        for c in range(3):
            hit = (group == 4 * s + c) & (cell == wanted)
            picks.append(jnp.where(hit, 1.0, 0.0).astype(BF))
    both = dot(lhs, jnp.concatenate(picks, axis=0)).reshape(4, 2, 16, 128)
    lower, upper = both[:, 0].reshape(64, 128), both[:, 1].reshape(64, 128)
    left = iota((64, 128), 1) < 64
    toward = [
        jnp.where(left, lower, pltpu.roll(upper, 64, 1)),
        jnp.where(left, pltpu.roll(lower, 64, 1), upper),
    ]
    cot_rows = []
    for k in range(2):
        own = cot_ref[k].astype(F32)[:, 0:128]
        row = 4 * planes + 16 * k
        cot_rows.append(jnp.concatenate([own, high[row : row + 1, :], jnp.zeros((7, 128), F32)], axis=0))
    cot_rows = jnp.where(iota((16, 128), 1) < 64, cot_rows[0], pltpu.roll(cot_rows[1], 64, 1))
    odd = place_y[0]
    for turn in range(count_y):
        toward_high = odd if turn == 1 else jnp.logical_not(odd)
        outs[turn][0:64, :] = jnp.where(toward_high, toward[0], toward[1]).astype(BF)
        outs[turn][64:80, :] = cot_rows.astype(BF)


def weights_kernel(one_ref, two_ref, w_one, w_two, halo_ref, rows_one):
    lane = iota((32, 256), 1)
    spread = jnp.where(iota((32, 256), 0) == (lane & 31), 1.0, 0.0).astype(BF)
    rows_one[80:88, :] = jnp.zeros((8, 32), F32)
    for i in range(27):
        rows_one[3 * i : 3 * i + 3, :] = one_ref[i].astype(F32)
    wide = dot(rows_one[...].astype(BF), spread)
    window = iota((32, 256), 0) - 2 * (lane >> 5)
    for tap in range(9):
        for c in range(3):
            block = jnp.zeros((32, 256), F32)
            for e in range(3):
                row = (3 * tap + e) * 3 + c
                block = jnp.where(window == e, wide[row : row + 1, :], block)
            w_one[128 * tap + 32 * c : 128 * tap + 32 * c + 32, :] = block.astype(BF)
        w_one[128 * tap + 96 : 128 * tap + 128, :] = jnp.zeros((32, 256), BF)

    lane = iota((64, 128), 1)
    spread = jnp.where(iota((64, 128), 0) == (lane & 63), 1.0, 0.0).astype(BF)
    twice = dot(two_ref[...], spread)
    left = iota((32, 128), 1) < 64
    for tap in range(9):
        k0, k1, k2 = (twice[32 * (3 * tap + e) : 32 * (3 * tap + e) + 32] for e in range(3))
        base = 128 * tap
        w_two[base : base + 32, 0:128] = jnp.where(left, k1, 0.0).astype(BF)
        w_two[base + 32 : base + 64, 0:128] = jnp.where(left, k2, k0).astype(BF)
        w_two[base + 64 : base + 96, 0:128] = jnp.where(left, 0.0, k1).astype(BF)
        w_two[base + 96 : base + 128, 0:128] = jnp.where(left, 0.0, k2).astype(BF)
        w_two[base : base + 96, 128:256] = jnp.zeros((96, 128), BF)
        w_two[base + 96 : base + 128, 128:256] = jnp.where(left, k0, 0.0).astype(BF)

    lane = iota((256, 256), 1)
    code = iota((256, 256), 0)
    offset = lane & 31
    part = (lane & 127) >> 5
    wanted = jnp.where(
        lane < 128,
        jnp.where(offset == 0, 3, -999),
        jnp.where(
            (offset >= 1) & (offset <= 4), 127 + offset, jnp.where((offset >= 14) & (offset <= 16), offset - 13, -999)
        ),
    )
    wanted = jnp.where(part < 3, wanted + 4 * part, -999)
    for s in range(4):
        for parity in range(2):
            hit = code - (64 * parity + 16 * s) == wanted
            base = 256 * (2 * s + parity)
            halo_ref[:, base : base + 256] = jnp.where(hit, 1.0, 0.0).astype(BF)


SLOTS = ((4, 0, 1), (1, 2, 3))


def first_level(pre, t):
    sig = jax.nn.sigmoid(pre)
    hidden = pre * sig
    slope = sig * (1.0 + pre * (1.0 - sig))
    if t == 0:
        return [(1, hidden)], slope
    rows, width = hidden.shape
    later = hidden.reshape(rows // 16, 16, width)
    later = jnp.concatenate([later[:, 15:16], later[:, 0:15]], axis=1).reshape(rows, width)
    return [(2, hidden), (0, later)], slope


def second_level(pre, cot):
    sig = jax.nn.sigmoid(pre)
    return pre * sig, cot * (sig * (1.0 + pre * (1.0 - sig)))


def short_pair(value, row):
    return jnp.concatenate([value[row : row + 8, 0:128], value[row : row + 8, 128:256]], axis=0)


def windows_kernel(count_x, split_ref, w_one, w_two, cot_ref, *refs):
    gx_refs, refs = refs[:count_x], refs[count_x:]
    short_ref, outer_ref, short_act, slope_ref, cot_all = refs[:5]
    ends_ref, feat_ref, here_ref, after_ref, grad_ref, inner_ref, act_ref = refs[5:]
    high_x = from_high(position("gx"), [ref[96:128, :].astype(F32) for ref in gx_refs])
    for k in range(2):
        cot = cot_ref[k].astype(F32)
        for m in range(16):
            row = 16 * k + m
            cot_all[k, 16 * m : 16 * m + 8, :] = cot[:, 128 * m : 128 * m + 128]
            cot_all[k, 16 * m + 8 : 16 * m + 16, :] = jnp.where(
                iota((8, 128), 0) == 0, high_x[row : row + 1, :], 0.0
            )

    lane = iota((128, 1152), 1)
    cell = iota((128, 1152), 0)
    block = lane >> 7
    offset = lane & 31
    part = (lane & 127) >> 5
    wanted = jnp.where(offset <= 16, 16 * block - 1 + offset, -9)
    wanted = jnp.where(block == 8, jnp.where(offset == 0, 127, -9), wanted)
    hit = cell == wanted
    picks = jnp.concatenate(
        [jnp.where(hit & (part == c), 1.0, 0.0).astype(BF) for c in range(3)], axis=0
    )
    for s in range(5):
        lhs = jnp.concatenate([split_ref[s, 128 * c : 128 * c + 128, :] for c in range(3)], axis=1)
        exact = dot(lhs, picks)
        found = exact.astype(BF)
        for z in range(8):
            for q in range(4):
                first = exact[16 * z : 16 * z + 8, 256 * q + 128 : 256 * q + 256]
                if q < 3:
                    second = exact[16 * z : 16 * z + 8, 256 * q + 256 : 256 * q + 384]
                else:
                    second = jnp.zeros((8, 128), F32)
                short_ref[s, z, 16 * q : 16 * q + 16, :] = jnp.concatenate([first, second], axis=0).astype(BF)
        for n in range(1, 8):
            for z in range(8):
                inner_ref[s, z, 16 * n - 16 : 16 * n, :] = found[16 * z : 16 * z + 16, 128 * n : 128 * n + 128]
        outer_ref[s, :, 0:128] = found[:, 0:128]
        outer_ref[s, :, 128:256] = found[:, 1024:1152]
    weights = w_one[...]
    for p in range(4):
        for t in range(2):
            pieces = []
            for a in range(3):
                for b in range(3):
                    z = 2 * p + a - 1
                    pieces.append(inner_ref[SLOTS[t][b], z] if z >= 0 else jnp.zeros((112, 128), BF))
            versions, slope = first_level(dot(jnp.concatenate(pieces, axis=1), weights), t)
            for b, value in versions:
                for n in range(7):
                    short_act[b, p, 16 * n : 16 * n + 16, :] = short_pair(value, 16 * n).astype(BF)
                value = value.astype(BF)
                for n in range(7):
                    act_ref[b, p, 32 * n : 32 * n + 16, :] = value[16 * n : 16 * n + 16, 0:128]
                    act_ref[b, p, 32 * n + 16 : 32 * n + 32, :] = value[16 * n : 16 * n + 16, 128:256]
            for n in range(7):
                slope_ref[p, t, 16 * n : 16 * n + 16, :] = short_pair(slope, 16 * n)
    weights = w_two[...]
    delta, patches = [], []
    for k in range(2):
        planes = [(b, 2 * k + a - 1) for a in range(3) for b in range(3)]
        lhs = [act_ref[b, p] if p >= 0 else jnp.zeros((224, 128), BF) for b, p in planes]
        out = dot(jnp.concatenate(lhs, axis=1), weights)
        ends_ref[k, 0] = out[0:16, 0:128]
        ends_ref[k, 1] = out[208:224, 128:256]
        feat, value = second_level(out[16:224, 0:128] + out[0:208, 128:256], cot_all[k, 48:256, :])
        feat_ref[k] = jnp.concatenate([feat[16 * m : 16 * m + 8] for m in range(13)], axis=1).astype(BF)
        value = value.reshape(13, 16, 128)
        here = value[:, 0:8].reshape(104, 128)
        here_ref[k] = here
        after_ref[k] = value[:, 1:9].reshape(104, 128)
        zero = jnp.zeros((8, 128), F32)
        both = [jnp.concatenate([zero, here], axis=0), jnp.concatenate([here, zero], axis=0)]
        delta.append(jnp.concatenate(both, axis=1).astype(BF))
        short = [short_act[b, p] if p >= 0 else jnp.zeros((112, 128), BF) for b, p in planes]
        patches.append(jnp.concatenate(short, axis=1))
    delta, patches = jnp.concatenate(delta, axis=0), jnp.concatenate(patches, axis=0)
    for first in range(0, 1152, 256):
        last = min(first + 256, 1152)
        grad_ref[:, first:last] = dot(delta, patches[:, first:last], ((0,), (0,)))[0:192]


def main_kernel(
    count_y,
    ranks,
    short_ref,
    outer_ref,
    short_act,
    slope_ref,
    cot_ref,
    ends_ref,
    feat_in,
    here_in,
    after_in,
    grad_in,
    halo_ref,
    w_one,
    w_two,
    *refs,
):
    gy_refs, refs = refs[:count_y], refs[count_y:]
    feat_hbm, level_hbm, refs = refs[0], refs[1], refs[2:]
    dealt, refs = refs[:ranks], refs[ranks:]
    edges, short_edges, outer_act, outer_short, outer_slope, rows_out, total, feat_ref, level_ref, sems = refs
    place_y = position("gy")
    copies = []

    got_y = [ref[...].astype(F32) for ref in gy_refs]
    low_y = from_low(place_y, got_y)
    high_y = from_high(place_y, got_y)
    halo = jnp.concatenate([low_y[0:64], high_y[0:64]], axis=1).astype(BF)
    first_half = iota((16, 128), 1) < 64
    cot_y = [jnp.where(first_half, value, 0.0) for value in (high_y[64:80], pltpu.roll(high_y[64:80], 64, 1))]
    brought = dot(halo, halo_ref[...])
    for s in range(5):
        base = 512 * min(s, 3)
        found = [brought[:, base + 256 * parity : base + 256 * parity + 256].reshape(4, 16, 256) for parity in range(2)]
        edge = jnp.stack(found, axis=1).reshape(8, 16, 256)
        if s == 4:
            edge = jnp.concatenate([edge[:, 15:16], edge[:, 0:15]], axis=1)
        exact = outer_ref[s].astype(F32) + edge.reshape(128, 256)
        value = exact.astype(BF)
        for z in range(8):
            edges[s, z, 0:16, :] = value[16 * z : 16 * z + 16, 0:128]
            edges[s, z, 16:32, :] = value[16 * z : 16 * z + 16, 128:256]
            other = short_ref[s, z, 48:64, :].astype(F32)
            short_edges[s, z] = jnp.concatenate([other[0:8], exact[16 * z : 16 * z + 8, 0:128]], axis=0).astype(BF)

    def window(s, z):
        if z < 0:
            return jnp.zeros((64, 128), BF)
        return jnp.concatenate([short_ref[s, z, 0:48, :], short_edges[s, z]], axis=0)

    weights = w_one[...]
    for t in range(2):
        rows = []
        for p in range(4):
            pieces = []
            for a in range(3):
                for b in range(3):
                    z = 2 * p + a - 1
                    pieces.append(edges[SLOTS[t][b], z] if z >= 0 else jnp.zeros((32, 128), BF))
            rows.append(jnp.concatenate(pieces, axis=1))
        versions, slope = first_level(dot(jnp.concatenate(rows, axis=0), weights), t)
        for p in range(4):
            first, second = 32 * p, 32 * p + 16
            for b, value in versions:
                before = jnp.concatenate([value[second : second + 8, 128:256], jnp.zeros((8, 128), F32)], axis=0)
                outer_short[b, p, 0:16, :] = before.astype(BF)
                outer_short[b, p, 16:32, :] = short_pair(value, first).astype(BF)
                outer_act[b, p, 0:16, :] = value[second : second + 16, 128:256].astype(BF)
                outer_act[b, p, 16:32, :] = value[first : first + 16, 0:128].astype(BF)
                outer_act[b, p, 32:48, :] = value[first : first + 16, 128:256].astype(BF)
                outer_act[b, p, 48:64, :] = value[second : second + 16, 0:128].astype(BF)
            outer_slope[p, t] = short_pair(slope, first)

    lhs = []
    for k in range(2):
        planes = [(b, 2 * k + a - 1) for a in range(3) for b in range(3)]
        lhs.append(
            jnp.concatenate([outer_act[b, p] if p >= 0 else jnp.zeros((64, 128), BF) for b, p in planes], axis=1)
        )
    out = dot(jnp.concatenate(lhs, axis=0), w_two[...])
    pairs, pairs_next, delta, patches = [], [], [], []
    for k in range(2):
        own = out[64 * k : 64 * k + 64]
        pre = jnp.concatenate(
            [own[16:48, 0:128], ends_ref[k, 0], own[48:64, 0:128]], axis=0
        ) + jnp.concatenate([own[0:48, 128:256], ends_ref[k, 1]], axis=0)
        feat, value = second_level(pre, jnp.concatenate([cot_ref[k, 0:48, :], cot_y[k]], axis=0))
        feat_ref[k, :, 0:384] = jnp.concatenate([feat[16 * m : 16 * m + 8] for m in range(3)], axis=1).astype(BF)
        feat_ref[k, :, 384:2048] = feat_in[k]
        copies.append(pltpu.make_async_copy(feat_ref.at[k], feat_hbm.at[k], sems.at[k]))
        copies[-1].start()
        value = value.reshape(4, 16, 128)
        outer = value[:, 0:8].reshape(32, 128)
        here = jnp.concatenate([outer[0:24], here_in[k], outer[24:32]], axis=0)
        outer_after = value[:, 1:9].reshape(32, 128)
        after = jnp.concatenate([outer_after[0:24], after_in[k], outer_after[24:32]], axis=0)
        pairs.append(jnp.concatenate([here[0:128], here[8:136]], axis=1).astype(BF))
        pairs_next.append(jnp.concatenate([after[0:128], after[8:136]], axis=1).astype(BF))
        zero = jnp.zeros((8, 128), F32)
        both = [
            jnp.concatenate([zero, zero, outer[0:24], zero], axis=0),
            jnp.concatenate([outer[0:8], zero, outer[8:24], zero, zero], axis=0),
        ]
        delta.append(jnp.concatenate(both, axis=1).astype(BF))
        short = []
        for a in range(3):
            for b in range(3):
                p = 2 * k + a - 1
                if p < 0:
                    short.append(jnp.zeros((48, 128), BF))
                else:
                    short.append(jnp.concatenate([outer_short[b, p], short_act[b, p, 0:16, :]], axis=0))
        patches.append(jnp.concatenate(short, axis=1))
    delta, patches = jnp.concatenate(delta, axis=0), jnp.concatenate(patches, axis=0)

    lhs_rows, rhs_rows = [], []
    for p in range(4):
        depth = [(1, p // 2)] if p % 2 == 0 else [(2, (p - 1) // 2), (0, (p + 1) // 2)]
        for t in range(2):
            width = [(1, pairs)] if t == 0 else [(2, pairs), (0, pairs_next)]
            taps = [(3 * a + b, source[k]) for a, k in depth if k < 2 for b, source in width]
            level = dot(
                jnp.concatenate([source for _, source in taps], axis=1),
                jnp.concatenate([w_two[128 * tap : 128 * tap + 128, :] for tap, _ in taps], axis=1),
                ((1,), (1,)),
            )
            level = level.astype(BF).astype(F32)
            for m in range(16):
                rows_out[m, pl.ds(t, 8, stride=2), :] = level[8 * m : 8 * m + 8]
            slope = jnp.concatenate([outer_slope[p, t], slope_ref[p, t]], axis=0)
            value = level * slope
            blocks = [
                jnp.concatenate([value[16 * n : 16 * n + 8], value[16 * n + 8 : 16 * n + 16]], axis=1)
                for n in (1, 2, 3, 4, 5, 6, 7, 0)
            ]
            lhs_rows.append(jnp.concatenate(blocks, axis=0).astype(BF))
            rhs_rows.append(
                jnp.concatenate([window(SLOTS[t][b], 2 * p + a - 1) for a in range(3) for b in range(3)], axis=1)
            )
        level_ref[p] = jnp.concatenate([rows_out[m] for m in range(16)], axis=1).astype(BF)
        copies.append(pltpu.make_async_copy(level_ref.at[p], level_hbm.at[p], sems.at[2 + p]))
        copies[-1].start()
    delta_one = jnp.concatenate(lhs_rows, axis=0).T
    windows = jnp.concatenate(rhs_rows, axis=0)

    place = iota((64, 128), 1) >> 5
    turned = []
    for ab in range(9):
        if ab % 2 == 0:
            first, last = 128 * ab, min(128 * ab + 256, 1152)
            grad = dot(delta, patches[:, first:last], ((0,), (0,)))[0:192] + grad_in[:, first:last]
        column = 128 * (ab % 2)
        a0, a1, a2 = (grad[64 * j : 64 * j + 64, column : column + 128] for j in range(3))
        r0, r1, r2 = (pltpu.roll(a, 64, 1) for a in (a0, a1, a2))
        joined = jnp.where(place == 0, a0 + r1, jnp.where(place == 1, a1 + r2, a1 + r0))
        shift = (3 * ab - 1) % 4
        other = (shift + 2) % 4
        outer = pltpu.roll(joined, 32 * shift, 1) if shift else joined
        inner = pltpu.roll(joined, 32 * other, 1) if other else joined
        turned += [outer, inner, outer]
    turned.append(jnp.zeros((64, 128), F32))
    for v in range(7):
        t0, t1, t2, t3 = turned[4 * v : 4 * v + 4]
        total[:, 128 * v : 128 * v + 128] = jnp.where(
            place < 2, jnp.where(place == 0, t0, t1), jnp.where(place == 2, t2, t3)
        )

    place = iota((32, 128), 1)
    found = jnp.zeros((32, 128), F32)
    for tap in range(9):
        if tap % 2 == 0:
            grad = dot(delta_one, windows[:, 128 * tap : min(128 * tap + 256, 1152)])
        column = 128 * (tap % 2)
        some = jnp.zeros((32, 128), F32)
        for t in range(8):
            piece = grad[32 * t : 32 * t + 32, column : column + 128]
            shift = (3 * tap - 2 * t) % 128
            some = some + (pltpu.roll(piece, shift, 1) if shift else piece)
        local = place & 31
        found = jnp.where((local >= 3 * tap) & (local < 3 * tap + 3), some, found)
    total[:, 896:1024] = jnp.zeros((64, 128), F32)
    tall, short = 64 // ranks, 32 // ranks
    for d in range(ranks):
        total[tall * d : tall * d + short, 896:1024] = found[short * d : short * d + short]
    rank = lax.axis_index("dp")
    for step, out in enumerate(dealt):
        if tall % 8 == 0:
            start = pl.multiple_of((rank ^ step) * tall, tall)
            picked = total[pl.ds(start, tall), :]
        else:
            picked = total[0:tall, :]
            for d in range(1, ranks):
                picked = jnp.where((rank ^ step) == d, total[d * tall : d * tall + tall, :], picked)
        out[...] = picked.astype(BF)
    for copy in copies:
        copy.wait()


def sum_kernel(*refs):
    parts, out_ref = refs[:-1], refs[-1]
    values = [ref[...].astype(F32) for ref in parts]
    while len(values) > 1:
        values = [values[i] + values[i + 1] for i in range(0, len(values), 2)]
    out_ref[...] = values[0].astype(out_ref.dtype)


def share_kernel(mine_ref, first_ref, second_ref, out_ref):
    first = first_ref[...].astype(F32)
    odd = position("gx")[0]
    out_ref[...] = first + jnp.where(odd, second_ref[...], mine_ref[...]).astype(F32)


def last_kernel(scale_one, scale_two, *refs):
    parts, (one_ref, two_ref) = refs[:-2], refs[-2:]
    values = [ref[...].astype(F32) for ref in parts]
    while len(values) > 1:
        values = [values[i] + values[i + 1] for i in range(0, len(values), 2)]
    value = values[0]
    tall = value.shape[0]
    short = tall // 2
    scaled = value[:, 0:896] * scale_two
    for tap in range(27):
        two_ref[tap] = scaled[:, 32 * tap : 32 * tap + 32]
    rows = value[0:short, 896:1024] * scale_one
    if short < 8:
        rows = jnp.concatenate([rows, jnp.zeros((8 - short, 128), F32)], axis=0)
    turned = rows.T
    for c in range(3):
        one_ref[:, c, :] = turned[32 * c : 32 * c + 27, 0:short]


def call(kernel, outs, args, scratch=(), space=pltpu.VMEM, in_hbm=0, flops=0):
    spaces = [pltpu.HBM] * in_hbm + [pltpu.VMEM] * (len(outs) - in_hbm)
    return pl.pallas_call(
        kernel,
        out_shape=outs,
        in_specs=[pl.BlockSpec(memory_space=space)] * len(args),
        out_specs=[pl.BlockSpec(memory_space=kind) for kind in spaces],
        scratch_shapes=list(scratch),
        compiler_params=pltpu.CompilerParams(vmem_limit_bytes=VMEM_LIMIT),
        cost_estimate=pl.CostEstimate(flops=flops, bytes_accessed=1 << 20, transcendentals=0),
    )(*args)


def shape(dims, dtype):
    return jax.ShapeDtypeStruct(dims, dtype)


def exchange(value, axis, step):
    return lax.ppermute(value, axis, [(i, i ^ step) for i in range(lax.axis_size(axis))])


def trade_shared(value, even_step, odd_step):
    count, columns, ranks = lax.axis_size("gy"), lax.axis_size("gx"), lax.axis_size("dp")
    pairs = []
    for d in range(ranks):
        for g in range(columns):
            for i in range(count):
                to_d, to_i = d, i ^ (odd_step if g % 2 else even_step)
                if g % 2 == 0 and even_step == 0:
                    to_d = (d ^ 1) % ranks
                pairs.append(((d * columns + g) * count + i, (to_d * columns + g) * count + to_i))
    return lax.ppermute(value, ("dp", "gx", "gy"), pairs)


def body(magnetic, kernel_one, kernel_two, cotangent):
    ranks, count_gx, count_gy = (lax.axis_size(axis) for axis in ("dp", "gx", "gy"))
    depth = magnetic.shape[2]
    samples_all = magnetic.shape[0] * ranks
    cells_x = magnetic.shape[3] * count_gx
    cells_y = magnetic.shape[4] * count_gy
    scale_one = 1.0 / math.sqrt(samples_all * (depth // 2) * (cells_x // 2) * (cells_y // 2))
    scale_two = 1.0 / math.sqrt(samples_all * (depth // 4) * (cells_x // 4) * (cells_y // 4))
    field = magnetic.reshape(24, 32, 128)
    cot = cotangent.reshape(2, 8, 2048)
    one = kernel_one.reshape(27, 3, 32)
    two = kernel_two.reshape(864, 64)

    swaps_x, swaps_y = swaps("gx"), swaps("gy")
    nx, ny = len(swaps_x), len(swaps_y)
    operands = [pltpu.with_memory_space_constraint(array, pltpu.HBM) for array in (field, cot, one, two)]
    field, cot, one, two, *edges = call(
        lambda *refs: edge_x_kernel(nx, *refs),
        [shape(array.shape, BF) for array in operands] + [shape((128, 128), BF)] * nx,
        operands,
        [pltpu.VMEM((128, 128), F32), pltpu.SemaphoreType.DMA((4,))],
        space=pltpu.HBM,
    )
    got_x = [lax.ppermute(edge, ("dp", "gx"), pairs) for edge, pairs in zip(edges, swaps_x)]
    w_one, w_two, picks = call(
        weights_kernel,
        [shape((1152, 256), BF), shape((1152, 256), BF), shape((256, 2048), BF)],
        (one, two),
        [pltpu.VMEM((88, 32), F32)],
        flops=1 << 30,
    )
    split, *edges = call(
        lambda *refs: edge_y_kernel(nx, ny, *refs),
        [shape((5, 384, 128), BF)] + [shape((80, 128), BF)] * ny,
        (field, cot, *got_x),
        [pltpu.VMEM((24, 72, 128), F32)],
    )
    got_y = [lax.ppermute(edge, ("dp", "gy"), pairs) for edge, pairs in zip(edges, swaps_y)]
    first = call(
        lambda *refs: windows_kernel(nx, *refs),
        [
            shape((5, 8, 64, 128), BF),
            shape((5, 128, 256), BF),
            shape((3, 4, 112, 128), BF),
            shape((4, 2, 112, 128), F32),
            shape((2, 256, 128), F32),
            shape((2, 2, 16, 128), F32),
            shape((2, 8, 1664), BF),
            shape((2, 104, 128), F32),
            shape((2, 104, 128), F32),
            shape((192, 1152), F32),
        ],
        (split, w_one, w_two, cot, *got_x),
        [pltpu.VMEM((5, 8, 112, 128), BF), pltpu.VMEM((3, 4, 224, 128), BF)],
        flops=1 << 31,
    )
    tall = 64 // ranks
    features, level, *dealt = call(
        lambda *refs: main_kernel(ny, ranks, *refs),
        [shape((2, 8, 2048), BF), shape((4, 16, 2048), BF)] + [shape((tall, 1024), BF)] * ranks,
        (*first, picks, w_one, w_two, *got_y),
        [
            pltpu.VMEM((5, 8, 32, 128), BF),
            pltpu.VMEM((5, 8, 16, 128), BF),
            pltpu.VMEM((3, 4, 64, 128), BF),
            pltpu.VMEM((3, 4, 32, 128), BF),
            pltpu.VMEM((4, 2, 16, 128), F32),
            pltpu.VMEM((16, 16, 128), F32),
            pltpu.VMEM((64, 1024), F32),
            pltpu.VMEM((2, 8, 2048), BF),
            pltpu.VMEM((4, 16, 2048), BF),
            pltpu.SemaphoreType.DMA((6,)),
        ],
        in_hbm=2,
    )
    terms = [exchange(dealt[step], "dp", step) for step in (ranks - 1, *range(1, ranks - 1))] + dealt[:1]
    mine, = call(sum_kernel, [shape((tall, 1024), BF)], terms)
    step = 1
    while step < count_gx:
        mine, = call(sum_kernel, [shape((tall, 1024), BF)], (mine, exchange(mine, "gx", step)))
        step *= 2
    if count_gy == 4:
        terms = [mine, trade_shared(mine, 1, 2), trade_shared(mine, 0, 3)]
        mine, = call(share_kernel, [shape((tall, 1024), F32)], terms)
        terms = [mine, exchange(mine, "gx", 1)]
    else:
        terms = [mine] + [exchange(mine, "gy", step) for step in range(1, count_gy)]
    grad_one, grad_two = call(
        lambda *refs: last_kernel(scale_one, scale_two, *refs),
        [shape((27, 3, tall // 2), F32), shape((27, tall, 32), F32)],
        terms,
    )
    grad_one = grad_one.reshape(3, 3, 3, 3, tall // 2)
    grad_two = jnp.transpose(grad_two.reshape(3, 3, 3, tall, 32), (0, 1, 2, 4, 3))
    return (
        features.reshape(1, 2, 8, 2048),
        level.reshape(1, 4, 16, 2048),
        grad_one,
        grad_two,
    )


def solution(mesh):
    in_specs = (P("dp", None, None, "gx", "gy"), P(), P(), P("dp", None, "gx", "gy"))
    out_specs = (
        P("dp", None, "gx", "gy"),
        P("dp", None, "gx", "gy"),
        P(None, None, None, None, "dp"),
        P(None, None, None, None, "dp"),
    )
    return jax.shard_map(body, mesh=mesh, in_specs=in_specs, out_specs=out_specs, check_vma=False)
```

```python
import math

import jax
import jax.numpy as jnp
from jax import lax
from jax.experimental import pallas as pl
from jax.experimental.pallas import tpu as pltpu
from jax.sharding import PartitionSpec as P

BF = jnp.bfloat16
F32 = jnp.float32
VMEM_LIMIT = 32 * 1024 * 1024


def iota(shape, dim):
    return lax.broadcasted_iota(jnp.int32, shape, dim)


def dot(lhs, rhs, contract=((1,), (0,))):
    return lax.dot_general(lhs, rhs, (contract, ((), ())), preferred_element_type=F32)


def swaps(axis):
    count, ranks = lax.axis_size(axis), lax.axis_size("dp")
    found = []
    for first in range(min(2, count - 1)):
        pairs = []
        for d in range(ranks):
            for i in range(count):
                other = i + 1 if i % 2 == first else i - 1
                if 0 <= other < count:
                    pairs.append((d * count + i, d * count + other))
                else:
                    pairs.append((d * count + i, (d ^ 1) % ranks * count + i))
        found.append(pairs)
    return found


def position(axis):
    index = lax.axis_index(axis)
    return lax.rem(index, 2) == 1, index == 0, index == lax.axis_size(axis) - 1


def from_low(place, got):
    odd, first, _ = place
    second = got[1] if len(got) > 1 else got[0]
    return jnp.where(first, 0.0, jnp.where(odd, got[0], second))


def from_high(place, got):
    odd, _, last = place
    second = got[1] if len(got) > 1 else got[0]
    return jnp.where(last, 0.0, jnp.where(odd, second, got[0]))


def edge_x_kernel(count, *refs):
    hbm, refs = refs[:4], refs[4:]
    held, outs, (stage, sems) = refs[:4], refs[4 : 4 + count], refs[4 + count :]
    fetches = [pltpu.make_async_copy(hbm[i], held[i], sems.at[i]) for i in range(4)]
    for fetch in fetches:
        fetch.start()
    mag_ref, cot_ref = held[:2]
    odd = position("gx")[0]
    planes = mag_ref.shape[0]
    blocks = cot_ref.shape[2] // 128
    for fetch in fetches[:2]:
        fetch.wait()
    field = mag_ref[...].astype(F32)
    low = field[:, 0:4, :]
    high = field[:, field.shape[1] - 4 :, :]
    cot = [cot_ref[k].astype(F32)[0:1, :] for k in range(2)]
    for turn in range(count):
        toward_high = odd if turn == 1 else jnp.logical_not(odd)
        picked = jnp.where(toward_high, high, low)
        for g in range(planes):
            stage[4 * g : 4 * g + 4, :] = picked[g]
        for k in range(2):
            for m in range(blocks):
                row = 4 * planes + 16 * k + m
                stage[row : row + 1, :] = cot[k][:, 128 * m : 128 * m + 128]
        outs[turn][...] = stage[...].astype(BF)
    for fetch in fetches[2:]:
        fetch.wait()


def edge_y_kernel(count_x, count_y, mag_ref, cot_ref, *refs):
    got_refs, refs = refs[:count_x], refs[count_x:]
    split_ref, outs = refs[0], refs[1 : 1 + count_y]
    tall, = refs[1 + count_y :]
    place_x, place_y = position("gx"), position("gy")
    planes = mag_ref.shape[0]
    got = [ref[...].astype(F32) for ref in got_refs]
    low = from_low(place_x, got)
    high = from_high(place_x, got)
    zeros = jnp.zeros((24, 128), F32)
    for g in range(planes):
        edge = low[4 * g : 4 * g + 4, :]
        tall[g, 0:8, :] = jnp.broadcast_to(edge[3:4, :], (8, 128))
        tall[g, 8:40, :] = mag_ref[g].astype(F32)
        tall[g, 40:44, :] = high[4 * g : 4 * g + 4, :]
        tall[g, 44:68, :] = zeros
        tall[g, 68:72, :] = edge
    starts = (8, 9, 10, 11, 7)
    split = []
    for slot in range(5):
        parts = [tall[g, pl.ds(starts[slot], 16, stride=4), :].astype(BF) for g in range(planes)]
        whole = jnp.concatenate(parts, axis=0)
        split_ref[slot] = whole
        split.append(whole)
    rows = planes // 3 * 16
    lhs = jnp.concatenate(
        [split[s][rows * c : rows * c + rows] for s in range(4) for c in range(3)], axis=1
    )
    lane = iota((128, 128), 1)
    cell = iota((128, 128), 0)
    slot = lane & 3
    wanted = jnp.where(lane < 64, 124 + slot, slot)
    group = (lane & 63) >> 2
    picks = []
    for s in range(4):
        for c in range(3):
            hit = (group == 4 * s + c) & (cell == wanted)
            picks.append(jnp.where(hit, 1.0, 0.0).astype(BF))
    both = dot(lhs, jnp.concatenate(picks, axis=0)).reshape(4, 2, 16, 128)
    lower, upper = both[:, 0].reshape(64, 128), both[:, 1].reshape(64, 128)
    left = iota((64, 128), 1) < 64
    toward = [
        jnp.where(left, lower, pltpu.roll(upper, 64, 1)),
        jnp.where(left, pltpu.roll(lower, 64, 1), upper),
    ]
    cot_rows = []
    for k in range(2):
        own = cot_ref[k].astype(F32)[:, 0:128]
        row = 4 * planes + 16 * k
        cot_rows.append(jnp.concatenate([own, high[row : row + 1, :], jnp.zeros((7, 128), F32)], axis=0))
    cot_rows = jnp.where(iota((16, 128), 1) < 64, cot_rows[0], pltpu.roll(cot_rows[1], 64, 1))
    odd = place_y[0]
    for turn in range(count_y):
        toward_high = odd if turn == 1 else jnp.logical_not(odd)
        outs[turn][0:64, :] = jnp.where(toward_high, toward[0], toward[1]).astype(BF)
        outs[turn][64:80, :] = cot_rows.astype(BF)


def weights_kernel(one_ref, two_ref, w_one, w_two, halo_ref, rows_one):
    lane = iota((32, 256), 1)
    spread = jnp.where(iota((32, 256), 0) == (lane & 31), 1.0, 0.0).astype(BF)
    rows_one[80:88, :] = jnp.zeros((8, 32), F32)
    for i in range(27):
        rows_one[3 * i : 3 * i + 3, :] = one_ref[i].astype(F32)
    wide = dot(rows_one[...].astype(BF), spread)
    window = iota((32, 256), 0) - 2 * (lane >> 5)
    for tap in range(9):
        for c in range(3):
            block = jnp.zeros((32, 256), F32)
            for e in range(3):
                row = (3 * tap + e) * 3 + c
                block = jnp.where(window == e, wide[row : row + 1, :], block)
            w_one[128 * tap + 32 * c : 128 * tap + 32 * c + 32, :] = block.astype(BF)
        w_one[128 * tap + 96 : 128 * tap + 128, :] = jnp.zeros((32, 256), BF)

    lane = iota((64, 128), 1)
    spread = jnp.where(iota((64, 128), 0) == (lane & 63), 1.0, 0.0).astype(BF)
    twice = dot(two_ref[...], spread)
    left = iota((32, 128), 1) < 64
    for tap in range(9):
        k0, k1, k2 = (twice[32 * (3 * tap + e) : 32 * (3 * tap + e) + 32] for e in range(3))
        base = 128 * tap
        w_two[base : base + 32, 0:128] = jnp.where(left, k1, 0.0).astype(BF)
        w_two[base + 32 : base + 64, 0:128] = jnp.where(left, k2, k0).astype(BF)
        w_two[base + 64 : base + 96, 0:128] = jnp.where(left, 0.0, k1).astype(BF)
        w_two[base + 96 : base + 128, 0:128] = jnp.where(left, 0.0, k2).astype(BF)
        w_two[base : base + 96, 128:256] = jnp.zeros((96, 128), BF)
        w_two[base + 96 : base + 128, 128:256] = jnp.where(left, k0, 0.0).astype(BF)

    lane = iota((256, 256), 1)
    code = iota((256, 256), 0)
    offset = lane & 31
    part = (lane & 127) >> 5
    wanted = jnp.where(
        lane < 128,
        jnp.where(offset == 0, 3, -999),
        jnp.where(
            (offset >= 1) & (offset <= 4), 127 + offset, jnp.where((offset >= 14) & (offset <= 16), offset - 13, -999)
        ),
    )
    wanted = jnp.where(part < 3, wanted + 4 * part, -999)
    for s in range(4):
        for parity in range(2):
            hit = code - (64 * parity + 16 * s) == wanted
            base = 256 * (2 * s + parity)
            halo_ref[:, base : base + 256] = jnp.where(hit, 1.0, 0.0).astype(BF)


SLOTS = ((4, 0, 1), (1, 2, 3))


def first_level(pre, t):
    sig = jax.nn.sigmoid(pre)
    hidden = pre * sig
    slope = sig * (1.0 + pre * (1.0 - sig))
    if t == 0:
        return [(1, hidden)], slope
    rows, width = hidden.shape
    later = hidden.reshape(rows // 16, 16, width)
    later = jnp.concatenate([later[:, 15:16], later[:, 0:15]], axis=1).reshape(rows, width)
    return [(2, hidden), (0, later)], slope


def second_level(pre, cot):
    sig = jax.nn.sigmoid(pre)
    return pre * sig, cot * (sig * (1.0 + pre * (1.0 - sig)))


def short_pair(value, row):
    return jnp.concatenate([value[row : row + 8, 0:128], value[row : row + 8, 128:256]], axis=0)


def windows_kernel(count_x, split_ref, w_one, w_two, cot_ref, *refs):
    gx_refs, refs = refs[:count_x], refs[count_x:]
    short_ref, outer_ref, short_act, slope_ref, cot_all = refs[:5]
    ends_ref, feat_ref, here_ref, after_ref, grad_ref, inner_ref, act_ref = refs[5:]
    high_x = from_high(position("gx"), [ref[96:128, :].astype(F32) for ref in gx_refs])
    for k in range(2):
        cot = cot_ref[k].astype(F32)
        for m in range(16):
            row = 16 * k + m
            cot_all[k, 16 * m : 16 * m + 8, :] = cot[:, 128 * m : 128 * m + 128]
            cot_all[k, 16 * m + 8 : 16 * m + 16, :] = jnp.where(
                iota((8, 128), 0) == 0, high_x[row : row + 1, :], 0.0
            )

    lane = iota((128, 1152), 1)
    cell = iota((128, 1152), 0)
    block = lane >> 7
    offset = lane & 31
    part = (lane & 127) >> 5
    wanted = jnp.where(offset <= 16, 16 * block - 1 + offset, -9)
    wanted = jnp.where(block == 8, jnp.where(offset == 0, 127, -9), wanted)
    hit = cell == wanted
    picks = jnp.concatenate(
        [jnp.where(hit & (part == c), 1.0, 0.0).astype(BF) for c in range(3)], axis=0
    )
    for s in range(5):
        lhs = jnp.concatenate([split_ref[s, 128 * c : 128 * c + 128, :] for c in range(3)], axis=1)
        exact = dot(lhs, picks)
        found = exact.astype(BF)
        for z in range(8):
            for q in range(4):
                first = exact[16 * z : 16 * z + 8, 256 * q + 128 : 256 * q + 256]
                if q < 3:
                    second = exact[16 * z : 16 * z + 8, 256 * q + 256 : 256 * q + 384]
                else:
                    second = jnp.zeros((8, 128), F32)
                short_ref[s, z, 16 * q : 16 * q + 16, :] = jnp.concatenate([first, second], axis=0).astype(BF)
        for n in range(1, 8):
            for z in range(8):
                inner_ref[s, z, 16 * n - 16 : 16 * n, :] = found[16 * z : 16 * z + 16, 128 * n : 128 * n + 128]
        outer_ref[s, :, 0:128] = found[:, 0:128]
        outer_ref[s, :, 128:256] = found[:, 1024:1152]
    weights = w_one[...]
    for p in range(4):
        for t in range(2):
            pieces = []
            for a in range(3):
                for b in range(3):
                    z = 2 * p + a - 1
                    pieces.append(inner_ref[SLOTS[t][b], z] if z >= 0 else jnp.zeros((112, 128), BF))
            versions, slope = first_level(dot(jnp.concatenate(pieces, axis=1), weights), t)
            for b, value in versions:
                for n in range(7):
                    short_act[b, p, 16 * n : 16 * n + 16, :] = short_pair(value, 16 * n).astype(BF)
                value = value.astype(BF)
                for n in range(7):
                    act_ref[b, p, 32 * n : 32 * n + 16, :] = value[16 * n : 16 * n + 16, 0:128]
                    act_ref[b, p, 32 * n + 16 : 32 * n + 32, :] = value[16 * n : 16 * n + 16, 128:256]
            for n in range(7):
                slope_ref[p, t, 16 * n : 16 * n + 16, :] = short_pair(slope, 16 * n)
    weights = w_two[...]
    delta, patches = [], []
    for k in range(2):
        planes = [(b, 2 * k + a - 1) for a in range(3) for b in range(3)]
        lhs = [act_ref[b, p] if p >= 0 else jnp.zeros((224, 128), BF) for b, p in planes]
        out = dot(jnp.concatenate(lhs, axis=1), weights)
        ends_ref[k, 0] = out[0:16, 0:128]
        ends_ref[k, 1] = out[208:224, 128:256]
        feat, value = second_level(out[16:224, 0:128] + out[0:208, 128:256], cot_all[k, 48:256, :])
        feat_ref[k] = jnp.concatenate([feat[16 * m : 16 * m + 8] for m in range(13)], axis=1).astype(BF)
        value = value.reshape(13, 16, 128)
        here = value[:, 0:8].reshape(104, 128)
        here_ref[k] = here
        after_ref[k] = value[:, 1:9].reshape(104, 128)
        zero = jnp.zeros((8, 128), F32)
        both = [jnp.concatenate([zero, here], axis=0), jnp.concatenate([here, zero], axis=0)]
        delta.append(jnp.concatenate(both, axis=1).astype(BF))
        short = [short_act[b, p] if p >= 0 else jnp.zeros((112, 128), BF) for b, p in planes]
        patches.append(jnp.concatenate(short, axis=1))
    delta, patches = jnp.concatenate(delta, axis=0), jnp.concatenate(patches, axis=0)
    for first in range(0, 1152, 256):
        last = min(first + 256, 1152)
        grad_ref[:, first:last] = dot(delta, patches[:, first:last], ((0,), (0,)))[0:192]


def main_kernel(
    count_y,
    ranks,
    short_ref,
    outer_ref,
    short_act,
    slope_ref,
    cot_ref,
    ends_ref,
    feat_in,
    here_in,
    after_in,
    grad_in,
    halo_ref,
    w_one,
    w_two,
    *refs,
):
    gy_refs, refs = refs[:count_y], refs[count_y:]
    feat_hbm, level_hbm, refs = refs[0], refs[1], refs[2:]
    dealt, refs = refs[:ranks], refs[ranks:]
    edges, short_edges, outer_act, outer_short, outer_slope, rows_out, total, feat_ref, level_ref, sems = refs
    place_y = position("gy")
    copies = []

    got_y = [ref[...].astype(F32) for ref in gy_refs]
    low_y = from_low(place_y, got_y)
    high_y = from_high(place_y, got_y)
    halo = jnp.concatenate([low_y[0:64], high_y[0:64]], axis=1).astype(BF)
    first_half = iota((16, 128), 1) < 64
    cot_y = [jnp.where(first_half, value, 0.0) for value in (high_y[64:80], pltpu.roll(high_y[64:80], 64, 1))]
    brought = dot(halo, halo_ref[...])
    for s in range(5):
        base = 512 * min(s, 3)
        found = [brought[:, base + 256 * parity : base + 256 * parity + 256].reshape(4, 16, 256) for parity in range(2)]
        edge = jnp.stack(found, axis=1).reshape(8, 16, 256)
        if s == 4:
            edge = jnp.concatenate([edge[:, 15:16], edge[:, 0:15]], axis=1)
        exact = outer_ref[s].astype(F32) + edge.reshape(128, 256)
        value = exact.astype(BF)
        for z in range(8):
            edges[s, z, 0:16, :] = value[16 * z : 16 * z + 16, 0:128]
            edges[s, z, 16:32, :] = value[16 * z : 16 * z + 16, 128:256]
            other = short_ref[s, z, 48:64, :].astype(F32)
            short_edges[s, z] = jnp.concatenate([other[0:8], exact[16 * z : 16 * z + 8, 0:128]], axis=0).astype(BF)

    def window(s, z):
        if z < 0:
            return jnp.zeros((64, 128), BF)
        return jnp.concatenate([short_ref[s, z, 0:48, :], short_edges[s, z]], axis=0)

    weights = w_one[...]
    for t in range(2):
        rows = []
        for p in range(4):
            pieces = []
            for a in range(3):
                for b in range(3):
                    z = 2 * p + a - 1
                    pieces.append(edges[SLOTS[t][b], z] if z >= 0 else jnp.zeros((32, 128), BF))
            rows.append(jnp.concatenate(pieces, axis=1))
        versions, slope = first_level(dot(jnp.concatenate(rows, axis=0), weights), t)
        for p in range(4):
            first, second = 32 * p, 32 * p + 16
            for b, value in versions:
                before = jnp.concatenate([value[second : second + 8, 128:256], jnp.zeros((8, 128), F32)], axis=0)
                outer_short[b, p, 0:16, :] = before.astype(BF)
                outer_short[b, p, 16:32, :] = short_pair(value, first).astype(BF)
                outer_act[b, p, 0:16, :] = value[second : second + 16, 128:256].astype(BF)
                outer_act[b, p, 16:32, :] = value[first : first + 16, 0:128].astype(BF)
                outer_act[b, p, 32:48, :] = value[first : first + 16, 128:256].astype(BF)
                outer_act[b, p, 48:64, :] = value[second : second + 16, 0:128].astype(BF)
            outer_slope[p, t] = short_pair(slope, first)

    lhs = []
    for k in range(2):
        planes = [(b, 2 * k + a - 1) for a in range(3) for b in range(3)]
        lhs.append(
            jnp.concatenate([outer_act[b, p] if p >= 0 else jnp.zeros((64, 128), BF) for b, p in planes], axis=1)
        )
    out = dot(jnp.concatenate(lhs, axis=0), w_two[...])
    pairs, pairs_next, delta, patches = [], [], [], []
    for k in range(2):
        own = out[64 * k : 64 * k + 64]
        pre = jnp.concatenate(
            [own[16:48, 0:128], ends_ref[k, 0], own[48:64, 0:128]], axis=0
        ) + jnp.concatenate([own[0:48, 128:256], ends_ref[k, 1]], axis=0)
        feat, value = second_level(pre, jnp.concatenate([cot_ref[k, 0:48, :], cot_y[k]], axis=0))
        feat_ref[k, :, 0:384] = jnp.concatenate([feat[16 * m : 16 * m + 8] for m in range(3)], axis=1).astype(BF)
        feat_ref[k, :, 384:2048] = feat_in[k]
        copies.append(pltpu.make_async_copy(feat_ref.at[k], feat_hbm.at[k], sems.at[k]))
        copies[-1].start()
        value = value.reshape(4, 16, 128)
        outer = value[:, 0:8].reshape(32, 128)
        here = jnp.concatenate([outer[0:24], here_in[k], outer[24:32]], axis=0)
        outer_after = value[:, 1:9].reshape(32, 128)
        after = jnp.concatenate([outer_after[0:24], after_in[k], outer_after[24:32]], axis=0)
        pairs.append(jnp.concatenate([here[0:128], here[8:136]], axis=1).astype(BF))
        pairs_next.append(jnp.concatenate([after[0:128], after[8:136]], axis=1).astype(BF))
        zero = jnp.zeros((8, 128), F32)
        both = [
            jnp.concatenate([zero, zero, outer[0:24], zero], axis=0),
            jnp.concatenate([outer[0:8], zero, outer[8:24], zero, zero], axis=0),
        ]
        delta.append(jnp.concatenate(both, axis=1).astype(BF))
        short = []
        for a in range(3):
            for b in range(3):
                p = 2 * k + a - 1
                if p < 0:
                    short.append(jnp.zeros((48, 128), BF))
                else:
                    short.append(jnp.concatenate([outer_short[b, p], short_act[b, p, 0:16, :]], axis=0))
        patches.append(jnp.concatenate(short, axis=1))
    delta, patches = jnp.concatenate(delta, axis=0), jnp.concatenate(patches, axis=0)

    lhs_rows, rhs_rows = [], []
    for p in range(4):
        depth = [(1, p // 2)] if p % 2 == 0 else [(2, (p - 1) // 2), (0, (p + 1) // 2)]
        for t in range(2):
            width = [(1, pairs)] if t == 0 else [(2, pairs), (0, pairs_next)]
            taps = [(3 * a + b, source[k]) for a, k in depth if k < 2 for b, source in width]
            level = dot(
                jnp.concatenate([source for _, source in taps], axis=1),
                jnp.concatenate([w_two[128 * tap : 128 * tap + 128, :] for tap, _ in taps], axis=1),
                ((1,), (1,)),
            )
            level = level.astype(BF).astype(F32)
            for m in range(16):
                rows_out[m, pl.ds(t, 8, stride=2), :] = level[8 * m : 8 * m + 8]
            slope = jnp.concatenate([outer_slope[p, t], slope_ref[p, t]], axis=0)
            value = level * slope
            blocks = [
                jnp.concatenate([value[16 * n : 16 * n + 8], value[16 * n + 8 : 16 * n + 16]], axis=1)
                for n in (1, 2, 3, 4, 5, 6, 7, 0)
            ]
            lhs_rows.append(jnp.concatenate(blocks, axis=0).astype(BF))
            rhs_rows.append(
                jnp.concatenate([window(SLOTS[t][b], 2 * p + a - 1) for a in range(3) for b in range(3)], axis=1)
            )
        level_ref[p] = jnp.concatenate([rows_out[m] for m in range(16)], axis=1).astype(BF)
        copies.append(pltpu.make_async_copy(level_ref.at[p], level_hbm.at[p], sems.at[2 + p]))
        copies[-1].start()
    delta_one = jnp.concatenate(lhs_rows, axis=0).T
    windows = jnp.concatenate(rhs_rows, axis=0)

    place = iota((64, 128), 1) >> 5
    local = iota((32, 128), 1) & 31
    turned = []
    found = jnp.zeros((32, 128), F32)
    for ab in range(9):
        if ab % 2 == 0:
            first, last = 128 * ab, min(128 * ab + 256, 1152)
            grad_two = dot(delta, patches[:, first:last], ((0,), (0,)))[0:192] + grad_in[:, first:last]
            grad_one = dot(delta_one, windows[:, first:last])
        column = 128 * (ab % 2)
        a0, a1, a2 = (grad_two[64 * j : 64 * j + 64, column : column + 128] for j in range(3))
        r0, r1, r2 = (pltpu.roll(a, 64, 1) for a in (a0, a1, a2))
        joined = jnp.where(place == 0, a0 + r1, jnp.where(place == 1, a1 + r2, a1 + r0))
        shift = (3 * ab - 1) % 4
        other = (shift + 2) % 4
        outer = pltpu.roll(joined, 32 * shift, 1) if shift else joined
        inner = pltpu.roll(joined, 32 * other, 1) if other else joined
        turned += [outer, inner, outer]
        some = jnp.zeros((32, 128), F32)
        for t in range(8):
            piece = grad_one[32 * t : 32 * t + 32, column : column + 128]
            shift = (3 * ab - 2 * t) % 128
            some = some + (pltpu.roll(piece, shift, 1) if shift else piece)
        found = jnp.where((local >= 3 * ab) & (local < 3 * ab + 3), some, found)
    turned.append(jnp.zeros((64, 128), F32))
    for v in range(7):
        t0, t1, t2, t3 = turned[4 * v : 4 * v + 4]
        total[:, 128 * v : 128 * v + 128] = jnp.where(
            place < 2, jnp.where(place == 0, t0, t1), jnp.where(place == 2, t2, t3)
        )
    total[:, 896:1024] = jnp.zeros((64, 128), F32)
    tall, short = 64 // ranks, 32 // ranks
    for d in range(ranks):
        total[tall * d : tall * d + short, 896:1024] = found[short * d : short * d + short]
    rank = lax.axis_index("dp")
    for step, out in enumerate(dealt):
        if tall % 8 == 0:
            start = pl.multiple_of((rank ^ step) * tall, tall)
            picked = total[pl.ds(start, tall), :]
        else:
            picked = total[0:tall, :]
            for d in range(1, ranks):
                picked = jnp.where((rank ^ step) == d, total[d * tall : d * tall + tall, :], picked)
        out[...] = picked.astype(BF)
    for copy in copies:
        copy.wait()


def sum_kernel(*refs):
    parts, out_ref = refs[:-1], refs[-1]
    values = [ref[...].astype(F32) for ref in parts]
    while len(values) > 1:
        values = [values[i] + values[i + 1] for i in range(0, len(values), 2)]
    out_ref[...] = values[0].astype(out_ref.dtype)


def share_kernel(mine_ref, first_ref, second_ref, out_ref):
    first = first_ref[...].astype(F32)
    odd = position("gx")[0]
    out_ref[...] = first + jnp.where(odd, second_ref[...], mine_ref[...]).astype(F32)


def last_kernel(scale_one, scale_two, *refs):
    parts, (one_ref, two_ref) = refs[:-2], refs[-2:]
    values = [ref[...].astype(F32) for ref in parts]
    while len(values) > 1:
        values = [values[i] + values[i + 1] for i in range(0, len(values), 2)]
    value = values[0]
    tall = value.shape[0]
    short = tall // 2
    scaled = value[:, 0:896] * scale_two
    for tap in range(27):
        two_ref[tap] = scaled[:, 32 * tap : 32 * tap + 32]
    rows = value[0:short, 896:1024] * scale_one
    if short < 8:
        rows = jnp.concatenate([rows, jnp.zeros((8 - short, 128), F32)], axis=0)
    turned = rows.T
    for c in range(3):
        one_ref[:, c, :] = turned[32 * c : 32 * c + 27, 0:short]


def call(kernel, outs, args, scratch=(), space=pltpu.VMEM, in_hbm=0, flops=0):
    spaces = [pltpu.HBM] * in_hbm + [pltpu.VMEM] * (len(outs) - in_hbm)
    return pl.pallas_call(
        kernel,
        out_shape=outs,
        in_specs=[pl.BlockSpec(memory_space=space)] * len(args),
        out_specs=[pl.BlockSpec(memory_space=kind) for kind in spaces],
        scratch_shapes=list(scratch),
        compiler_params=pltpu.CompilerParams(vmem_limit_bytes=VMEM_LIMIT),
        cost_estimate=pl.CostEstimate(flops=flops, bytes_accessed=1 << 20, transcendentals=0),
    )(*args)


def shape(dims, dtype):
    return jax.ShapeDtypeStruct(dims, dtype)


def exchange(value, axis, step):
    return lax.ppermute(value, axis, [(i, i ^ step) for i in range(lax.axis_size(axis))])


def trade_shared(value, even_step, odd_step):
    count, columns, ranks = lax.axis_size("gy"), lax.axis_size("gx"), lax.axis_size("dp")
    pairs = []
    for d in range(ranks):
        for g in range(columns):
            for i in range(count):
                to_d, to_i = d, i ^ (odd_step if g % 2 else even_step)
                if g % 2 == 0 and even_step == 0:
                    to_d = (d ^ 1) % ranks
                pairs.append(((d * columns + g) * count + i, (to_d * columns + g) * count + to_i))
    return lax.ppermute(value, ("dp", "gx", "gy"), pairs)


def body(magnetic, kernel_one, kernel_two, cotangent):
    ranks, count_gx, count_gy = (lax.axis_size(axis) for axis in ("dp", "gx", "gy"))
    depth = magnetic.shape[2]
    samples_all = magnetic.shape[0] * ranks
    cells_x = magnetic.shape[3] * count_gx
    cells_y = magnetic.shape[4] * count_gy
    scale_one = 1.0 / math.sqrt(samples_all * (depth // 2) * (cells_x // 2) * (cells_y // 2))
    scale_two = 1.0 / math.sqrt(samples_all * (depth // 4) * (cells_x // 4) * (cells_y // 4))
    field = magnetic.reshape(24, 32, 128)
    cot = cotangent.reshape(2, 8, 2048)
    one = kernel_one.reshape(27, 3, 32)
    two = kernel_two.reshape(864, 64)

    swaps_x, swaps_y = swaps("gx"), swaps("gy")
    nx, ny = len(swaps_x), len(swaps_y)
    operands = [pltpu.with_memory_space_constraint(array, pltpu.HBM) for array in (field, cot, one, two)]
    field, cot, one, two, *edges = call(
        lambda *refs: edge_x_kernel(nx, *refs),
        [shape(array.shape, BF) for array in operands] + [shape((128, 128), BF)] * nx,
        operands,
        [pltpu.VMEM((128, 128), F32), pltpu.SemaphoreType.DMA((4,))],
        space=pltpu.HBM,
    )
    got_x = [lax.ppermute(edge, ("dp", "gx"), pairs) for edge, pairs in zip(edges, swaps_x)]
    w_one, w_two, picks = call(
        weights_kernel,
        [shape((1152, 256), BF), shape((1152, 256), BF), shape((256, 2048), BF)],
        (one, two),
        [pltpu.VMEM((88, 32), F32)],
        flops=1 << 30,
    )
    split, *edges = call(
        lambda *refs: edge_y_kernel(nx, ny, *refs),
        [shape((5, 384, 128), BF)] + [shape((80, 128), BF)] * ny,
        (field, cot, *got_x),
        [pltpu.VMEM((24, 72, 128), F32)],
    )
    got_y = [lax.ppermute(edge, ("dp", "gy"), pairs) for edge, pairs in zip(edges, swaps_y)]
    first = call(
        lambda *refs: windows_kernel(nx, *refs),
        [
            shape((5, 8, 64, 128), BF),
            shape((5, 128, 256), BF),
            shape((3, 4, 112, 128), BF),
            shape((4, 2, 112, 128), F32),
            shape((2, 256, 128), F32),
            shape((2, 2, 16, 128), F32),
            shape((2, 8, 1664), BF),
            shape((2, 104, 128), F32),
            shape((2, 104, 128), F32),
            shape((192, 1152), F32),
        ],
        (split, w_one, w_two, cot, *got_x),
        [pltpu.VMEM((5, 8, 112, 128), BF), pltpu.VMEM((3, 4, 224, 128), BF)],
        flops=1 << 31,
    )
    tall = 64 // ranks
    features, level, *dealt = call(
        lambda *refs: main_kernel(ny, ranks, *refs),
        [shape((2, 8, 2048), BF), shape((4, 16, 2048), BF)] + [shape((tall, 1024), BF)] * ranks,
        (*first, picks, w_one, w_two, *got_y),
        [
            pltpu.VMEM((5, 8, 32, 128), BF),
            pltpu.VMEM((5, 8, 16, 128), BF),
            pltpu.VMEM((3, 4, 64, 128), BF),
            pltpu.VMEM((3, 4, 32, 128), BF),
            pltpu.VMEM((4, 2, 16, 128), F32),
            pltpu.VMEM((16, 16, 128), F32),
            pltpu.VMEM((64, 1024), F32),
            pltpu.VMEM((2, 8, 2048), BF),
            pltpu.VMEM((4, 16, 2048), BF),
            pltpu.SemaphoreType.DMA((6,)),
        ],
        in_hbm=2,
    )
    terms = [exchange(dealt[step], "dp", step) for step in (ranks - 1, *range(1, ranks - 1))] + dealt[:1]
    mine, = call(sum_kernel, [shape((tall, 1024), BF)], terms)
    step = 1
    while step < count_gx:
        mine, = call(sum_kernel, [shape((tall, 1024), BF)], (mine, exchange(mine, "gx", step)))
        step *= 2
    if count_gy == 4:
        terms = [mine, trade_shared(mine, 1, 2), trade_shared(mine, 0, 3)]
        mine, = call(share_kernel, [shape((tall, 1024), F32)], terms)
        terms = [mine, exchange(mine, "gx", 1)]
    else:
        terms = [mine] + [exchange(mine, "gy", step) for step in range(1, count_gy)]
    grad_one, grad_two = call(
        lambda *refs: last_kernel(scale_one, scale_two, *refs),
        [shape((27, 3, tall // 2), F32), shape((27, tall, 32), F32)],
        terms,
    )
    grad_one = grad_one.reshape(3, 3, 3, 3, tall // 2)
    grad_two = jnp.transpose(grad_two.reshape(3, 3, 3, tall, 32), (0, 1, 2, 4, 3))
    return (
        features.reshape(1, 2, 8, 2048),
        level.reshape(1, 4, 16, 2048),
        grad_one,
        grad_two,
    )


def solution(mesh):
    in_specs = (P("dp", None, None, "gx", "gy"), P(), P(), P("dp", None, "gx", "gy"))
    out_specs = (
        P("dp", None, "gx", "gy"),
        P("dp", None, "gx", "gy"),
        P(None, None, None, None, "dp"),
        P(None, None, None, None, "dp"),
    )
    return jax.shard_map(body, mesh=mesh, in_specs=in_specs, out_specs=out_specs, check_vma=False)
```

```python
import math

import jax
import jax.numpy as jnp
from jax import lax
from jax.experimental import pallas as pl
from jax.experimental.pallas import tpu as pltpu
from jax.sharding import PartitionSpec as P

BF = jnp.bfloat16
F32 = jnp.float32
VMEM_LIMIT = 32 * 1024 * 1024


def iota(shape, dim):
    return lax.broadcasted_iota(jnp.int32, shape, dim)


def dot(lhs, rhs, contract=((1,), (0,))):
    return lax.dot_general(lhs, rhs, (contract, ((), ())), preferred_element_type=F32)


def swaps(axis):
    count, ranks = lax.axis_size(axis), lax.axis_size("dp")
    found = []
    for first in range(min(2, count - 1)):
        pairs = []
        for d in range(ranks):
            for i in range(count):
                other = i + 1 if i % 2 == first else i - 1
                if 0 <= other < count:
                    pairs.append((d * count + i, d * count + other))
                else:
                    pairs.append((d * count + i, (d ^ 1) % ranks * count + i))
        found.append(pairs)
    return found


def position(axis):
    index = lax.axis_index(axis)
    return lax.rem(index, 2) == 1, index == 0, index == lax.axis_size(axis) - 1


def from_low(place, got):
    odd, first, _ = place
    second = got[1] if len(got) > 1 else got[0]
    return jnp.where(first, 0.0, jnp.where(odd, got[0], second))


def from_high(place, got):
    odd, _, last = place
    second = got[1] if len(got) > 1 else got[0]
    return jnp.where(last, 0.0, jnp.where(odd, second, got[0]))


def edge_x_kernel(count, *refs):
    hbm, refs = refs[:4], refs[4:]
    held, outs, (stage, sems) = refs[:4], refs[4 : 4 + count], refs[4 + count :]
    fetches = [pltpu.make_async_copy(hbm[i], held[i], sems.at[i]) for i in range(4)]
    for fetch in fetches:
        fetch.start()
    mag_ref, cot_ref = held[:2]
    odd = position("gx")[0]
    planes = mag_ref.shape[0]
    blocks = cot_ref.shape[2] // 128
    for fetch in fetches[:2]:
        fetch.wait()
    field = mag_ref[...].astype(F32)
    low = field[:, 0:4, :]
    high = field[:, field.shape[1] - 4 :, :]
    cot = [cot_ref[k].astype(F32)[0:1, :] for k in range(2)]
    for turn in range(count):
        toward_high = odd if turn == 1 else jnp.logical_not(odd)
        picked = jnp.where(toward_high, high, low)
        for g in range(planes):
            stage[4 * g : 4 * g + 4, :] = picked[g]
        for k in range(2):
            for m in range(blocks):
                row = 4 * planes + 16 * k + m
                stage[row : row + 1, :] = cot[k][:, 128 * m : 128 * m + 128]
        outs[turn][...] = stage[...].astype(BF)
    for fetch in fetches[2:]:
        fetch.wait()


def edge_y_kernel(count_x, count_y, mag_ref, cot_ref, *refs):
    got_refs, refs = refs[:count_x], refs[count_x:]
    split_ref, outs = refs[0], refs[1 : 1 + count_y]
    tall, = refs[1 + count_y :]
    place_x, place_y = position("gx"), position("gy")
    planes = mag_ref.shape[0]
    got = [ref[...].astype(F32) for ref in got_refs]
    low = from_low(place_x, got)
    high = from_high(place_x, got)
    zeros = jnp.zeros((24, 128), F32)
    for g in range(planes):
        edge = low[4 * g : 4 * g + 4, :]
        tall[g, 0:8, :] = jnp.broadcast_to(edge[3:4, :], (8, 128))
        tall[g, 8:40, :] = mag_ref[g].astype(F32)
        tall[g, 40:44, :] = high[4 * g : 4 * g + 4, :]
        tall[g, 44:68, :] = zeros
        tall[g, 68:72, :] = edge
    starts = (8, 9, 10, 11, 7)
    split = []
    for slot in range(5):
        parts = [tall[g, pl.ds(starts[slot], 16, stride=4), :].astype(BF) for g in range(planes)]
        whole = jnp.concatenate(parts, axis=0)
        split_ref[slot] = whole
        split.append(whole)
    rows = planes // 3 * 16
    lhs = jnp.concatenate(
        [split[s][rows * c : rows * c + rows] for s in range(4) for c in range(3)], axis=1
    )
    lane = iota((128, 128), 1)
    cell = iota((128, 128), 0)
    slot = lane & 3
    wanted = jnp.where(lane < 64, 124 + slot, slot)
    group = (lane & 63) >> 2
    picks = []
    for s in range(4):
        for c in range(3):
            hit = (group == 4 * s + c) & (cell == wanted)
            picks.append(jnp.where(hit, 1.0, 0.0).astype(BF))
    both = dot(lhs, jnp.concatenate(picks, axis=0)).reshape(4, 2, 16, 128)
    lower, upper = both[:, 0].reshape(64, 128), both[:, 1].reshape(64, 128)
    left = iota((64, 128), 1) < 64
    toward = [
        jnp.where(left, lower, pltpu.roll(upper, 64, 1)),
        jnp.where(left, pltpu.roll(lower, 64, 1), upper),
    ]
    cot_rows = []
    for k in range(2):
        own = cot_ref[k].astype(F32)[:, 0:128]
        row = 4 * planes + 16 * k
        cot_rows.append(jnp.concatenate([own, high[row : row + 1, :], jnp.zeros((7, 128), F32)], axis=0))
    cot_rows = jnp.where(iota((16, 128), 1) < 64, cot_rows[0], pltpu.roll(cot_rows[1], 64, 1))
    odd = place_y[0]
    for turn in range(count_y):
        toward_high = odd if turn == 1 else jnp.logical_not(odd)
        outs[turn][0:64, :] = jnp.where(toward_high, toward[0], toward[1]).astype(BF)
        outs[turn][64:80, :] = cot_rows.astype(BF)


def weights_kernel(one_ref, two_ref, w_one, w_two, halo_ref, rows_one):
    lane = iota((32, 256), 1)
    spread = jnp.where(iota((32, 256), 0) == (lane & 31), 1.0, 0.0).astype(BF)
    rows_one[80:88, :] = jnp.zeros((8, 32), F32)
    for i in range(27):
        rows_one[3 * i : 3 * i + 3, :] = one_ref[i].astype(F32)
    wide = dot(rows_one[...].astype(BF), spread)
    window = iota((32, 256), 0) - 2 * (lane >> 5)
    for tap in range(9):
        for c in range(3):
            block = jnp.zeros((32, 256), F32)
            for e in range(3):
                row = (3 * tap + e) * 3 + c
                block = jnp.where(window == e, wide[row : row + 1, :], block)
            w_one[128 * tap + 32 * c : 128 * tap + 32 * c + 32, :] = block.astype(BF)
        w_one[128 * tap + 96 : 128 * tap + 128, :] = jnp.zeros((32, 256), BF)

    lane = iota((64, 128), 1)
    spread = jnp.where(iota((64, 128), 0) == (lane & 63), 1.0, 0.0).astype(BF)
    twice = dot(two_ref[...], spread)
    left = iota((32, 128), 1) < 64
    for tap in range(9):
        k0, k1, k2 = (twice[32 * (3 * tap + e) : 32 * (3 * tap + e) + 32] for e in range(3))
        base = 128 * tap
        w_two[base : base + 32, 0:128] = jnp.where(left, k1, 0.0).astype(BF)
        w_two[base + 32 : base + 64, 0:128] = jnp.where(left, k2, k0).astype(BF)
        w_two[base + 64 : base + 96, 0:128] = jnp.where(left, 0.0, k1).astype(BF)
        w_two[base + 96 : base + 128, 0:128] = jnp.where(left, 0.0, k2).astype(BF)
        w_two[base : base + 96, 128:256] = jnp.zeros((96, 128), BF)
        w_two[base + 96 : base + 128, 128:256] = jnp.where(left, k0, 0.0).astype(BF)

    lane = iota((256, 256), 1)
    code = iota((256, 256), 0)
    offset = lane & 31
    part = (lane & 127) >> 5
    wanted = jnp.where(
        lane < 128,
        jnp.where(offset == 0, 3, -999),
        jnp.where(
            (offset >= 1) & (offset <= 4), 127 + offset, jnp.where((offset >= 14) & (offset <= 16), offset - 13, -999)
        ),
    )
    wanted = jnp.where(part < 3, wanted + 4 * part, -999)
    for s in range(4):
        for parity in range(2):
            hit = code - (64 * parity + 16 * s) == wanted
            base = 256 * (2 * s + parity)
            halo_ref[:, base : base + 256] = jnp.where(hit, 1.0, 0.0).astype(BF)


SLOTS = ((4, 0, 1), (1, 2, 3))


def first_level(pre, t):
    sig = jax.nn.sigmoid(pre)
    hidden = pre * sig
    slope = sig * (1.0 + pre * (1.0 - sig))
    if t == 0:
        return [(1, hidden)], slope
    rows, width = hidden.shape
    later = hidden.reshape(rows // 16, 16, width)
    later = jnp.concatenate([later[:, 15:16], later[:, 0:15]], axis=1).reshape(rows, width)
    return [(2, hidden), (0, later)], slope


def second_level(pre, cot):
    sig = jax.nn.sigmoid(pre)
    return pre * sig, cot * (sig * (1.0 + pre * (1.0 - sig)))


def short_pair(value, row):
    return jnp.concatenate([value[row : row + 8, 0:128], value[row : row + 8, 128:256]], axis=0)


def windows_kernel(count_x, split_ref, w_one, w_two, cot_ref, *refs):
    gx_refs, refs = refs[:count_x], refs[count_x:]
    short_ref, outer_ref, short_act, slope_ref, cot_all = refs[:5]
    ends_ref, feat_ref, here_ref, after_ref, grad_ref, inner_ref, act_ref = refs[5:]
    high_x = from_high(position("gx"), [ref[96:128, :].astype(F32) for ref in gx_refs])
    for k in range(2):
        cot = cot_ref[k].astype(F32)
        for m in range(16):
            row = 16 * k + m
            cot_all[k, 16 * m : 16 * m + 8, :] = cot[:, 128 * m : 128 * m + 128]
            cot_all[k, 16 * m + 8 : 16 * m + 16, :] = jnp.where(
                iota((8, 128), 0) == 0, high_x[row : row + 1, :], 0.0
            )

    lane = iota((128, 1152), 1)
    cell = iota((128, 1152), 0)
    block = lane >> 7
    offset = lane & 31
    part = (lane & 127) >> 5
    wanted = jnp.where(offset <= 16, 16 * block - 1 + offset, -9)
    wanted = jnp.where(block == 8, jnp.where(offset == 0, 127, -9), wanted)
    hit = cell == wanted
    picks = jnp.concatenate(
        [jnp.where(hit & (part == c), 1.0, 0.0).astype(BF) for c in range(3)], axis=0
    )
    for s in range(5):
        lhs = jnp.concatenate([split_ref[s, 128 * c : 128 * c + 128, :] for c in range(3)], axis=1)
        exact = dot(lhs, picks)
        found = exact.astype(BF)
        for z in range(8):
            for q in range(4):
                first = exact[16 * z : 16 * z + 8, 256 * q + 128 : 256 * q + 256]
                if q < 3:
                    second = exact[16 * z : 16 * z + 8, 256 * q + 256 : 256 * q + 384]
                else:
                    second = jnp.zeros((8, 128), F32)
                short_ref[s, z, 16 * q : 16 * q + 16, :] = jnp.concatenate([first, second], axis=0).astype(BF)
        for n in range(1, 8):
            for z in range(8):
                inner_ref[s, z, 16 * n - 16 : 16 * n, :] = found[16 * z : 16 * z + 16, 128 * n : 128 * n + 128]
        outer_ref[s, :, 0:128] = found[:, 0:128]
        outer_ref[s, :, 128:256] = found[:, 1024:1152]
    weights = w_one[...]
    for p in range(4):
        for t in range(2):
            pieces = []
            for a in range(3):
                for b in range(3):
                    z = 2 * p + a - 1
                    pieces.append(inner_ref[SLOTS[t][b], z] if z >= 0 else jnp.zeros((112, 128), BF))
            versions, slope = first_level(dot(jnp.concatenate(pieces, axis=1), weights), t)
            for b, value in versions:
                for n in range(7):
                    short_act[b, p, 16 * n : 16 * n + 16, :] = short_pair(value, 16 * n).astype(BF)
                value = value.astype(BF)
                for n in range(7):
                    act_ref[b, p, 32 * n : 32 * n + 16, :] = value[16 * n : 16 * n + 16, 0:128]
                    act_ref[b, p, 32 * n + 16 : 32 * n + 32, :] = value[16 * n : 16 * n + 16, 128:256]
            for n in range(7):
                slope_ref[p, t, 16 * n : 16 * n + 16, :] = short_pair(slope, 16 * n)
    weights = w_two[...]
    delta, patches = [], []
    for k in range(2):
        planes = [(b, 2 * k + a - 1) for a in range(3) for b in range(3)]
        lhs = [act_ref[b, p] if p >= 0 else jnp.zeros((224, 128), BF) for b, p in planes]
        out = dot(jnp.concatenate(lhs, axis=1), weights)
        ends_ref[k, 0] = out[0:16, 0:128]
        ends_ref[k, 1] = out[208:224, 128:256]
        feat, value = second_level(out[16:224, 0:128] + out[0:208, 128:256], cot_all[k, 48:256, :])
        feat_ref[k] = jnp.concatenate([feat[16 * m : 16 * m + 8] for m in range(13)], axis=1).astype(BF)
        value = value.reshape(13, 16, 128)
        here = value[:, 0:8].reshape(104, 128)
        here_ref[k] = here
        after_ref[k] = value[:, 1:9].reshape(104, 128)
        zero = jnp.zeros((8, 128), F32)
        both = [jnp.concatenate([zero, here], axis=0), jnp.concatenate([here, zero], axis=0)]
        delta.append(jnp.concatenate(both, axis=1).astype(BF))
        short = [short_act[b, p] if p >= 0 else jnp.zeros((112, 128), BF) for b, p in planes]
        patches.append(jnp.concatenate(short, axis=1))
    delta, patches = jnp.concatenate(delta, axis=0), jnp.concatenate(patches, axis=0)
    for first in range(0, 1152, 256):
        last = min(first + 256, 1152)
        grad_ref[:, first:last] = dot(delta, patches[:, first:last], ((0,), (0,)))[0:192]


def main_kernel(
    count_y,
    ranks,
    short_ref,
    outer_ref,
    short_act,
    slope_ref,
    cot_ref,
    ends_ref,
    feat_in,
    here_in,
    after_in,
    grad_in,
    halo_ref,
    w_one,
    w_two,
    *refs,
):
    gy_refs, refs = refs[:count_y], refs[count_y:]
    feat_hbm, level_hbm, refs = refs[0], refs[1], refs[2:]
    dealt, refs = refs[:ranks], refs[ranks:]
    edges, short_edges, outer_act, outer_short, outer_slope, rows_out, total, feat_ref, level_ref, sems = refs
    place_y = position("gy")
    copies = []

    got_y = [ref[...].astype(F32) for ref in gy_refs]
    low_y = from_low(place_y, got_y)
    high_y = from_high(place_y, got_y)
    halo = jnp.concatenate([low_y[0:64], high_y[0:64]], axis=1).astype(BF)
    first_half = iota((16, 128), 1) < 64
    cot_y = [jnp.where(first_half, value, 0.0) for value in (high_y[64:80], pltpu.roll(high_y[64:80], 64, 1))]
    brought = dot(halo, halo_ref[...])
    for s in range(5):
        base = 512 * min(s, 3)
        found = [brought[:, base + 256 * parity : base + 256 * parity + 256].reshape(4, 16, 256) for parity in range(2)]
        edge = jnp.stack(found, axis=1).reshape(8, 16, 256)
        if s == 4:
            edge = jnp.concatenate([edge[:, 15:16], edge[:, 0:15]], axis=1)
        exact = outer_ref[s].astype(F32) + edge.reshape(128, 256)
        value = exact.astype(BF)
        for z in range(8):
            edges[s, z, 0:16, :] = value[16 * z : 16 * z + 16, 0:128]
            edges[s, z, 16:32, :] = value[16 * z : 16 * z + 16, 128:256]
            other = short_ref[s, z, 48:64, :].astype(F32)
            short_edges[s, z] = jnp.concatenate([other[0:8], exact[16 * z : 16 * z + 8, 0:128]], axis=0).astype(BF)

    def window(s, z):
        if z < 0:
            return jnp.zeros((64, 128), BF)
        return jnp.concatenate([short_ref[s, z, 0:48, :], short_edges[s, z]], axis=0)

    weights = w_one[...]
    for t in range(2):
        rows = []
        for p in range(4):
            pieces = []
            for a in range(3):
                for b in range(3):
                    z = 2 * p + a - 1
                    pieces.append(edges[SLOTS[t][b], z] if z >= 0 else jnp.zeros((32, 128), BF))
            rows.append(jnp.concatenate(pieces, axis=1))
        versions, slope = first_level(dot(jnp.concatenate(rows, axis=0), weights), t)
        for p in range(4):
            first, second = 32 * p, 32 * p + 16
            for b, value in versions:
                before = jnp.concatenate([value[second : second + 8, 128:256], jnp.zeros((8, 128), F32)], axis=0)
                outer_short[b, p, 0:16, :] = before.astype(BF)
                outer_short[b, p, 16:32, :] = short_pair(value, first).astype(BF)
                outer_act[b, p, 0:16, :] = value[second : second + 16, 128:256].astype(BF)
                outer_act[b, p, 16:32, :] = value[first : first + 16, 0:128].astype(BF)
                outer_act[b, p, 32:48, :] = value[first : first + 16, 128:256].astype(BF)
                outer_act[b, p, 48:64, :] = value[second : second + 16, 0:128].astype(BF)
            outer_slope[p, t] = short_pair(slope, first)

    lhs = []
    for k in range(2):
        planes = [(b, 2 * k + a - 1) for a in range(3) for b in range(3)]
        lhs.append(
            jnp.concatenate([outer_act[b, p] if p >= 0 else jnp.zeros((64, 128), BF) for b, p in planes], axis=1)
        )
    out = dot(jnp.concatenate(lhs, axis=0), w_two[...])
    pairs, pairs_next, delta, patches, feats = [], [], [], [], []
    for k in range(2):
        own = out[64 * k : 64 * k + 64]
        pre = jnp.concatenate(
            [own[16:48, 0:128], ends_ref[k, 0], own[48:64, 0:128]], axis=0
        ) + jnp.concatenate([own[0:48, 128:256], ends_ref[k, 1]], axis=0)
        feat, value = second_level(pre, jnp.concatenate([cot_ref[k, 0:48, :], cot_y[k]], axis=0))
        feats.append(feat)
        value = value.reshape(4, 16, 128)
        outer = value[:, 0:8].reshape(32, 128)
        here = jnp.concatenate([outer[0:24], here_in[k], outer[24:32]], axis=0)
        outer_after = value[:, 1:9].reshape(32, 128)
        after = jnp.concatenate([outer_after[0:24], after_in[k], outer_after[24:32]], axis=0)
        pairs.append(jnp.concatenate([here[0:128], here[8:136]], axis=1).astype(BF))
        pairs_next.append(jnp.concatenate([after[0:128], after[8:136]], axis=1).astype(BF))
        zero = jnp.zeros((8, 128), F32)
        both = [
            jnp.concatenate([zero, zero, outer[0:24], zero], axis=0),
            jnp.concatenate([outer[0:8], zero, outer[8:24], zero, zero], axis=0),
        ]
        delta.append(jnp.concatenate(both, axis=1).astype(BF))
        short = []
        for a in range(3):
            for b in range(3):
                p = 2 * k + a - 1
                if p < 0:
                    short.append(jnp.zeros((48, 128), BF))
                else:
                    short.append(jnp.concatenate([outer_short[b, p], short_act[b, p, 0:16, :]], axis=0))
        patches.append(jnp.concatenate(short, axis=1))
    delta, patches = jnp.concatenate(delta, axis=0), jnp.concatenate(patches, axis=0)

    lhs_rows, rhs_rows = [], []
    for p in range(4):
        depth = [(1, p // 2)] if p % 2 == 0 else [(2, (p - 1) // 2), (0, (p + 1) // 2)]
        for t in range(2):
            width = [(1, pairs)] if t == 0 else [(2, pairs), (0, pairs_next)]
            taps = [(3 * a + b, source[k]) for a, k in depth if k < 2 for b, source in width]
            level = dot(
                jnp.concatenate([source for _, source in taps], axis=1),
                jnp.concatenate([w_two[128 * tap : 128 * tap + 128, :] for tap, _ in taps], axis=1),
                ((1,), (1,)),
            )
            level = level.astype(BF).astype(F32)
            for m in range(16):
                rows_out[m, pl.ds(t, 8, stride=2), :] = level[8 * m : 8 * m + 8]
            slope = jnp.concatenate([outer_slope[p, t], slope_ref[p, t]], axis=0)
            value = level * slope
            blocks = [
                jnp.concatenate([value[16 * n : 16 * n + 8], value[16 * n + 8 : 16 * n + 16]], axis=1)
                for n in (1, 2, 3, 4, 5, 6, 7, 0)
            ]
            lhs_rows.append(jnp.concatenate(blocks, axis=0).astype(BF))
            rhs_rows.append(
                jnp.concatenate([window(SLOTS[t][b], 2 * p + a - 1) for a in range(3) for b in range(3)], axis=1)
            )
        level_ref[p] = jnp.concatenate([rows_out[m] for m in range(16)], axis=1).astype(BF)
        copies.append(pltpu.make_async_copy(level_ref.at[p], level_hbm.at[p], sems.at[2 + p]))
        copies[-1].start()
    for k, feat in enumerate(feats):
        feat_ref[k, :, 0:384] = jnp.concatenate([feat[16 * m : 16 * m + 8] for m in range(3)], axis=1).astype(BF)
        feat_ref[k, :, 384:2048] = feat_in[k]
        copies.append(pltpu.make_async_copy(feat_ref.at[k], feat_hbm.at[k], sems.at[k]))
        copies[-1].start()
    delta_one = jnp.concatenate(lhs_rows, axis=0).T
    windows = jnp.concatenate(rhs_rows, axis=0)

    place = iota((64, 128), 1) >> 5
    turned = []
    for ab in range(9):
        if ab % 2 == 0:
            first, last = 128 * ab, min(128 * ab + 256, 1152)
            grad = dot(delta, patches[:, first:last], ((0,), (0,)))[0:192] + grad_in[:, first:last]
        column = 128 * (ab % 2)
        a0, a1, a2 = (grad[64 * j : 64 * j + 64, column : column + 128] for j in range(3))
        r0, r1, r2 = (pltpu.roll(a, 64, 1) for a in (a0, a1, a2))
        joined = jnp.where(place == 0, a0 + r1, jnp.where(place == 1, a1 + r2, a1 + r0))
        shift = (3 * ab - 1) % 4
        other = (shift + 2) % 4
        outer = pltpu.roll(joined, 32 * shift, 1) if shift else joined
        inner = pltpu.roll(joined, 32 * other, 1) if other else joined
        turned += [outer, inner, outer]
    turned.append(jnp.zeros((64, 128), F32))
    for v in range(7):
        t0, t1, t2, t3 = turned[4 * v : 4 * v + 4]
        total[:, 128 * v : 128 * v + 128] = jnp.where(
            place < 2, jnp.where(place == 0, t0, t1), jnp.where(place == 2, t2, t3)
        )

    place = iota((32, 128), 1)
    found = jnp.zeros((32, 128), F32)
    for tap in range(9):
        if tap % 2 == 0:
            grad = dot(delta_one, windows[:, 128 * tap : min(128 * tap + 256, 1152)])
        column = 128 * (tap % 2)
        some = jnp.zeros((32, 128), F32)
        for t in range(8):
            piece = grad[32 * t : 32 * t + 32, column : column + 128]
            shift = (3 * tap - 2 * t) % 128
            some = some + (pltpu.roll(piece, shift, 1) if shift else piece)
        local = place & 31
        found = jnp.where((local >= 3 * tap) & (local < 3 * tap + 3), some, found)
    total[:, 896:1024] = jnp.zeros((64, 128), F32)
    tall, short = 64 // ranks, 32 // ranks
    for d in range(ranks):
        total[tall * d : tall * d + short, 896:1024] = found[short * d : short * d + short]
    rank = lax.axis_index("dp")
    for step, out in enumerate(dealt):
        if tall % 8 == 0:
            start = pl.multiple_of((rank ^ step) * tall, tall)
            picked = total[pl.ds(start, tall), :]
        else:
            picked = total[0:tall, :]
            for d in range(1, ranks):
                picked = jnp.where((rank ^ step) == d, total[d * tall : d * tall + tall, :], picked)
        out[...] = picked.astype(BF)
    for copy in copies:
        copy.wait()


def sum_kernel(*refs):
    parts, out_ref = refs[:-1], refs[-1]
    values = [ref[...].astype(F32) for ref in parts]
    while len(values) > 1:
        values = [values[i] + values[i + 1] for i in range(0, len(values), 2)]
    out_ref[...] = values[0].astype(out_ref.dtype)


def share_kernel(mine_ref, first_ref, second_ref, out_ref):
    first = first_ref[...].astype(F32)
    odd = position("gx")[0]
    out_ref[...] = first + jnp.where(odd, second_ref[...], mine_ref[...]).astype(F32)


def last_kernel(scale_one, scale_two, *refs):
    parts, (one_ref, two_ref) = refs[:-2], refs[-2:]
    values = [ref[...].astype(F32) for ref in parts]
    while len(values) > 1:
        values = [values[i] + values[i + 1] for i in range(0, len(values), 2)]
    value = values[0]
    tall = value.shape[0]
    short = tall // 2
    scaled = value[:, 0:896] * scale_two
    for tap in range(27):
        two_ref[tap] = scaled[:, 32 * tap : 32 * tap + 32]
    rows = value[0:short, 896:1024] * scale_one
    if short < 8:
        rows = jnp.concatenate([rows, jnp.zeros((8 - short, 128), F32)], axis=0)
    turned = rows.T
    for c in range(3):
        one_ref[:, c, :] = turned[32 * c : 32 * c + 27, 0:short]


def call(kernel, outs, args, scratch=(), space=pltpu.VMEM, in_hbm=0, flops=0):
    spaces = [pltpu.HBM] * in_hbm + [pltpu.VMEM] * (len(outs) - in_hbm)
    return pl.pallas_call(
        kernel,
        out_shape=outs,
        in_specs=[pl.BlockSpec(memory_space=space)] * len(args),
        out_specs=[pl.BlockSpec(memory_space=kind) for kind in spaces],
        scratch_shapes=list(scratch),
        compiler_params=pltpu.CompilerParams(vmem_limit_bytes=VMEM_LIMIT),
        cost_estimate=pl.CostEstimate(flops=flops, bytes_accessed=1 << 20, transcendentals=0),
    )(*args)


def shape(dims, dtype):
    return jax.ShapeDtypeStruct(dims, dtype)


def exchange(value, axis, step):
    return lax.ppermute(value, axis, [(i, i ^ step) for i in range(lax.axis_size(axis))])


def trade_shared(value, even_step, odd_step):
    count, columns, ranks = lax.axis_size("gy"), lax.axis_size("gx"), lax.axis_size("dp")
    pairs = []
    for d in range(ranks):
        for g in range(columns):
            for i in range(count):
                to_d, to_i = d, i ^ (odd_step if g % 2 else even_step)
                if g % 2 == 0 and even_step == 0:
                    to_d = (d ^ 1) % ranks
                pairs.append(((d * columns + g) * count + i, (to_d * columns + g) * count + to_i))
    return lax.ppermute(value, ("dp", "gx", "gy"), pairs)


def body(magnetic, kernel_one, kernel_two, cotangent):
    ranks, count_gx, count_gy = (lax.axis_size(axis) for axis in ("dp", "gx", "gy"))
    depth = magnetic.shape[2]
    samples_all = magnetic.shape[0] * ranks
    cells_x = magnetic.shape[3] * count_gx
    cells_y = magnetic.shape[4] * count_gy
    scale_one = 1.0 / math.sqrt(samples_all * (depth // 2) * (cells_x // 2) * (cells_y // 2))
    scale_two = 1.0 / math.sqrt(samples_all * (depth // 4) * (cells_x // 4) * (cells_y // 4))
    field = magnetic.reshape(24, 32, 128)
    cot = cotangent.reshape(2, 8, 2048)
    one = kernel_one.reshape(27, 3, 32)
    two = kernel_two.reshape(864, 64)

    swaps_x, swaps_y = swaps("gx"), swaps("gy")
    nx, ny = len(swaps_x), len(swaps_y)
    operands = [pltpu.with_memory_space_constraint(array, pltpu.HBM) for array in (field, cot, one, two)]
    field, cot, one, two, *edges = call(
        lambda *refs: edge_x_kernel(nx, *refs),
        [shape(array.shape, BF) for array in operands] + [shape((128, 128), BF)] * nx,
        operands,
        [pltpu.VMEM((128, 128), F32), pltpu.SemaphoreType.DMA((4,))],
        space=pltpu.HBM,
    )
    got_x = [lax.ppermute(edge, ("dp", "gx"), pairs) for edge, pairs in zip(edges, swaps_x)]
    w_one, w_two, picks = call(
        weights_kernel,
        [shape((1152, 256), BF), shape((1152, 256), BF), shape((256, 2048), BF)],
        (one, two),
        [pltpu.VMEM((88, 32), F32)],
        flops=1 << 30,
    )
    split, *edges = call(
        lambda *refs: edge_y_kernel(nx, ny, *refs),
        [shape((5, 384, 128), BF)] + [shape((80, 128), BF)] * ny,
        (field, cot, *got_x),
        [pltpu.VMEM((24, 72, 128), F32)],
    )
    got_y = [lax.ppermute(edge, ("dp", "gy"), pairs) for edge, pairs in zip(edges, swaps_y)]
    first = call(
        lambda *refs: windows_kernel(nx, *refs),
        [
            shape((5, 8, 64, 128), BF),
            shape((5, 128, 256), BF),
            shape((3, 4, 112, 128), BF),
            shape((4, 2, 112, 128), F32),
            shape((2, 256, 128), F32),
            shape((2, 2, 16, 128), F32),
            shape((2, 8, 1664), BF),
            shape((2, 104, 128), F32),
            shape((2, 104, 128), F32),
            shape((192, 1152), F32),
        ],
        (split, w_one, w_two, cot, *got_x),
        [pltpu.VMEM((5, 8, 112, 128), BF), pltpu.VMEM((3, 4, 224, 128), BF)],
        flops=1 << 31,
    )
    tall = 64 // ranks
    features, level, *dealt = call(
        lambda *refs: main_kernel(ny, ranks, *refs),
        [shape((2, 8, 2048), BF), shape((4, 16, 2048), BF)] + [shape((tall, 1024), BF)] * ranks,
        (*first, picks, w_one, w_two, *got_y),
        [
            pltpu.VMEM((5, 8, 32, 128), BF),
            pltpu.VMEM((5, 8, 16, 128), BF),
            pltpu.VMEM((3, 4, 64, 128), BF),
            pltpu.VMEM((3, 4, 32, 128), BF),
            pltpu.VMEM((4, 2, 16, 128), F32),
            pltpu.VMEM((16, 16, 128), F32),
            pltpu.VMEM((64, 1024), F32),
            pltpu.VMEM((2, 8, 2048), BF),
            pltpu.VMEM((4, 16, 2048), BF),
            pltpu.SemaphoreType.DMA((6,)),
        ],
        in_hbm=2,
    )
    terms = [exchange(dealt[step], "dp", step) for step in (ranks - 1, *range(1, ranks - 1))] + dealt[:1]
    mine, = call(sum_kernel, [shape((tall, 1024), BF)], terms)
    step = 1
    while step < count_gx:
        mine, = call(sum_kernel, [shape((tall, 1024), BF)], (mine, exchange(mine, "gx", step)))
        step *= 2
    if count_gy == 4:
        terms = [mine, trade_shared(mine, 1, 2), trade_shared(mine, 0, 3)]
        mine, = call(share_kernel, [shape((tall, 1024), F32)], terms)
        terms = [mine, exchange(mine, "gx", 1)]
    else:
        terms = [mine] + [exchange(mine, "gy", step) for step in range(1, count_gy)]
    grad_one, grad_two = call(
        lambda *refs: last_kernel(scale_one, scale_two, *refs),
        [shape((27, 3, tall // 2), F32), shape((27, tall, 32), F32)],
        terms,
    )
    grad_one = grad_one.reshape(3, 3, 3, 3, tall // 2)
    grad_two = jnp.transpose(grad_two.reshape(3, 3, 3, tall, 32), (0, 1, 2, 4, 3))
    return (
        features.reshape(1, 2, 8, 2048),
        level.reshape(1, 4, 16, 2048),
        grad_one,
        grad_two,
    )


def solution(mesh):
    in_specs = (P("dp", None, None, "gx", "gy"), P(), P(), P("dp", None, "gx", "gy"))
    out_specs = (
        P("dp", None, "gx", "gy"),
        P("dp", None, "gx", "gy"),
        P(None, None, None, None, "dp"),
        P(None, None, None, None, "dp"),
    )
    return jax.shard_map(body, mesh=mesh, in_specs=in_specs, out_specs=out_specs, check_vma=False)
```
